256 devices in a mesh: dp: 2 (over core), ctx: 16 (over y, x), tp: 8 (over z).
Axes of the slice: x: 4, y: 4, z: 8, core: 2. Of those that a mesh axis runs over, the one named last changes fastest.
Arguments:
- queries: bfloat16 [2, 2048, 8192], P('dp', 'ctx', 'tp'), may hold values from -160 to 160
- keys: bfloat16 [2, 2048, 512], P('dp', 'ctx'), may hold values from -6 to 6
- attention_values: bfloat16 [2, 2048, 512], P('dp', 'ctx'), may hold values from -6 to 6
- key_start: int32 [2, 2048], P('dp', 'ctx'), may hold values from 0 to 2040, as said below
- out_weight: bfloat16 [8192, 4096], P('tp', 'ctx'), may hold values from -0.29882812 to 0.29882812
- residual: bfloat16 [2, 2048, 4096], P('dp', ('ctx', 'tp')), may hold values from -40 to 40
- norm_gain: bfloat16 [4096], replicated, may hold values from 0.099609375 to 1.8984375
- router_weight: bfloat16 [4096, 128], replicated, may hold values from -0.015625 to 0.015625
- routes: int32 [2, 2048, 8], P('dp', ('ctx', 'tp')), may hold values from 0 to 127, all different within a row; in each aligned block of 16 rows (0 to 15, 16 to 31, ..., all dimensions but the last counted through in order) at most 2 rows name the same one
- block_masks: int32 [2, 2048, 8], P('dp', ('ctx', 'tp')), may hold values from 0 to 63
- gate_weight: bfloat16 [128, 4096, 768], P(('ctx', 'tp'), None, 'dp'), may hold values from -0.09375 to 0.09375
- up_weight: bfloat16 [128, 4096, 768], P(('ctx', 'tp'), None, 'dp'), may hold values from -0.09375 to 0.09375
- down_weight: bfloat16 [128, 768, 4096], P(('ctx', 'tp'), 'dp'), may hold values from -0.875 to 0.875
Outputs:
- layer_out: bfloat16 [2, 2048, 4096], P('dp', ('ctx', 'tp'))
The draws below stay inside these ranges and needn't reach their ends.
Inputs may be any that keep to these rules, and one draw needn't show every extreme that they name: key_start[w, i] is the first position of token i's document in window w: a multiple of 8, at most i, equal for all tokens of a document; a window holds at most 4 documents. `routes`: each token names 8 different experts; among the rows of one device (aligned blocks of 16 tokens) no expert is named by more than 2 rows, a bound that some block reaches. `block_masks`: bit b keeps hidden units b * 128 up to (b + 1) * 128 - 1 of the route's expert.
All inputs are finite; a program needn't handle non-finite values.
Results may differ from the reference program's by a relative error of at most 0.017.
Values may be sent and summed in bfloat16 or wider, within the bound.
No kernel may reach another device: no remote copies, remote signals or barrier semaphores. Data moves between devices by JAX's collectives and lax.ppermute only.
A program may use at most 128 MiB of HBM per device.

```python
import math
import jax
import jax.numpy as jnp
import numpy as np
from jax import lax

D = 4096
QUERY_HEADS = 64
KEY_VALUE_HEADS = 4
HEAD_SIZE = 128
FF = 768
MASK_BLOCKS = 6
TOP = 8
SEQUENCE_WINDOWS = 2
WINDOW_TOKENS = 2048
TOK_DEV = 16
EXPERTS = 128
CAP = 2


def shared_keys(key):
    noise_key = jnp.clip(jax.random.normal(key, (SEQUENCE_WINDOWS, WINDOW_TOKENS, KEY_VALUE_HEADS, HEAD_SIZE), jnp.float32), -6.0, 6.0)
    return noise_key


def draw_keys(key, part):
    noise_key = shared_keys(key)
    final_result = noise_key
    return final_result.reshape(SEQUENCE_WINDOWS, WINDOW_TOKENS, KEY_VALUE_HEADS * HEAD_SIZE).astype(jnp.bfloat16)


def draw_queries(key, part):
    key = jax.random.fold_in(key, 2)
    noise = jnp.clip(2.0 * jax.random.normal(key, (SEQUENCE_WINDOWS, WINDOW_TOKENS, QUERY_HEADS, HEAD_SIZE), jnp.float32), -12.0, 12.0)
    return noise.reshape(SEQUENCE_WINDOWS, WINDOW_TOKENS, QUERY_HEADS * HEAD_SIZE).astype(jnp.bfloat16)


def draw_key_start(key, part):
    key = jax.random.fold_in(key, 3)
    inner = jax.random.randint(key, (SEQUENCE_WINDOWS, 2), 1, WINDOW_TOKENS // 8 - 1) * 8
    last = jnp.full((SEQUENCE_WINDOWS, 1), WINDOW_TOKENS - 8, jnp.int32)
    bounds = jnp.concatenate([jnp.zeros((SEQUENCE_WINDOWS, 1), jnp.int32), inner.astype(jnp.int32), last], axis=1)
    positions = jnp.arange(WINDOW_TOKENS, dtype=jnp.int32)
    below = bounds[:, None, :] <= positions[None, :, None]
    return jnp.max(jnp.where(below, bounds[:, None, :], 0), axis=2).astype(jnp.int32)


def draw_residual(key, part):
    key = jax.random.fold_in(key, 4)
    row_key, col_key, base_key = jax.random.split(key, 3)
    row_scale = jnp.exp(jax.random.uniform(row_key, (SEQUENCE_WINDOWS, WINDOW_TOKENS, 1), jnp.float32, math.log(0.3), math.log(3.0)))
    col_scale = jnp.exp(jax.random.uniform(col_key, (1, 1, D), jnp.float32, math.log(0.3), math.log(3.0)))
    base = jax.random.normal(base_key, (SEQUENCE_WINDOWS, WINDOW_TOKENS, D), jnp.float32)
    return jnp.clip(base * row_scale * col_scale, -40.0, 40.0).astype(jnp.bfloat16)


def touch_ends(result, key, low, largest):
    index_at = [jax.random.randint(jax.random.fold_in(key, axis), (), 0, length) for axis, length in enumerate(result.shape)]
    longest = result.shape.index(max(result.shape))
    neighbour = index_at[:longest] + [(index_at[longest] + 1) % result.shape[longest]] + index_at[longest + 1:]
    return result.at[tuple(index_at)].set(low).at[tuple(neighbour)].set(largest)


def level_of(stream_key, extent, shards, low, largest):
    level, own = 1.0, jax.random.fold_in(stream_key, 6)
    for position, parts in shards:
        draws = jnp.exp(jax.random.uniform(jax.random.fold_in(own, position), (parts,), jnp.float32, low / len(shards), largest / len(shards)))
        level = level * jnp.repeat(draws, extent[position] // parts).reshape([-1 if axis == position else 1 for axis in range(len(extent))])
    return level


def deal_out(own_key, own, number, rows, amount, top, most, lean):
    order = jax.random.permutation(own_key, amount)
    crowded, common = load_shares(amount, rows * top, most, lean, True), load_shares(amount, rows * top, most, lean, False)
    places = jnp.arange(amount)

    def named(sizes, rotation):
        used = int((sizes > 0).sum())
        fixed = max(1, used // 4)
        shifted = fixed + (places - fixed + rotation * (used - fixed)) % max(1, amount - fixed)
        return jnp.zeros((amount,), jnp.int32).at[order[jnp.where(places < fixed, places, shifted)]].set(jnp.asarray(sizes, jnp.int32))

    sizes = jnp.where(number % 4 == 0, named(crowded, number // 4), named(common, number - number // 4 - 1))
    mixed = jax.random.permutation(jax.random.fold_in(own, 3), amount)
    source_of, receiver = mixed[0:amount // 2 * 2:2], mixed[1:amount // 2 * 2:2]
    margin = jnp.minimum(sizes[source_of] - 1, most - sizes[receiver]) // 2
    margin = jnp.where((source_of == order[0]) | (receiver == order[0]) | (sizes[receiver] == 0), 0, jnp.maximum(margin, 0))
    shifted = jax.random.randint(jax.random.fold_in(own, 4), (amount // 2,), 0, 1 << 20) % (margin + 1)
    sizes = sizes.at[source_of].add(-shifted).at[receiver].add(shifted)
    members = jnp.searchsorted(jnp.cumsum(sizes), jnp.arange(rows * top), side="right").astype(jnp.int32)
    listing = members.reshape(top, rows).T
    listing = listing[jax.random.permutation(jax.random.fold_in(own, 1), rows)]
    rotation = jax.random.randint(jax.random.fold_in(own, 2), (rows, 1), 0, top)
    return jnp.take_along_axis(listing, (jnp.arange(top)[None, :] + rotation) % top, axis=1)


def load_shares(number_of, total, most, slope, full):
    loads = [(1 << 20) // math.isqrt(grade ** slope) + 1 for grade in range(1, number_of + 1)]
    largest = most if full else min(most, max(-(-total // number_of), total * loads[0] // sum(loads)))
    least = 1 if total - largest >= number_of - 1 else 0
    given, rest = [largest] + [least] * (number_of - 1), total - largest - least * (number_of - 1)
    while rest > 0:
        candidates = [i for i in range(1, number_of) if given[i] < largest] or [i for i in range(1, number_of) if given[i] < most]
        mass, remaining = sum([loads[i] for i in candidates]), rest
        for i in candidates:
            extra = min(most - given[i], max(1, remaining * loads[i] // mass), rest)
            given[i] = given[i] + extra
            rest = rest - extra
    return np.array(given)


def bell_draw(key, extent, deviation, bound, shards=(), held_as=jnp.bfloat16):
    entries = jax.random.normal(key, extent, jnp.float32) * deviation
    if len(shards) > 0:
        entries = level_of(key, extent, shards, -0.22, 0.18) * entries
    return jnp.clip(entries, min=-bound, max=bound).astype(held_as)


def setup_inputs(seed: int = 0) -> dict:
    key_list = jax.random.split(jax.random.key(seed), 14)
    queries = draw_queries(jax.random.fold_in(key_list[13], 71), 0)
    keys = draw_keys(jax.random.fold_in(key_list[13], 71), 0)
    attention_values = bell_draw(key_list[2], (SEQUENCE_WINDOWS, WINDOW_TOKENS, KEY_VALUE_HEADS * HEAD_SIZE), 1.0, 6.0, ((0, 2), (1, 16)))
    key_start = draw_key_start(jax.random.fold_in(key_list[13], 71), 0)
    out_weight = bell_draw(key_list[4], (QUERY_HEADS * HEAD_SIZE, D), 0.05, 0.29882812, ((0, 8), (1, 16)))
    residual = draw_residual(jax.random.fold_in(key_list[13], 71), 0)
    norm_gain = jnp.clip(1.0 + 0.18 * jax.random.normal(key_list[6], (D,), jnp.float32), 0.099609375, 1.8984375).astype(jnp.bfloat16)
    router_weight = bell_draw(key_list[7], (D, EXPERTS), (D * 40) ** -0.5, 0.015625)
    routes_keys = jax.random.split(jax.random.fold_in(key_list[8], 1), SEQUENCE_WINDOWS * WINDOW_TOKENS // TOK_DEV)
    routes_turns = jax.random.permutation(jax.random.fold_in(key_list[8], 3), SEQUENCE_WINDOWS * WINDOW_TOKENS // TOK_DEV)
    routes = jax.vmap(lambda own, number: deal_out(jax.random.fold_in(key_list[8], 2), own, number, TOK_DEV, EXPERTS, TOP, CAP, 2))(routes_keys, routes_turns).reshape((SEQUENCE_WINDOWS, WINDOW_TOKENS, TOP))
    block_masks = touch_ends(jax.random.randint(key_list[9], (SEQUENCE_WINDOWS, WINDOW_TOKENS, TOP), 0, 2 ** MASK_BLOCKS), jax.random.fold_in(key_list[9], 1), 0, (2 ** MASK_BLOCKS) - 1).astype(jnp.int32)
    gate_weight = bell_draw(key_list[10], (EXPERTS, D, FF), D ** -0.5, 0.09375, ((0, 128), (2, 2)))
    up_weight = bell_draw(key_list[11], (EXPERTS, D, FF), D ** -0.5, 0.09375, ((0, 128), (2, 2)))
    down_weight = bell_draw(key_list[12], (EXPERTS, FF, D), (max(1, FF // 16)) ** -0.5, 0.875, ((0, 128), (1, 2)))
    return dict(queries=queries, keys=keys, attention_values=attention_values, key_start=key_start, out_weight=out_weight, residual=residual, norm_gain=norm_gain, router_weight=router_weight, routes=routes, block_masks=block_masks, gate_weight=gate_weight, up_weight=up_weight, down_weight=down_weight)


def attend_window(queries, keys, attention_values, key_start):
    query_group_size = QUERY_HEADS // KEY_VALUE_HEADS
    query_heads = jnp.transpose(queries.reshape(WINDOW_TOKENS, QUERY_HEADS, HEAD_SIZE), (1, 0, 2))
    repeated_key_heads = jnp.transpose(keys.reshape(WINDOW_TOKENS, KEY_VALUE_HEADS, HEAD_SIZE), (1, 0, 2))
    repeated_value_heads = jnp.transpose(attention_values.reshape(WINDOW_TOKENS, KEY_VALUE_HEADS, HEAD_SIZE), (1, 0, 2))
    positions = jnp.arange(WINDOW_TOKENS, dtype=jnp.int32)
    visible = (positions[None, :] >= key_start[:, None]) & (positions[None, :] <= positions[:, None])

    def one_head(inputs):
        query_head, head_index = inputs
        kv_index = (head_index // query_group_size).astype(jnp.int32)
        key_head = lax.dynamic_index_in_dim(repeated_key_heads, kv_index, 0, keepdims=False)
        value_head = lax.dynamic_index_in_dim(repeated_value_heads, kv_index, 0, keepdims=False)
        scores = jnp.dot(query_head, key_head.T, preferred_element_type=jnp.float32) / math.sqrt(HEAD_SIZE)
        scores = jnp.where(visible, scores, -1e+30)
        row_max = lax.optimization_barrier(jnp.max(scores, axis=1, keepdims=True))
        raw_weights = jnp.where(visible, jnp.exp(scores - row_max), 0.0)
        row_sum = lax.optimization_barrier(jnp.sum(raw_weights, axis=1, keepdims=True))
        mixed = jnp.dot(raw_weights.astype(jnp.bfloat16), value_head, preferred_element_type=jnp.float32)
        return (mixed / row_sum).astype(jnp.bfloat16)
    attended = lax.map(one_head, (query_heads, jnp.arange(QUERY_HEADS, dtype=jnp.int32)))
    return jnp.transpose(attended, (1, 0, 2)).reshape(WINDOW_TOKENS, QUERY_HEADS * HEAD_SIZE)

def experts_window(normed, routes, block_masks, router_weight, gate_weight, up_weight, down_weight):
    logits = jnp.dot(normed, router_weight, preferred_element_type=jnp.float32)
    chosen = jnp.take_along_axis(logits, routes, axis=1)
    route_exp = jnp.exp(chosen)
    route_weights = (route_exp / lax.optimization_barrier(jnp.sum(route_exp, axis=1, keepdims=True))).reshape(-1)
    flat_ids = routes.reshape(-1).astype(jnp.int32)
    flat_masks = block_masks.reshape(-1).astype(jnp.int32)
    order = jnp.argsort(flat_ids, stable=True).astype(jnp.int32)
    expert_ids = jnp.arange(EXPERTS, dtype=jnp.int32)
    counts = lax.optimization_barrier(jnp.sum((flat_ids[None, :] == expert_ids[:, None]).astype(jnp.int32), axis=1)).astype(jnp.int32)
    firsts = (jnp.cumsum(counts) - counts).astype(jnp.int32)
    limit = WINDOW_TOKENS // TOK_DEV * CAP
    slots = jnp.arange(limit, dtype=jnp.int32)
    bit_ids = jnp.arange(MASK_BLOCKS, dtype=jnp.int32)
    total_assign = WINDOW_TOKENS * TOP

    def one_expert(mixture, expert):
        picked = order[jnp.clip(firsts[expert] + slots, 0, total_assign - 1)].astype(jnp.int32)
        valid = slots < counts[expert]
        token_ids = (picked // TOP).astype(jnp.int32)
        rows = normed[token_ids]
        gate_act = jnp.dot(rows, gate_weight[expert], preferred_element_type=jnp.float32)
        up_act = jnp.dot(rows, up_weight[expert], preferred_element_type=jnp.float32)
        bits = jnp.right_shift(flat_masks[picked][:, None], bit_ids[None, :]) & 1
        unit_mask = jnp.repeat(bits, FF // MASK_BLOCKS, axis=1).astype(jnp.float32)
        activated = (jax.nn.silu(gate_act) * up_act * unit_mask).astype(jnp.bfloat16)
        rounded = jnp.dot(activated, down_weight[expert], preferred_element_type=jnp.float32).astype(jnp.bfloat16)
        outputs = lax.optimization_barrier(rounded).astype(jnp.float32)
        scaled = outputs * jnp.where(valid, route_weights[picked], 0.0)[:, None]
        return (mixture.at[token_ids].add(scaled), None)
    mixture, unused = lax.scan(one_expert, jnp.zeros((WINDOW_TOKENS, D), jnp.float32), expert_ids)
    return mixture

def reference(queries, keys, attention_values, key_start, out_weight, residual, norm_gain, router_weight, routes, block_masks, gate_weight, up_weight, down_weight):
    results = []
    for window in range(SEQUENCE_WINDOWS):
        attended = attend_window(queries[window], keys[window], attention_values[window], key_start[window])
        projected = jnp.dot(attended, out_weight, preferred_element_type=jnp.float32)
        hidden_state = (residual[window].astype(jnp.float32) + projected).astype(jnp.bfloat16)
        state_wide = lax.optimization_barrier(hidden_state).astype(jnp.float32)
        inverse = lax.rsqrt(lax.optimization_barrier(jnp.mean(state_wide * state_wide, axis=1, keepdims=True)) + 1e-06)
        normed = (state_wide * inverse * norm_gain.astype(jnp.float32)).astype(jnp.bfloat16)
        mixture = experts_window(normed, routes[window], block_masks[window], router_weight, gate_weight, up_weight, down_weight)
        results.append((state_wide + mixture).astype(jnp.bfloat16))
    return jnp.stack(results)
```

```python
import functools
import math

import jax
import jax.numpy as jnp
from jax import lax
from jax.experimental import pallas as pl
from jax.experimental.pallas import tpu as pltpu
from jax.sharding import Mesh
from jax.sharding import PartitionSpec as P

QUERY_HEADS = 64
KEY_VALUE_HEADS = 4
HEAD_SIZE = 128
MASK_BLOCKS = 6
TOP = 8
EXPERTS = 128
CAP = 2
SCORE_FLOOR = -1e30
LANES = 128
SUB = 16
VMEM_LIMIT = 60 * 1024 * 1024

CY, CX, ZHI, ZLO = 4, 4, 4, 2
CTX = ("cy", "cx")
F32, BF16, I32 = jnp.float32, jnp.bfloat16, jnp.int32


def call(kernel, out_shape, args, scalars=(), any_args=(), scratch=(), flops=0, moved=0):
    specs = [pl.BlockSpec(memory_space=pltpu.SMEM) for _ in scalars]
    specs += [pl.BlockSpec(memory_space=pltpu.VMEM) for _ in args]
    specs += [pl.BlockSpec(memory_space=pl.ANY) for _ in any_args]
    many = isinstance(out_shape, (list, tuple))
    vmem = pl.BlockSpec(memory_space=pltpu.VMEM)
    return pl.pallas_call(
        kernel,
        out_shape=out_shape,
        in_specs=specs,
        out_specs=[vmem] * len(out_shape) if many else vmem,
        scratch_shapes=list(scratch),
        cost_estimate=pl.CostEstimate(flops=flops, bytes_accessed=moved, transcendentals=0),
        compiler_params=pltpu.CompilerParams(vmem_limit_bytes=VMEM_LIMIT),
    )(*scalars, *args, *any_args)


def attend_kernel(first_ref, query_ref, kv_ref, start_ref, out_ref, bias_ref):
    tokens = query_ref.shape[0]
    heads = query_ref.shape[1] // HEAD_SIZE
    keys = kv_ref.shape[0] * kv_ref.shape[1]
    key_rows = kv_ref[:, :, :HEAD_SIZE].reshape(keys, HEAD_SIZE)
    value_rows = kv_ref[:, :, HEAD_SIZE:].reshape(keys, HEAD_SIZE)
    position = first_ref[0] + lax.broadcasted_iota(I32, (tokens, keys), 0)
    key_pos = lax.broadcasted_iota(I32, (tokens, keys), 1)
    visible = (key_pos >= start_ref[...]) & (key_pos <= position)
    bias_ref[...] = jnp.where(visible, 0.0, SCORE_FLOOR)
    scale = math.log2(math.e) / math.sqrt(HEAD_SIZE)
    for head in range(heads):
        columns = slice(head * HEAD_SIZE, (head + 1) * HEAD_SIZE)
        scores = lax.dot_general(
            query_ref[:, columns], key_rows, (((1,), (1,)), ((), ())), preferred_element_type=F32
        )
        scores = scores * scale + bias_ref[...]
        row_max = jnp.max(scores, axis=1, keepdims=True)
        weights = jnp.exp2(scores - row_max)
        row_sum = jnp.sum(weights, axis=1, keepdims=True)
        mixed = jnp.dot(weights.astype(BF16), value_rows, preferred_element_type=F32)
        attended = (mixed / row_sum).astype(BF16)
        for z in range(ZHI * ZLO):
            block = attended[z * SUB : (z + 1) * SUB]
            rows = slice((z // ZLO) * SUB, (z // ZLO + 1) * SUB)
            for y in range(CY):
                out_ref[y * ZLO + z % ZLO, rows, columns] = block


def project_kernel(dp_ref, zlo_ref, att_ref, own_ref, other_ref, out_ref):
    dp, zlo = dp_ref[0], zlo_ref[0]
    half = own_ref.shape[2]
    group_rows = CY * ZHI * SUB
    width = own_ref.shape[3]
    for x in range(CX):
        total = jnp.zeros((group_rows, width), F32)
        for piece_ref, part in ((own_ref, dp), (other_ref, 1 - dp)):
            for near in range(ZLO):
                source = zlo if near == 0 else 1 - zlo
                columns = pl.ds(pl.multiple_of(part * half, half), half)
                rows = jnp.concatenate([att_ref[y * ZLO + source, :, columns] for y in range(CY)])
                total += jnp.dot(rows, piece_ref[x, near], preferred_element_type=F32)
        out_ref[:, :, x * width : (x + 1) * width] = total.astype(BF16).reshape(
            CY * ZHI, SUB, width
        )


def norm_kernel(parts_ref, residual_ref, gain_ref, meta_ref, ext_ref, hidden_ref):
    model_width = residual_ref.shape[1]
    width = model_width // CY
    pieces = []
    square_sum = jnp.zeros((SUB, 1), F32)
    for y in range(CY):
        columns = slice(y * width, (y + 1) * width)
        projected = sum(parts_ref[y * ZHI + z].astype(F32) for z in range(ZHI))
        hidden = (residual_ref[:, columns].astype(F32) + projected).astype(BF16)
        hidden_ref[:, columns] = hidden
        wide = hidden.astype(F32)
        square_sum += jnp.sum(wide * wide, axis=1, keepdims=True)
        pieces.append(wide)
    inverse = lax.rsqrt(square_sum / model_width + 1e-06)
    for y in range(CY):
        columns = slice(y * width, (y + 1) * width)
        normed = (pieces[y] * inverse * gain_ref[:, columns].astype(F32)).astype(BF16)
        for z in range(ZHI):
            ext_ref[z, :, columns] = normed
    for z in range(ZHI):
        ext_ref[z, :, model_width:] = meta_ref[...]


def slot_hits(meta, zhi, slots, slot_capacity):
    tokens = meta.shape[0]
    slot = lax.broadcasted_iota(I32, (tokens, slots), 1)
    dest = slot // slot_capacity
    expert = (dest // ZLO) * (ZHI * ZLO) + zhi * ZLO + dest % ZLO
    hits = [meta[:, k : k + 1].astype(F32).astype(I32) == expert for k in range(TOP)]
    named = sum(h.astype(F32) for h in hits)
    later = lax.broadcasted_iota(I32, (tokens, tokens), 0) > lax.broadcasted_iota(
        I32, (tokens, tokens), 1
    )
    earlier = jnp.dot(later.astype(BF16), named.astype(BF16), preferred_element_type=F32)
    place = (slot % slot_capacity).astype(F32)
    chosen = jnp.where((named > 0.5) & (earlier == place), 1.0, 0.0)
    return hits, chosen


def dispatch_kernel(zhi_ref, ext_ref, rows_ref):
    tokens = ext_ref.shape[0] * ext_ref.shape[1]
    ext_width = ext_ref.shape[2]
    model_width = ext_width - LANES
    slots = rows_ref.shape[0]
    meta = ext_ref[:, :, model_width:].reshape(tokens, LANES)
    hits, chosen = slot_hits(meta, zhi_ref[0], slots, tokens // SUB * CAP)
    masks = sum(
        jnp.where(hits[k], meta[:, TOP + k : TOP + k + 1].astype(F32), 0.0) for k in range(TOP)
    )
    along = (((0,), (0,)), ((), ()))
    pick = chosen.astype(BF16)
    normed = ext_ref[:, :, :model_width].reshape(tokens, model_width)
    rows_ref[:, :model_width] = lax.dot_general(
        pick, normed, along, preferred_element_type=F32
    ).astype(BF16)
    masked = (masks * chosen).astype(BF16)
    ones = jnp.ones((tokens, LANES), BF16)
    rows_ref[:, model_width:] = lax.dot_general(
        masked, ones, along, preferred_element_type=F32
    ).astype(BF16)


def weight_kernel(zhi_ref, ext_ref, router_ref, out_ref):
    tokens = ext_ref.shape[0] * ext_ref.shape[1]
    model_width = ext_ref.shape[2] - LANES
    slots = out_ref.shape[1]
    meta = ext_ref[:, :, model_width:].reshape(tokens, LANES)
    normed = ext_ref[:, :, :model_width].reshape(tokens, model_width)
    logits = jnp.dot(normed, router_ref[...], preferred_element_type=F32)
    lanes = lax.broadcasted_iota(I32, (tokens, EXPERTS), 1)
    exps = []
    for k in range(TOP):
        route = meta[:, k : k + 1].astype(F32).astype(I32)
        picked = jnp.sum(jnp.where(lanes == route, logits, 0.0), axis=1, keepdims=True)
        exps.append(jnp.exp(picked))
    total = sum(exps)
    hits, chosen = slot_hits(meta, zhi_ref[0], slots, tokens // SUB * CAP)
    route_weight = sum(jnp.where(hits[k], exps[k] / total, 0.0) for k in range(TOP))
    out_ref[...] = route_weight * chosen


def expert_kernel(
    dp_ref, rows_ref, *refs
):
    weights, out_ref, held, sems = refs[:6], refs[6], refs[7:13], refs[13]
    order = (0, 1, 3, 4, 2, 5)
    copies = [pltpu.make_async_copy(weights[i], held[i], sems.at[i]) for i in range(6)]
    for i in order:
        copies[i].start()
    model_width = out_ref.shape[1]
    slots = out_ref.shape[0]
    masks = rows_ref[:, model_width:].astype(F32).astype(I32)
    rows = rows_ref[:, :model_width]
    blocks = MASK_BLOCKS // 2
    acts = []
    for part in range(2):
        gate_ref, up_ref = held[3 * part], held[3 * part + 1]
        first = (dp_ref[0] if part == 0 else 1 - dp_ref[0]) * blocks
        copies[3 * part].wait()
        gate = jnp.dot(rows, gate_ref[...], preferred_element_type=F32)
        copies[3 * part + 1].wait()
        up = jnp.dot(rows, up_ref[...], preferred_element_type=F32)
        keep = jnp.concatenate(
            [(jnp.right_shift(masks, first + b) & 1).astype(F32) for b in range(blocks)], axis=1
        )
        acts.append((jax.nn.silu(gate) * up * keep).astype(BF16))
    copies[2].wait()
    copies[5].wait()
    step = 512
    for j in range(model_width // step):
        columns = slice(j * step, (j + 1) * step)
        total = jnp.dot(acts[0], held[2][:, columns], preferred_element_type=F32)
        total += jnp.dot(acts[1], held[5][:, columns], preferred_element_type=F32)
        out_ref[:, columns] = total.astype(BF16)


def combine_kernel(weight_ref, back_ref, out_ref):
    weight = weight_ref[...]
    high = weight.astype(BF16)
    rest = weight - high.astype(F32)
    middle = rest.astype(BF16)
    low = (rest - middle.astype(F32)).astype(BF16)
    stacked = jnp.concatenate([high, middle, low], axis=0)
    tokens = weight.shape[0]
    model_width = back_ref.shape[1]
    step = 1024
    for j in range(model_width // step):
        columns = slice(j * step, (j + 1) * step)
        parts = jnp.dot(stacked, back_ref[:, columns], preferred_element_type=F32)
        total = parts[:tokens] + parts[tokens : 2 * tokens] + parts[2 * tokens :]
        out_ref[:, :, columns] = total.astype(BF16).reshape(tokens // SUB, SUB, step)


def swap(n):
    return [(i, i ^ 1) for i in range(n)]


def exchange(x, axes):
    return lax.all_to_all(x, axes, split_axis=0, concat_axis=0, tiled=True)


def local(
    queries,
    keys,
    attention_values,
    key_start,
    out_weight,
    residual,
    norm_gain,
    router_weight,
    routes,
    block_masks,
    gate_weight,
    up_weight,
    down_weight,
):
    dp = lax.axis_index("dp").astype(I32)
    ctx = lax.axis_index(CTX).astype(I32)
    zhi, zlo = lax.axis_index("zhi").astype(I32), lax.axis_index("zlo").astype(I32)
    tokens = queries.shape[1]
    model_width = residual.shape[2]
    token_rows = residual.shape[1]
    ctx_count = CY * CX
    scalar = lambda v: v.reshape(1)

    with jax.named_scope("keys_values"):
        heads = queries.shape[2] // HEAD_SIZE
        kv_head = (zhi * ZLO + zlo) * heads // (QUERY_HEADS // KEY_VALUE_HEADS)
        own_kv = jnp.concatenate(
            [
                lax.dynamic_slice_in_dim(a[0], kv_head * HEAD_SIZE, HEAD_SIZE, 1)
                for a in (keys, attention_values)
            ],
            axis=1,
        )
        all_kv = exchange(jnp.broadcast_to(own_kv[None], (ctx_count,) + own_kv.shape), CTX)

    with jax.named_scope("out_weight"):
        half = out_weight.shape[0] // 2
        own_half = lax.dynamic_slice_in_dim(out_weight, dp * half, half, 0)
        pair = jnp.stack([own_half, lax.ppermute(own_half, "zlo", swap(ZLO))])
        near_weight = lax.all_gather(pair, "cx", axis=0, tiled=False)
        far_weight = lax.ppermute(near_weight, "dp", swap(2))

    with jax.named_scope("expert_weights"):
        own_experts = [a[0] for a in (gate_weight, up_weight, down_weight)]
        other_experts = [lax.ppermute(a, "dp", swap(2)) for a in own_experts]

    with jax.named_scope("attention"):
        attended = call(
            attend_kernel,
            jax.ShapeDtypeStruct((CY * ZLO, tokens // ZLO, queries.shape[2]), BF16),
            (queries[0], all_kv, key_start.reshape(tokens, 1)),
            scalars=(scalar(ctx * tokens),),
            scratch=[pltpu.VMEM((tokens, ctx_count * tokens), F32)],
            flops=4 * tokens * heads * ctx_count * tokens * HEAD_SIZE,
            moved=4 << 20,
        )
        gathered = exchange(attended, ("cy", "zlo"))

    with jax.named_scope("projection"):
        partial = call(
            project_kernel,
            jax.ShapeDtypeStruct((CY * ZHI, SUB, model_width // CY), BF16),
            (gathered, near_weight, far_weight),
            scalars=(scalar(dp), scalar(zlo)),
            flops=2 * 256 * 2048 * 1024,
            moved=6 << 20,
        )
        parts = exchange(partial, ("cy", "zhi"))

    with jax.named_scope("norm"):
        meta = jnp.concatenate([routes[0], block_masks[0]], axis=1).astype(BF16)
        meta = jnp.pad(meta, ((0, 0), (0, LANES - 2 * TOP)))
        ext, hidden_state = call(
            norm_kernel,
            [
                jax.ShapeDtypeStruct((ZHI, token_rows, model_width + LANES), BF16),
                jax.ShapeDtypeStruct((token_rows, model_width), BF16),
            ],
            (parts, residual[0], norm_gain.reshape(1, model_width), meta),
            moved=2 << 20,
        )
        near_ext = exchange(ext, "zhi")

    with jax.named_scope("dispatch"):
        dests = ctx_count * ZLO
        capacity = ZHI * token_rows // SUB * CAP
        slots = dests * capacity
        rows = call(
            dispatch_kernel,
            jax.ShapeDtypeStruct((slots, model_width + LANES), BF16),
            (near_ext,),
            scalars=(scalar(zhi),),
            flops=2 * slots * 64 * model_width,
            moved=3 << 20,
        )
        slot_weight = call(
            weight_kernel,
            jax.ShapeDtypeStruct((ZHI * token_rows, slots), F32),
            (near_ext, router_weight),
            scalars=(scalar(zhi),),
            flops=2 * 64 * EXPERTS * model_width,
            moved=2 << 20,
        )
        over = ("cy", "cx", "zlo")
        got = exchange(rows.reshape(dests, capacity, model_width + LANES), over)

    with jax.named_scope("experts"):
        every = own_experts + other_experts
        expert_out = call(
            expert_kernel,
            jax.ShapeDtypeStruct((slots, model_width), BF16),
            (got.reshape(slots, model_width + LANES),),
            scalars=(scalar(dp),),
            any_args=every,
            scratch=[pltpu.VMEM(a.shape, a.dtype) for a in every] + [pltpu.SemaphoreType.DMA((6,))],
            flops=6 * slots * model_width * 768,
            moved=22 << 20,
        )
        back = exchange(expert_out.reshape(dests, capacity, model_width), over)

    with jax.named_scope("combine"):
        mixed = call(
            combine_kernel,
            jax.ShapeDtypeStruct((ZHI, token_rows, model_width), BF16),
            (slot_weight, back.reshape(slots, model_width)),
            flops=6 * 64 * slots * model_width,
            moved=3 << 20,
        )
        mixture = jnp.sum(exchange(mixed, "zhi").astype(F32), axis=0)
        layer_out = (hidden_state.astype(F32) + mixture).astype(BF16)
    return layer_out[None]


def solution(mesh):
    fine = Mesh(
        mesh.devices.reshape(2, CY, CX, ZHI, ZLO), ("dp", "cy", "cx", "zhi", "zlo")
    )
    tp = ("zhi", "zlo")
    all_ctx = CTX + tp
    in_specs = (
        P("dp", CTX, tp),
        P("dp", CTX, None),
        P("dp", CTX, None),
        P("dp", CTX),
        P(tp, CTX),
        P("dp", all_ctx, None),
        P(),
        P(),
        P("dp", all_ctx, None),
        P("dp", all_ctx, None),
        P(all_ctx, None, "dp"),
        P(all_ctx, None, "dp"),
        P(all_ctx, "dp", None),
    )
    out_specs = P("dp", all_ctx, None)
    return jax.shard_map(local, mesh=fine, in_specs=in_specs, out_specs=out_specs, check_vma=False)
```

```python
import math

import jax
import jax.numpy as jnp
from jax import lax
from jax.experimental import pallas as pl
from jax.experimental.pallas import tpu as pltpu
from jax.sharding import Mesh
from jax.sharding import PartitionSpec as P

QUERY_HEADS = 64
KEY_VALUE_HEADS = 4
HEAD_SIZE = 128
MASK_BLOCKS = 6
TOP = 8
EXPERTS = 128
CAP = 2
SCORE_FLOOR = -1e30
LANES = 128
SUB = 16
MIB = 1024 * 1024

CY, CX, ZHI, ZLO = 4, 4, 4, 2
CTX = ("cy", "cx")
F32, BF16, I32 = jnp.float32, jnp.bfloat16, jnp.int32


def call(kernel, out_shape, args, vmem, scalars=(), scratch=(), flops=0, moved=0):
    specs = [pl.BlockSpec(memory_space=pltpu.SMEM) for _ in scalars]
    specs += [pl.BlockSpec(memory_space=pltpu.VMEM) for _ in args]
    many = isinstance(out_shape, (list, tuple))
    whole = pl.BlockSpec(memory_space=pltpu.VMEM)
    return pl.pallas_call(
        kernel,
        out_shape=out_shape,
        in_specs=specs,
        out_specs=[whole] * len(out_shape) if many else whole,
        scratch_shapes=list(scratch),
        cost_estimate=pl.CostEstimate(flops=flops, bytes_accessed=moved, transcendentals=0),
        compiler_params=pltpu.CompilerParams(vmem_limit_bytes=vmem * MIB),
    )(*scalars, *args)


def attend_kernel(first_ref, query_ref, kv_ref, start_ref, out_ref, bias_ref):
    tokens = query_ref.shape[0]
    heads = query_ref.shape[1] // HEAD_SIZE
    keys = kv_ref.shape[0] * kv_ref.shape[1]
    key_rows = kv_ref[:, :, :HEAD_SIZE].reshape(keys, HEAD_SIZE)
    value_rows = kv_ref[:, :, HEAD_SIZE:].reshape(keys, HEAD_SIZE)
    position = first_ref[0] + lax.broadcasted_iota(I32, (tokens, keys), 0)
    key_pos = lax.broadcasted_iota(I32, (tokens, keys), 1)
    visible = (key_pos >= start_ref[...]) & (key_pos <= position)
    bias_ref[...] = jnp.where(visible, 0.0, SCORE_FLOOR)
    scale = math.log2(math.e) / math.sqrt(HEAD_SIZE)
    for head in range(heads):
        columns = slice(head * HEAD_SIZE, (head + 1) * HEAD_SIZE)
        scores = lax.dot_general(
            query_ref[:, columns], key_rows, (((1,), (1,)), ((), ())), preferred_element_type=F32
        )
        scores = scores * scale + bias_ref[...]
        row_max = jnp.max(scores, axis=1, keepdims=True)
        weights = jnp.exp2(scores - row_max)
        row_sum = jnp.sum(weights, axis=1, keepdims=True)
        mixed = jnp.dot(weights.astype(BF16), value_rows, preferred_element_type=F32)
        attended = (mixed / row_sum).astype(BF16)
        for z in range(ZHI * ZLO):
            block = attended[z * SUB : (z + 1) * SUB]
            rows = slice((z // ZLO) * SUB, (z // ZLO + 1) * SUB)
            for y in range(CY):
                out_ref[y * ZLO + z % ZLO, rows, columns] = block


def project_kernel(dp_ref, x_ref, zlo_ref, att_ref, *refs):
    out_ref = refs[-1]
    pieces = (refs[:5], refs[5:10])
    half, width = refs[3].shape
    rows = att_ref.shape[0] * att_ref.shape[2]
    for step, away in enumerate((0, CX - 1, 1, 2)):
        total = jnp.zeros((rows, width), F32)
        for near in range(ZLO):
            source = zlo_ref[0] if near == 0 else 1 - zlo_ref[0]
            for refs_of, part in ((pieces[0], dp_ref[0]), (pieces[1], 1 - dp_ref[0])):
                weight = refs_of[3 + near][...] if step == 3 else refs_of[step][near]
                columns = pl.ds(pl.multiple_of(part * half, half), half)
                total += jnp.dot(
                    att_ref[:, source, :, columns].reshape(rows, half),
                    weight,
                    preferred_element_type=F32,
                )
        place = pl.multiple_of(((x_ref[0] + away) & (CX - 1)) * width, width)
        out_ref[:, :, pl.ds(place, width)] = total.astype(BF16).reshape(rows // SUB, SUB, width)


def norm_kernel(parts_ref, residual_ref, gain_ref, meta_ref, ext_ref, hidden_ref):
    model_width = residual_ref.shape[1]
    width = model_width // CY
    zs = ZHI
    pieces = []
    square_sum = jnp.zeros((SUB, 1), F32)
    for y in range(CY):
        columns = slice(y * width, (y + 1) * width)
        projected = sum(parts_ref[y * zs + z].astype(F32) for z in range(zs))
        hidden = (residual_ref[:, columns].astype(F32) + projected).astype(BF16)
        hidden_ref[:, columns] = hidden
        wide = hidden.astype(F32)
        square_sum += jnp.sum(wide * wide, axis=1, keepdims=True)
        pieces.append(wide)
    inverse = lax.rsqrt(square_sum / model_width + 1e-06)
    for y in range(CY):
        columns = slice(y * width, (y + 1) * width)
        normed = (pieces[y] * inverse * gain_ref[:, columns].astype(F32)).astype(BF16)
        for z in range(ZHI):
            ext_ref[z, :, columns] = normed
    for z in range(ZHI):
        ext_ref[z, :, model_width:] = meta_ref[...]


def slot_hits(meta, zhi, slots, slot_capacity):
    tokens = meta.shape[0]
    slot = lax.broadcasted_iota(I32, (tokens, slots), 1)
    dest = slot >> (slot_capacity.bit_length() - 1)
    expert = (dest >> 1) * (ZHI * ZLO) + zhi * ZLO + (dest & 1)
    hits = [meta[:, k : k + 1].astype(F32).astype(I32) == expert for k in range(TOP)]
    named = sum(h.astype(F32) for h in hits)
    later = lax.broadcasted_iota(I32, (tokens, tokens), 0) > lax.broadcasted_iota(
        I32, (tokens, tokens), 1
    )
    earlier = jnp.dot(later.astype(BF16), named.astype(BF16), preferred_element_type=F32)
    place = (slot & (slot_capacity - 1)).astype(F32)
    chosen = jnp.where((named > 0.5) & (earlier == place), 1.0, 0.0)
    return hits, chosen


def dispatch_kernel(zhi_ref, ext_ref, rows_ref):
    tokens = ext_ref.shape[0] * ext_ref.shape[1]
    ext_width = ext_ref.shape[2]
    model_width = ext_width - LANES
    slots = rows_ref.shape[0]
    meta = ext_ref[:, :, model_width:].reshape(tokens, LANES)
    hits, chosen = slot_hits(meta, zhi_ref[0], slots, tokens // SUB * CAP)
    masks = sum(
        jnp.where(hits[k], meta[:, TOP + k : TOP + k + 1].astype(F32), 0.0) for k in range(TOP)
    )
    along = (((0,), (0,)), ((), ()))
    pick = chosen.astype(BF16)
    normed = ext_ref[:, :, :model_width].reshape(tokens, model_width)
    rows_ref[:, :model_width] = lax.dot_general(
        pick, normed, along, preferred_element_type=F32
    ).astype(BF16)
    masked = (masks * chosen).astype(BF16)
    ones = jnp.ones((tokens, LANES), BF16)
    rows_ref[:, model_width:] = lax.dot_general(
        masked, ones, along, preferred_element_type=F32
    ).astype(BF16)


def weight_kernel(zhi_ref, ext_ref, router_ref, out_ref):
    tokens = ext_ref.shape[0] * ext_ref.shape[1]
    model_width = ext_ref.shape[2] - LANES
    slots = out_ref.shape[1]
    meta = ext_ref[:, :, model_width:].reshape(tokens, LANES)
    normed = ext_ref[:, :, :model_width].reshape(tokens, model_width)
    logits = jnp.dot(normed, router_ref[...], preferred_element_type=F32)
    lanes = lax.broadcasted_iota(I32, (tokens, EXPERTS), 1)
    exps = []
    for k in range(TOP):
        route = meta[:, k : k + 1].astype(F32).astype(I32)
        picked = jnp.sum(jnp.where(lanes == route, logits, 0.0), axis=1, keepdims=True)
        exps.append(jnp.exp(picked))
    total = sum(exps)
    hits, chosen = slot_hits(meta, zhi_ref[0], slots, tokens // SUB * CAP)
    route_weight = sum(jnp.where(hits[k], exps[k] / total, 0.0) for k in range(TOP))
    out_ref[...] = route_weight * chosen


def expert_kernel(dp_ref, rows_ref, *refs):
    weights, out_ref = refs[:6], refs[6]
    model_width = out_ref.shape[1]
    masks = rows_ref[:, model_width:].astype(F32).astype(I32)
    blocks = MASK_BLOCKS // 2
    acts = []
    for part in range(2):
        gate_ref, up_ref = weights[3 * part], weights[3 * part + 1]
        first = (dp_ref[0] if part == 0 else 1 - dp_ref[0]) * blocks
        rows = rows_ref[:, :model_width]
        gate = jnp.dot(rows, gate_ref[...], preferred_element_type=F32)
        up = jnp.dot(rows, up_ref[...], preferred_element_type=F32)
        keep = jnp.concatenate(
            [(jnp.right_shift(masks, first + b) & 1).astype(F32) for b in range(blocks)], axis=1
        )
        acts.append((jax.nn.silu(gate) * up * keep).astype(BF16))
    step = 512
    for j in range(model_width // step):
        columns = slice(j * step, (j + 1) * step)
        total = jnp.dot(acts[0], weights[2][:, columns], preferred_element_type=F32)
        total += jnp.dot(acts[1], weights[5][:, columns], preferred_element_type=F32)
        out_ref[:, columns] = total.astype(BF16)


def combine_kernel(weight_ref, back_ref, out_ref):
    weight = weight_ref[...]
    high = weight.astype(BF16)
    rest = weight - high.astype(F32)
    middle = rest.astype(BF16)
    low = (rest - middle.astype(F32)).astype(BF16)
    stacked = jnp.concatenate([high, middle, low], axis=0)
    tokens = weight.shape[0]
    model_width = back_ref.shape[1]
    step = 1024
    for j in range(model_width // step):
        columns = slice(j * step, (j + 1) * step)
        parts = jnp.dot(stacked, back_ref[:, columns], preferred_element_type=F32)
        total = parts[:tokens] + parts[tokens : 2 * tokens] + parts[2 * tokens :]
        out_ref[:, :, columns] = total.astype(BF16).reshape(tokens // SUB, SUB, step)


def swap(n):
    return [(i, i ^ 1) for i in range(n)]


def ring(n, step):
    return [(i, (i + step) % n) for i in range(n)]


def exchange(x, axes):
    return lax.all_to_all(x, axes, split_axis=0, concat_axis=0, tiled=True)


def local(
    queries,
    keys,
    attention_values,
    key_start,
    out_weight,
    residual,
    norm_gain,
    router_weight,
    routes,
    block_masks,
    gate_weight,
    up_weight,
    down_weight,
):
    dp = lax.axis_index("dp").astype(I32)
    ctx = lax.axis_index(CTX).astype(I32)
    zhi, zlo = lax.axis_index("zhi").astype(I32), lax.axis_index("zlo").astype(I32)
    tokens = queries.shape[1]
    model_width = residual.shape[2]
    token_rows = residual.shape[1]
    ctx_count = CY * CX
    scalar = lambda v: v.reshape(1)

    with jax.named_scope("keys_values"):
        heads = queries.shape[2] // HEAD_SIZE
        kv_head = (zhi * ZLO + zlo) * heads // (QUERY_HEADS // KEY_VALUE_HEADS)
        own_kv = jnp.concatenate(
            [
                lax.dynamic_slice_in_dim(a[0], kv_head * HEAD_SIZE, HEAD_SIZE, 1)
                for a in (keys, attention_values)
            ],
            axis=1,
        )
        all_kv = exchange(jnp.broadcast_to(own_kv[None], (ctx_count,) + own_kv.shape), CTX)

    with jax.named_scope("out_weight"):
        half = out_weight.shape[0] // 2
        own_half = lax.dynamic_slice_in_dim(out_weight, dp * half, half, 0)
        pair = jnp.stack([own_half, lax.ppermute(own_half, "zlo", swap(ZLO))])
        from_left = lax.ppermute(pair, "cx", ring(CX, 1))
        from_right = lax.ppermute(pair, "cx", ring(CX, -1))
        all_kv, from_left, from_right = lax.optimization_barrier((all_kv, from_left, from_right))
        far = [
            lax.ppermute(from_left[0], "cx", ring(CX, 1)),
            lax.ppermute(from_right[1], "cx", ring(CX, -1)),
        ]
        near_weight = [pair, from_left, from_right] + far
        far_weight = [lax.ppermute(w, "dp", swap(2)) for w in near_weight[:3]]

    with jax.named_scope("attention"):
        attended = call(
            attend_kernel,
            jax.ShapeDtypeStruct((CY * ZLO, tokens // ZLO, queries.shape[2]), BF16),
            (queries[0], all_kv, key_start.reshape(tokens, 1)),
            vmem=16,
            scalars=(scalar(ctx * tokens),),
            scratch=[pltpu.VMEM((tokens, ctx_count * tokens), F32)],
            flops=4 * tokens * heads * ctx_count * tokens * HEAD_SIZE,
            moved=4 << 20,
        )
        attended, far, far_weight = lax.optimization_barrier((attended, far, far_weight))
        near_weight = near_weight[:3] + far
        far_weight = far_weight + [lax.ppermute(w, "dp", swap(2)) for w in far]
        gathered = exchange(attended, ("cy", "zlo"))
        gathered = gathered.reshape(CY, ZLO, tokens // ZLO, queries.shape[2])

    with jax.named_scope("expert_weights"):
        own_experts = [a[0] for a in (gate_weight, up_weight, down_weight)]
        gathered, *sent_experts = lax.optimization_barrier((gathered, *own_experts))
        other_experts = [lax.ppermute(a, "dp", swap(2)) for a in sent_experts]

    with jax.named_scope("projection"):
        partial = call(
            project_kernel,
            jax.ShapeDtypeStruct((CY * ZHI, SUB, model_width // CY), BF16),
            (gathered, *near_weight, *far_weight),
            vmem=12,
            scalars=(scalar(dp), scalar(lax.axis_index("cx").astype(I32)), scalar(zlo)),
            flops=2 * 512 * 1024 * 1024,
            moved=6 << 20,
        )
        parts = exchange(partial, ("cy", "zhi"))
        parts, other_experts = lax.optimization_barrier((parts, other_experts))

    with jax.named_scope("norm"):
        meta = jnp.concatenate([routes[0], block_masks[0]], axis=1).astype(BF16)
        meta = jnp.pad(meta, ((0, 0), (0, LANES - 2 * TOP)))
        ext, hidden_state = call(
            norm_kernel,
            [
                jax.ShapeDtypeStruct((ZHI, token_rows, model_width + LANES), BF16),
                jax.ShapeDtypeStruct((token_rows, model_width), BF16),
            ],
            (parts, residual[0], norm_gain.reshape(1, model_width), meta),
            vmem=6,
            moved=2 << 20,
        )
        near_ext = exchange(ext, "zhi")

    with jax.named_scope("dispatch"):
        dests = ctx_count * ZLO
        capacity = ZHI * token_rows // SUB * CAP
        slots = dests * capacity
        rows = call(
            dispatch_kernel,
            jax.ShapeDtypeStruct((slots, model_width + LANES), BF16),
            (near_ext,),
            vmem=16,
            scalars=(scalar(zhi),),
            flops=2 * slots * 64 * model_width,
            moved=3 << 20,
        )
        slot_weight = call(
            weight_kernel,
            jax.ShapeDtypeStruct((ZHI * token_rows, slots), F32),
            (near_ext, router_weight),
            vmem=8,
            scalars=(scalar(zhi),),
            flops=2 * 64 * EXPERTS * model_width,
            moved=2 << 20,
        )
        over = ("cy", "cx", "zlo")
        got = exchange(rows.reshape(dests, capacity, model_width + LANES), over)

    with jax.named_scope("experts"):
        every = own_experts + other_experts
        expert_out = call(
            expert_kernel,
            jax.ShapeDtypeStruct((slots, model_width), BF16),
            (got.reshape(slots, model_width + LANES), *every),
            vmem=26,
            scalars=(scalar(dp),),
            flops=6 * slots * model_width * 768,
            moved=22 << 20,
        )
        back = exchange(expert_out.reshape(dests, capacity, model_width), over)

    with jax.named_scope("combine"):
        mixed = call(
            combine_kernel,
            jax.ShapeDtypeStruct((ZHI, token_rows, model_width), BF16),
            (slot_weight, back.reshape(slots, model_width)),
            vmem=14,
            flops=6 * 64 * slots * model_width,
            moved=3 << 20,
        )
        mixture = jnp.sum(exchange(mixed, "zhi").astype(F32), axis=0)
        layer_out = (hidden_state.astype(F32) + mixture).astype(BF16)
    return layer_out[None]


def solution(mesh):
    fine = Mesh(
        mesh.devices.reshape(2, CY, CX, ZHI, ZLO), ("dp", "cy", "cx", "zhi", "zlo")
    )
    tp = ("zhi", "zlo")
    all_ctx = CTX + tp
    in_specs = (
        P("dp", CTX, tp),
        P("dp", CTX, None),
        P("dp", CTX, None),
        P("dp", CTX),
        P(tp, CTX),
        P("dp", all_ctx, None),
        P(),
        P(),
        P("dp", all_ctx, None),
        P("dp", all_ctx, None),
        P(all_ctx, None, "dp"),
        P(all_ctx, None, "dp"),
        P(all_ctx, "dp", None),
    )
    out_specs = P("dp", all_ctx, None)
    return jax.shard_map(local, mesh=fine, in_specs=in_specs, out_specs=out_specs, check_vma=False)
```

```python
import math

import jax
import jax.numpy as jnp
from jax import lax
from jax.experimental import pallas as pl
from jax.experimental.pallas import tpu as pltpu
from jax.sharding import Mesh
from jax.sharding import PartitionSpec as P

QUERY_HEADS = 64
KEY_VALUE_HEADS = 4
HEAD_SIZE = 128
MASK_BLOCKS = 6
TOP = 8
EXPERTS = 128
CAP = 2
SCORE_FLOOR = -1e30
LANES = 128
SUB = 16
MIB = 1024 * 1024

CY, CX, ZHI, ZLO = 4, 4, 4, 2
CTX = ("cy", "cx")
F32, BF16, I32 = jnp.float32, jnp.bfloat16, jnp.int32


def call(kernel, out_shape, args, vmem, scalars=(), any_args=(), scratch=(), flops=0, moved=0):
    specs = [pl.BlockSpec(memory_space=pltpu.SMEM) for _ in scalars]
    specs += [pl.BlockSpec(memory_space=pltpu.VMEM) for _ in args]
    specs += [pl.BlockSpec(memory_space=pl.ANY) for _ in any_args]
    many = isinstance(out_shape, (list, tuple))
    whole = pl.BlockSpec(memory_space=pltpu.VMEM)
    return pl.pallas_call(
        kernel,
        out_shape=out_shape,
        in_specs=specs,
        out_specs=[whole] * len(out_shape) if many else whole,
        scratch_shapes=list(scratch),
        cost_estimate=pl.CostEstimate(flops=flops, bytes_accessed=moved, transcendentals=0),
        compiler_params=pltpu.CompilerParams(vmem_limit_bytes=vmem * MIB),
    )(*scalars, *args, *any_args)


def head_kernel(head_ref, key_ref, value_ref, out_ref):
    columns = pl.ds(pl.multiple_of(head_ref[0] * HEAD_SIZE, HEAD_SIZE), HEAD_SIZE)
    pair = jnp.concatenate([key_ref[:, columns], value_ref[:, columns]], axis=1)
    for c in range(out_ref.shape[0]):
        out_ref[c] = pair


def attend_kernel(first_ref, query_ref, kv_ref, start_ref, out_ref, bias_ref):
    tokens = query_ref.shape[0]
    heads = query_ref.shape[1] // HEAD_SIZE
    keys = kv_ref.shape[0] * kv_ref.shape[1]
    key_rows = kv_ref[:, :, :HEAD_SIZE].reshape(keys, HEAD_SIZE)
    value_rows = kv_ref[:, :, HEAD_SIZE:].reshape(keys, HEAD_SIZE)
    position = first_ref[0] + lax.broadcasted_iota(I32, (tokens, keys), 0)
    key_pos = lax.broadcasted_iota(I32, (tokens, keys), 1)
    visible = (key_pos >= start_ref[...]) & (key_pos <= position)
    bias_ref[...] = jnp.where(visible, 0.0, SCORE_FLOOR)
    scale = math.log2(math.e) / math.sqrt(HEAD_SIZE)
    for head in range(heads):
        columns = slice(head * HEAD_SIZE, (head + 1) * HEAD_SIZE)
        scores = lax.dot_general(
            query_ref[:, columns], key_rows, (((1,), (1,)), ((), ())), preferred_element_type=F32
        )
        scores = scores * scale + bias_ref[...]
        row_max = jnp.max(scores, axis=1, keepdims=True)
        weights = jnp.exp2(scores - row_max)
        row_sum = jnp.sum(weights, axis=1, keepdims=True)
        mixed = jnp.dot(weights.astype(BF16), value_rows, preferred_element_type=F32)
        attended = (mixed / row_sum).astype(BF16)
        for z in range(ZHI * ZLO):
            block = attended[z * SUB : (z + 1) * SUB]
            rows = slice((z // ZLO) * SUB, (z // ZLO + 1) * SUB)
            for y in range(CY):
                out_ref[y * ZLO + z % ZLO, rows, columns] = block


def project_kernel(dp_ref, x_ref, zlo_ref, att_ref, *refs):
    out_ref = refs[-1]
    pieces = (refs[:5], refs[5:10])
    half, width = refs[3].shape
    rows = att_ref.shape[0] * att_ref.shape[2]
    for step, away in enumerate((0, CX - 1, 1, 2)):
        total = jnp.zeros((rows, width), F32)
        for near in range(ZLO):
            source = zlo_ref[0] if near == 0 else 1 - zlo_ref[0]
            for refs_of, part in ((pieces[0], dp_ref[0]), (pieces[1], 1 - dp_ref[0])):
                weight = refs_of[3 + near][...] if step == 3 else refs_of[step][near]
                columns = pl.ds(pl.multiple_of(part * half, half), half)
                total += jnp.dot(
                    att_ref[:, source, :, columns].reshape(rows, half),
                    weight,
                    preferred_element_type=F32,
                )
        place = pl.multiple_of(((x_ref[0] + away) & (CX - 1)) * width, width)
        out_ref[:, :, pl.ds(place, width)] = total.astype(BF16).reshape(rows // SUB, SUB, width)


def norm_kernel(parts_ref, residual_ref, gain_ref, meta_ref, ext_ref, hidden_ref):
    model_width = residual_ref.shape[1]
    width = model_width // CY
    zs = ZHI
    pieces = []
    square_sum = jnp.zeros((SUB, 1), F32)
    for y in range(CY):
        columns = slice(y * width, (y + 1) * width)
        projected = sum(parts_ref[y * zs + z].astype(F32) for z in range(zs))
        hidden = (residual_ref[:, columns].astype(F32) + projected).astype(BF16)
        hidden_ref[:, columns] = hidden
        wide = hidden.astype(F32)
        square_sum += jnp.sum(wide * wide, axis=1, keepdims=True)
        pieces.append(wide)
    inverse = lax.rsqrt(square_sum / model_width + 1e-06)
    for y in range(CY):
        columns = slice(y * width, (y + 1) * width)
        normed = (pieces[y] * inverse * gain_ref[:, columns].astype(F32)).astype(BF16)
        for z in range(ZHI):
            ext_ref[z, :, columns] = normed
    for z in range(ZHI):
        ext_ref[z, :, model_width:] = meta_ref[...]


def slot_hits(meta, zhi, slots, slot_capacity):
    tokens = meta.shape[0]
    slot = lax.broadcasted_iota(I32, (tokens, slots), 1)
    dest = slot >> (slot_capacity.bit_length() - 1)
    expert = (dest >> 1) * (ZHI * ZLO) + zhi * ZLO + (dest & 1)
    hits = [meta[:, k : k + 1].astype(F32).astype(I32) == expert for k in range(TOP)]
    named = sum(h.astype(F32) for h in hits)
    later = lax.broadcasted_iota(I32, (tokens, tokens), 0) > lax.broadcasted_iota(
        I32, (tokens, tokens), 1
    )
    earlier = jnp.dot(later.astype(BF16), named.astype(BF16), preferred_element_type=F32)
    place = (slot & (slot_capacity - 1)).astype(F32)
    chosen = jnp.where((named > 0.5) & (earlier == place), 1.0, 0.0)
    return hits, chosen


def dispatch_kernel(zhi_ref, ext_ref, rows_ref):
    tokens = ext_ref.shape[0] * ext_ref.shape[1]
    ext_width = ext_ref.shape[2]
    model_width = ext_width - LANES
    slots = rows_ref.shape[0]
    meta = ext_ref[:, :, model_width:].reshape(tokens, LANES)
    hits, chosen = slot_hits(meta, zhi_ref[0], slots, tokens // SUB * CAP)
    masks = sum(
        jnp.where(hits[k], meta[:, TOP + k : TOP + k + 1].astype(F32), 0.0) for k in range(TOP)
    )
    along = (((0,), (0,)), ((), ()))
    pick = chosen.astype(BF16)
    normed = ext_ref[:, :, :model_width].reshape(tokens, model_width)
    rows_ref[:, :model_width] = lax.dot_general(
        pick, normed, along, preferred_element_type=F32
    ).astype(BF16)
    masked = (masks * chosen).astype(BF16)
    ones = jnp.ones((tokens, LANES), BF16)
    rows_ref[:, model_width:] = lax.dot_general(
        masked, ones, along, preferred_element_type=F32
    ).astype(BF16)


def weight_kernel(zhi_ref, ext_ref, router_ref, out_ref):
    tokens = ext_ref.shape[0] * ext_ref.shape[1]
    model_width = ext_ref.shape[2] - LANES
    slots = out_ref.shape[1]
    meta = ext_ref[:, :, model_width:].reshape(tokens, LANES)
    normed = ext_ref[:, :, :model_width].reshape(tokens, model_width)
    logits = jnp.dot(normed, router_ref[...], preferred_element_type=F32)
    lanes = lax.broadcasted_iota(I32, (tokens, EXPERTS), 1)
    exps = []
    for k in range(TOP):
        route = meta[:, k : k + 1].astype(F32).astype(I32)
        picked = jnp.sum(jnp.where(lanes == route, logits, 0.0), axis=1, keepdims=True)
        exps.append(jnp.exp(picked))
    total = sum(exps)
    hits, chosen = slot_hits(meta, zhi_ref[0], slots, tokens // SUB * CAP)
    route_weight = sum(jnp.where(hits[k], exps[k] / total, 0.0) for k in range(TOP))
    out_ref[...] = route_weight * chosen


def expert_kernel(dp_ref, rows_ref, *refs):
    weights, out_ref, held, sems = refs[:6], refs[6], refs[7:13], refs[13]
    copies = [pltpu.make_async_copy(weights[i], held[i], sems.at[i]) for i in range(6)]
    for i in (0, 1, 3, 4, 2, 5):
        copies[i].start()
    model_width = out_ref.shape[1]
    masks = rows_ref[:, model_width:].astype(F32).astype(I32)
    blocks = MASK_BLOCKS // 2
    acts = []
    for part in range(2):
        gate_ref, up_ref = held[3 * part], held[3 * part + 1]
        first = (dp_ref[0] if part == 0 else 1 - dp_ref[0]) * blocks
        copies[3 * part].wait()
        copies[3 * part + 1].wait()
        both = jnp.dot(
            rows_ref[:, :model_width],
            jnp.concatenate([gate_ref[...], up_ref[...]], axis=1),
            preferred_element_type=F32,
        )
        units = gate_ref.shape[1]
        keep = jnp.concatenate(
            [(jnp.right_shift(masks, first + b) & 1).astype(F32) for b in range(blocks)], axis=1
        )
        acts.append((jax.nn.silu(both[:, :units]) * both[:, units:] * keep).astype(BF16))
    copies[2].wait()
    copies[5].wait()
    activated = jnp.concatenate(acts, axis=1)
    step = 512
    for j in range(model_width // step):
        columns = slice(j * step, (j + 1) * step)
        down = jnp.concatenate([held[2][:, columns], held[5][:, columns]], axis=0)
        out_ref[:, columns] = jnp.dot(activated, down, preferred_element_type=F32).astype(BF16)


def combine_kernel(weight_ref, back_ref, out_ref):
    weight = weight_ref[...]
    high = weight.astype(BF16)
    rest = weight - high.astype(F32)
    middle = rest.astype(BF16)
    low = (rest - middle.astype(F32)).astype(BF16)
    stacked = jnp.concatenate([high, middle, low], axis=0)
    tokens = weight.shape[0]
    model_width = back_ref.shape[1]
    step = 1024
    for j in range(model_width // step):
        columns = slice(j * step, (j + 1) * step)
        parts = jnp.dot(stacked, back_ref[:, columns], preferred_element_type=F32)
        total = parts[:tokens] + parts[tokens : 2 * tokens] + parts[2 * tokens :]
        out_ref[:, :, columns] = total.astype(BF16).reshape(tokens // SUB, SUB, step)


def swap(n):
    return [(i, i ^ 1) for i in range(n)]


def ring(n, step):
    return [(i, (i + step) % n) for i in range(n)]


def exchange(x, axes):
    return lax.all_to_all(x, axes, split_axis=0, concat_axis=0, tiled=True)


def local(
    queries,
    keys,
    attention_values,
    key_start,
    out_weight,
    residual,
    norm_gain,
    router_weight,
    routes,
    block_masks,
    gate_weight,
    up_weight,
    down_weight,
):
    dp = lax.axis_index("dp").astype(I32)
    ctx = lax.axis_index(CTX).astype(I32)
    zhi, zlo = lax.axis_index("zhi").astype(I32), lax.axis_index("zlo").astype(I32)
    tokens = queries.shape[1]
    model_width = residual.shape[2]
    token_rows = residual.shape[1]
    ctx_count = CY * CX
    scalar = lambda v: v.reshape(1)

    with jax.named_scope("keys_values"):
        heads = queries.shape[2] // HEAD_SIZE
        kv_head = (zhi * ZLO + zlo) * heads // (QUERY_HEADS // KEY_VALUE_HEADS)
        copies = call(
            head_kernel,
            jax.ShapeDtypeStruct((ctx_count, tokens, 2 * HEAD_SIZE), BF16),
            (keys[0], attention_values[0]),
            vmem=4,
            scalars=(scalar(kv_head),),
            moved=2 << 20,
        )
        all_kv = exchange(copies, CTX)

    with jax.named_scope("out_weight"):
        half = out_weight.shape[0] // 2
        own_half = lax.dynamic_slice_in_dim(out_weight, dp * half, half, 0)
        beside = lax.ppermute(own_half, "zlo", swap(ZLO))
        far = lax.ppermute(own_half, "cx", ring(CX, 2))
        all_kv, beside, far = lax.optimization_barrier((all_kv, beside, far))
        pair = jnp.stack([own_half, beside])
        from_left = lax.ppermute(pair, "cx", ring(CX, 1))
        from_right = lax.ppermute(pair, "cx", ring(CX, -1))
        far_beside = lax.ppermute(far, "zlo", swap(ZLO))
        early = [pair, far, far_beside]
        early_other = [lax.ppermute(w, "dp", swap(2)) for w in early[:2]]

    with jax.named_scope("attention"):
        attended = call(
            attend_kernel,
            jax.ShapeDtypeStruct((CY * ZLO, tokens // ZLO, queries.shape[2]), BF16),
            (queries[0], all_kv, key_start.reshape(tokens, 1)),
            vmem=16,
            scalars=(scalar(ctx * tokens),),
            scratch=[pltpu.VMEM((tokens, ctx_count * tokens), F32)],
            flops=4 * tokens * heads * ctx_count * tokens * HEAD_SIZE,
            moved=4 << 20,
        )
        attended, early, early_other = lax.optimization_barrier((attended, early, early_other))
        gathered = exchange(attended, ("cy", "zlo"))
        gathered = gathered.reshape(CY, ZLO, tokens // ZLO, queries.shape[2])

    with jax.named_scope("out_weight"):
        gathered, from_left, from_right = lax.optimization_barrier((gathered, from_left, from_right))
        near_weight = [early[0], from_left, from_right, early[1], early[2]]
        late_other = [lax.ppermute(w, "dp", swap(2)) for w in (from_left, from_right, early[2])]
        far_weight = [early_other[0], late_other[0], late_other[1], early_other[1], late_other[2]]

    with jax.named_scope("projection"):
        partial = call(
            project_kernel,
            jax.ShapeDtypeStruct((CY * ZHI, SUB, model_width // CY), BF16),
            (gathered, *near_weight, *far_weight),
            vmem=12,
            scalars=(scalar(dp), scalar(lax.axis_index("cx").astype(I32)), scalar(zlo)),
            flops=2 * 512 * 1024 * 1024,
            moved=6 << 20,
        )
        own_experts = [a[0] for a in (gate_weight, up_weight, down_weight)]
        partial, *sent_experts = lax.optimization_barrier((partial, *own_experts))
        other_experts = [lax.ppermute(a, "dp", swap(2)) for a in sent_experts]
        parts = exchange(partial, ("cy", "zhi"))
        parts, other_experts = lax.optimization_barrier((parts, other_experts))

    with jax.named_scope("norm"):
        meta = jnp.concatenate([routes[0], block_masks[0]], axis=1).astype(BF16)
        meta = jnp.pad(meta, ((0, 0), (0, LANES - 2 * TOP)))
        ext, hidden_state = call(
            norm_kernel,
            [
                jax.ShapeDtypeStruct((ZHI, token_rows, model_width + LANES), BF16),
                jax.ShapeDtypeStruct((token_rows, model_width), BF16),
            ],
            (parts, residual[0], norm_gain.reshape(1, model_width), meta),
            vmem=6,
            moved=2 << 20,
        )
        near_ext = exchange(ext, "zhi")

    with jax.named_scope("dispatch"):
        dests = ctx_count * ZLO
        capacity = ZHI * token_rows // SUB * CAP
        slots = dests * capacity
        rows = call(
            dispatch_kernel,
            jax.ShapeDtypeStruct((slots, model_width + LANES), BF16),
            (near_ext,),
            vmem=16,
            scalars=(scalar(zhi),),
            flops=2 * slots * 64 * model_width,
            moved=3 << 20,
        )
        slot_weight = call(
            weight_kernel,
            jax.ShapeDtypeStruct((ZHI * token_rows, slots), F32),
            (near_ext, router_weight),
            vmem=8,
            scalars=(scalar(zhi),),
            flops=2 * 64 * EXPERTS * model_width,
            moved=2 << 20,
        )
        over = ("cy", "cx", "zlo")
        got = exchange(rows.reshape(dests, capacity, model_width + LANES), over)

    with jax.named_scope("experts"):
        every = own_experts + other_experts
        expert_out = call(
            expert_kernel,
            jax.ShapeDtypeStruct((slots, model_width), BF16),
            (got.reshape(slots, model_width + LANES),),
            vmem=32,
            scalars=(scalar(dp),),
            any_args=every,
            scratch=[pltpu.VMEM(a.shape, a.dtype) for a in every] + [pltpu.SemaphoreType.DMA((6,))],
            flops=6 * slots * model_width * 768,
            moved=22 << 20,
        )
        back = exchange(expert_out.reshape(dests, capacity, model_width), over)

    with jax.named_scope("combine"):
        mixed = call(
            combine_kernel,
            jax.ShapeDtypeStruct((ZHI, token_rows, model_width), BF16),
            (slot_weight, back.reshape(slots, model_width)),
            vmem=14,
            flops=6 * 64 * slots * model_width,
            moved=3 << 20,
        )
        mixture = jnp.sum(exchange(mixed, "zhi").astype(F32), axis=0)
        layer_out = (hidden_state.astype(F32) + mixture).astype(BF16)
    return layer_out[None]


def solution(mesh):
    fine = Mesh(
        mesh.devices.reshape(2, CY, CX, ZHI, ZLO), ("dp", "cy", "cx", "zhi", "zlo")
    )
    tp = ("zhi", "zlo")
    all_ctx = CTX + tp
    in_specs = (
        P("dp", CTX, tp),
        P("dp", CTX, None),
        P("dp", CTX, None),
        P("dp", CTX),
        P(tp, CTX),
        P("dp", all_ctx, None),
        P(),
        P(),
        P("dp", all_ctx, None),
        P("dp", all_ctx, None),
        P(all_ctx, None, "dp"),
        P(all_ctx, None, "dp"),
        P(all_ctx, "dp", None),
    )
    out_specs = P("dp", all_ctx, None)
    return jax.shard_map(local, mesh=fine, in_specs=in_specs, out_specs=out_specs, check_vma=False)
```

```python
import math

import jax
import jax.numpy as jnp
from jax import lax
from jax.experimental import pallas as pl
from jax.experimental.pallas import tpu as pltpu
from jax.sharding import Mesh
from jax.sharding import PartitionSpec as P

QUERY_HEADS = 64
KEY_VALUE_HEADS = 4
HEAD_SIZE = 128
MASK_BLOCKS = 6
TOP = 8
EXPERTS = 128
CAP = 2
SCORE_FLOOR = -1e30
LANES = 128
SUB = 16
MIB = 1024 * 1024

CY, CX, ZHI, ZLO = 4, 4, 4, 2
CTX = ("cy", "cx")
F32, BF16, I32 = jnp.float32, jnp.bfloat16, jnp.int32


def call(kernel, out_shape, args, vmem, scalars=(), any_args=(), scratch=(), flops=0, moved=0):
    specs = [pl.BlockSpec(memory_space=pltpu.SMEM) for _ in scalars]
    specs += [pl.BlockSpec(memory_space=pltpu.VMEM) for _ in args]
    specs += [pl.BlockSpec(memory_space=pl.ANY) for _ in any_args]
    many = isinstance(out_shape, (list, tuple))
    whole = pl.BlockSpec(memory_space=pltpu.VMEM)
    return pl.pallas_call(
        kernel,
        out_shape=out_shape,
        in_specs=specs,
        out_specs=[whole] * len(out_shape) if many else whole,
        scratch_shapes=list(scratch),
        cost_estimate=pl.CostEstimate(flops=flops, bytes_accessed=moved, transcendentals=0),
        compiler_params=pltpu.CompilerParams(vmem_limit_bytes=vmem * MIB),
    )(*scalars, *args, *any_args)


def head_kernel(head_ref, key_ref, value_ref, out_ref, pair_ref, sems):
    columns = pl.ds(pl.multiple_of(head_ref[0] * HEAD_SIZE, HEAD_SIZE), HEAD_SIZE)
    copies = [
        pltpu.make_async_copy(ref.at[:, columns], pair_ref.at[i], sems.at[i])
        for i, ref in enumerate((key_ref, value_ref))
    ]
    for copy in copies:
        copy.start()
    for copy in copies:
        copy.wait()
    pair = jnp.concatenate([pair_ref[0], pair_ref[1]], axis=1)
    for c in range(out_ref.shape[0]):
        out_ref[c] = pair


def attend_kernel(first_ref, query_ref, kv_ref, start_ref, out_ref, bias_ref):
    tokens = query_ref.shape[0]
    heads = query_ref.shape[1] // HEAD_SIZE
    keys = kv_ref.shape[0] * kv_ref.shape[1]
    key_rows = kv_ref[:, :, :HEAD_SIZE].reshape(keys, HEAD_SIZE)
    value_rows = kv_ref[:, :, HEAD_SIZE:].reshape(keys, HEAD_SIZE)
    position = first_ref[0] + lax.broadcasted_iota(I32, (tokens, keys), 0)
    key_pos = lax.broadcasted_iota(I32, (tokens, keys), 1)
    visible = (key_pos >= start_ref[...]) & (key_pos <= position)
    bias_ref[...] = jnp.where(visible, 0.0, SCORE_FLOOR)
    scale = math.log2(math.e) / math.sqrt(HEAD_SIZE)
    for head in range(heads):
        columns = slice(head * HEAD_SIZE, (head + 1) * HEAD_SIZE)
        scores = lax.dot_general(
            query_ref[:, columns], key_rows, (((1,), (1,)), ((), ())), preferred_element_type=F32
        )
        scores = scores * scale + bias_ref[...]
        row_max = jnp.max(scores, axis=1, keepdims=True)
        weights = jnp.exp2(scores - row_max)
        row_sum = jnp.sum(weights, axis=1, keepdims=True)
        mixed = jnp.dot(weights.astype(BF16), value_rows, preferred_element_type=F32)
        attended = (mixed / row_sum).astype(BF16)
        for z in range(ZHI * ZLO):
            block = attended[z * SUB : (z + 1) * SUB]
            rows = slice((z // ZLO) * SUB, (z // ZLO + 1) * SUB)
            for y in range(CY):
                out_ref[y * ZLO + z % ZLO, rows, columns] = block


def project_kernel(dp_ref, x_ref, zlo_ref, att_ref, *refs):
    out_ref = refs[-1]
    pieces = (refs[:5], refs[5:10])
    half, width = refs[3].shape
    rows = att_ref.shape[0] * att_ref.shape[2]
    for step, away in enumerate((0, CX - 1, 1, 2)):
        total = jnp.zeros((rows, width), F32)
        for near in range(ZLO):
            source = zlo_ref[0] if near == 0 else 1 - zlo_ref[0]
            for refs_of, part in ((pieces[0], dp_ref[0]), (pieces[1], 1 - dp_ref[0])):
                weight = refs_of[3 + near][...] if step == 3 else refs_of[step][near]
                columns = pl.ds(pl.multiple_of(part * half, half), half)
                total += jnp.dot(
                    att_ref[:, source, :, columns].reshape(rows, half),
                    weight,
                    preferred_element_type=F32,
                )
        place = pl.multiple_of(((x_ref[0] + away) & (CX - 1)) * width, width)
        out_ref[:, :, pl.ds(place, width)] = total.astype(BF16).reshape(rows // SUB, SUB, width)


def norm_kernel(parts_ref, residual_ref, gain_ref, meta_ref, first_ref, second_ref, hidden_ref):
    model_width = residual_ref.shape[1]
    width = model_width // CY
    zs = ZHI
    pieces = []
    square_sum = jnp.zeros((SUB, 1), F32)
    for y in range(CY):
        columns = slice(y * width, (y + 1) * width)
        projected = sum(parts_ref[y * zs + z].astype(F32) for z in range(zs))
        hidden = (residual_ref[:, columns].astype(F32) + projected).astype(BF16)
        hidden_ref[:, columns] = hidden
        wide = hidden.astype(F32)
        square_sum += jnp.sum(wide * wide, axis=1, keepdims=True)
        pieces.append(wide)
    inverse = lax.rsqrt(square_sum / model_width + 1e-06)
    for y in range(CY):
        columns = slice(y * width, (y + 1) * width)
        normed = (pieces[y] * inverse * gain_ref[:, columns].astype(F32)).astype(BF16)
        out_ref = first_ref if y < CY // 2 else second_ref
        place = (y % (CY // 2)) * width
        out_ref[:, place : place + width] = normed
    first_ref[:, model_width // 2 :] = meta_ref[...]


def slot_hits(meta, zhi, slots, slot_capacity):
    tokens = meta.shape[0]
    slot = lax.broadcasted_iota(I32, (tokens, slots), 1)
    dest = slot >> (slot_capacity.bit_length() - 1)
    expert = (dest >> 1) * (ZHI * ZLO) + zhi * ZLO + (dest & 1)
    hits = [meta[:, k : k + 1].astype(F32).astype(I32) == expert for k in range(TOP)]
    named = sum(h.astype(F32) for h in hits)
    later = lax.broadcasted_iota(I32, (tokens, tokens), 0) > lax.broadcasted_iota(
        I32, (tokens, tokens), 1
    )
    earlier = jnp.dot(later.astype(BF16), named.astype(BF16), preferred_element_type=F32)
    place = (slot & (slot_capacity - 1)).astype(F32)
    chosen = jnp.where((named > 0.5) & (earlier == place), 1.0, 0.0)
    return hits, chosen


def dispatch_kernel(zhi_ref, *refs):
    pieces, rows_ref, chosen_ref = refs[:ZHI], refs[ZHI], refs[ZHI + 1]
    ext = jnp.concatenate([piece[...] for piece in pieces], axis=0)
    tokens = ext.shape[0]
    width = ext.shape[1] - LANES
    slots = rows_ref.shape[0]
    meta = ext[:, width:]
    hits, chosen = slot_hits(meta, zhi_ref[0], slots, tokens // SUB * CAP)
    masks = sum(
        jnp.where(hits[k], meta[:, TOP + k : TOP + k + 1].astype(F32), 0.0) for k in range(TOP)
    )
    chosen_ref[...] = chosen.astype(BF16)
    rows_ref[:, :width] = pick_rows(chosen.astype(BF16), ext[:, :width])
    ones = jnp.ones((tokens, LANES), BF16)
    rows_ref[:, width:] = pick_rows((masks * chosen).astype(BF16), ones)


def pick_rows(chosen, tokens):
    along = (((0,), (0,)), ((), ()))
    return lax.dot_general(chosen, tokens, along, preferred_element_type=F32).astype(BF16)


def pick_kernel(chosen_ref, *refs):
    refs[-1][...] = pick_rows(
        chosen_ref[...], jnp.concatenate([piece[...] for piece in refs[:-1]], axis=0)
    )


def weight_kernel(zhi_ref, router_ref, *refs):
    first, second, out_ref = refs[:ZHI], refs[ZHI : 2 * ZHI], refs[2 * ZHI]
    ext = jnp.concatenate([piece[...] for piece in first], axis=0)
    tokens = ext.shape[0]
    width = ext.shape[1] - LANES
    slots = out_ref.shape[1]
    meta = ext[:, width:]
    rest = jnp.concatenate([piece[...] for piece in second], axis=0)
    logits = jnp.dot(ext[:, :width], router_ref[:width], preferred_element_type=F32)
    logits += jnp.dot(rest, router_ref[width:], preferred_element_type=F32)
    lanes = lax.broadcasted_iota(I32, (tokens, EXPERTS), 1)
    exps = []
    for k in range(TOP):
        route = meta[:, k : k + 1].astype(F32).astype(I32)
        picked = jnp.sum(jnp.where(lanes == route, logits, 0.0), axis=1, keepdims=True)
        exps.append(jnp.exp(picked))
    total = sum(exps)
    hits, chosen = slot_hits(meta, zhi_ref[0], slots, tokens // SUB * CAP)
    route_weight = sum(jnp.where(hits[k], exps[k] / total, 0.0) for k in range(TOP))
    out_ref[...] = route_weight * chosen


def hidden_kernel(rows_ref, *refs):
    weights, out_ref, held, sems = refs[:4], refs[4], refs[5:9], refs[9]
    width = held[0].shape[0]
    copies = [
        pltpu.make_async_copy(weights[i].at[pl.ds(0, width)], held[i], sems.at[i]) for i in range(4)
    ]
    for copy in copies:
        copy.start()
    units = held[0].shape[1]
    for part in range(2):
        copies[2 * part].wait()
        copies[2 * part + 1].wait()
        out_ref[:, 2 * part * units : 2 * (part + 1) * units] = jnp.dot(
            rows_ref[:, :width],
            jnp.concatenate([held[2 * part][...], held[2 * part + 1][...]], axis=1),
            preferred_element_type=F32,
        )


def expert_kernel(dp_ref, mask_ref, rows_ref, begun_ref, *refs):
    weights, out_ref, held, sems = refs[:6], refs[6], refs[7:13], refs[13]
    width = rows_ref.shape[1]
    copies = [
        pltpu.make_async_copy(weights[i].at[pl.ds(width, width)], held[i], sems.at[i])
        for i in range(4)
    ]
    copies += [pltpu.make_async_copy(weights[i], held[i], sems.at[i]) for i in (4, 5)]
    for copy in copies:
        copy.start()
    model_width = out_ref.shape[1]
    masks = mask_ref[...].astype(F32).astype(I32)
    blocks = MASK_BLOCKS // 2
    units = held[0].shape[1]
    acts = []
    for part in range(2):
        first = (dp_ref[0] if part == 0 else 1 - dp_ref[0]) * blocks
        keep = jnp.concatenate(
            [(jnp.right_shift(masks, first + b) & 1).astype(F32) for b in range(blocks)], axis=1
        )
        copies[2 * part].wait()
        copies[2 * part + 1].wait()
        both = begun_ref[:, 2 * part * units : 2 * (part + 1) * units] + jnp.dot(
            rows_ref[...],
            jnp.concatenate([held[2 * part][...], held[2 * part + 1][...]], axis=1),
            preferred_element_type=F32,
        )
        acts.append((jax.nn.silu(both[:, :units]) * both[:, units:] * keep).astype(BF16))
    copies[4].wait()
    copies[5].wait()
    activated = jnp.concatenate(acts, axis=1)
    step = 512
    for j in range(model_width // step):
        columns = slice(j * step, (j + 1) * step)
        down = jnp.concatenate([held[4][:, columns], held[5][:, columns]], axis=0)
        out_ref[:, columns] = jnp.dot(activated, down, preferred_element_type=F32).astype(BF16)


def combine_kernel(zhi_ref, weight_ref, back_ref, out_ref):
    weight = weight_ref[...]
    high = weight.astype(BF16)
    rest = weight - high.astype(F32)
    middle = rest.astype(BF16)
    low = (rest - middle.astype(F32)).astype(BF16)
    stacked = jnp.concatenate([high, middle, low], axis=0)
    tokens = weight.shape[0]
    model_width = back_ref.shape[1]
    step = 1024
    for j in range(model_width // step):
        columns = slice(j * step, (j + 1) * step)
        parts = jnp.dot(stacked, back_ref[:, columns], preferred_element_type=F32)
        total = parts[:tokens] + parts[tokens : 2 * tokens] + parts[2 * tokens :]
        total = total.astype(BF16)
        for away in range(tokens // SUB):
            home = (zhi_ref[0] + ZHI - away) & (ZHI - 1)
            out_ref[home, :, columns] = total[away * SUB : (away + 1) * SUB]


def swap(n):
    return [(i, i ^ 1) for i in range(n)]


def ring(n, step):
    return [(i, (i + step) % n) for i in range(n)]


def exchange(x, axes):
    return lax.all_to_all(x, axes, split_axis=0, concat_axis=0, tiled=True)


def local(
    queries,
    keys,
    attention_values,
    key_start,
    out_weight,
    residual,
    norm_gain,
    router_weight,
    routes,
    block_masks,
    gate_weight,
    up_weight,
    down_weight,
):
    dp = lax.axis_index("dp").astype(I32)
    ctx = lax.axis_index(CTX).astype(I32)
    zhi, zlo = lax.axis_index("zhi").astype(I32), lax.axis_index("zlo").astype(I32)
    tokens = queries.shape[1]
    model_width = residual.shape[2]
    token_rows = residual.shape[1]
    ctx_count = CY * CX
    scalar = lambda v: v.reshape(1)

    with jax.named_scope("keys_values"):
        heads = queries.shape[2] // HEAD_SIZE
        kv_head = (zhi * ZLO + zlo) * heads // (QUERY_HEADS // KEY_VALUE_HEADS)
        copies = call(
            head_kernel,
            jax.ShapeDtypeStruct((ctx_count, tokens, 2 * HEAD_SIZE), BF16),
            (),
            vmem=40,
            scalars=(scalar(kv_head),),
            any_args=(keys[0], attention_values[0]),
            scratch=[pltpu.VMEM((2, tokens, HEAD_SIZE), BF16), pltpu.SemaphoreType.DMA((2,))],
            moved=2 << 20,
        )
        all_kv = exchange(copies, CTX)

    with jax.named_scope("out_weight"):
        half = out_weight.shape[0] // 2
        own_half = lax.dynamic_slice_in_dim(out_weight, dp * half, half, 0)
        beside = lax.ppermute(own_half, "zlo", swap(ZLO))
        far = lax.ppermute(own_half, "cx", ring(CX, 2))
        all_kv, beside, far = lax.optimization_barrier((all_kv, beside, far))
        pair = jnp.stack([own_half, beside])
        from_left = lax.ppermute(pair, "cx", ring(CX, 1))
        from_right = lax.ppermute(pair, "cx", ring(CX, -1))
        far_beside = lax.ppermute(far, "zlo", swap(ZLO))
        early = [pair, far, far_beside]
        early_other = [lax.ppermute(w, "dp", swap(2)) for w in early[:2]]

    with jax.named_scope("attention"):
        attended = call(
            attend_kernel,
            jax.ShapeDtypeStruct((CY * ZLO, tokens // ZLO, queries.shape[2]), BF16),
            (queries[0], all_kv, key_start.reshape(tokens, 1)),
            vmem=16,
            scalars=(scalar(ctx * tokens),),
            scratch=[pltpu.VMEM((tokens, ctx_count * tokens), F32)],
            flops=4 * tokens * heads * ctx_count * tokens * HEAD_SIZE,
            moved=4 << 20,
        )
        attended, early, early_other = lax.optimization_barrier((attended, early, early_other))
        gathered = exchange(attended, ("cy", "zlo"))
        gathered = gathered.reshape(CY, ZLO, tokens // ZLO, queries.shape[2])

    with jax.named_scope("out_weight"):
        gathered, from_left, from_right = lax.optimization_barrier((gathered, from_left, from_right))
        near_weight = [early[0], from_left, from_right, early[1], early[2]]
        late_other = [lax.ppermute(w, "dp", swap(2)) for w in (from_left, from_right, early[2])]
        far_weight = [early_other[0], late_other[0], late_other[1], early_other[1], late_other[2]]

    with jax.named_scope("projection"):
        partial = call(
            project_kernel,
            jax.ShapeDtypeStruct((CY * ZHI, SUB, model_width // CY), BF16),
            (gathered, *near_weight, *far_weight),
            vmem=12,
            scalars=(scalar(dp), scalar(lax.axis_index("cx").astype(I32)), scalar(zlo)),
            flops=2 * 512 * 1024 * 1024,
            moved=6 << 20,
        )
        own_experts = [a[0] for a in (gate_weight, up_weight, down_weight)]
        partial, *sent_experts = lax.optimization_barrier((partial, *own_experts))
        other_experts = [lax.ppermute(a, "dp", swap(2)) for a in sent_experts]
        parts = exchange(partial, ("cy", "zhi"))
        parts, other_experts = lax.optimization_barrier((parts, other_experts))

    with jax.named_scope("norm"):
        meta = jnp.concatenate([routes[0], block_masks[0]], axis=1).astype(BF16)
        meta = jnp.pad(meta, ((0, 0), (0, LANES - 2 * TOP)))
        half_width = model_width // 2
        first, second, hidden_state = call(
            norm_kernel,
            [
                jax.ShapeDtypeStruct((token_rows, half_width + LANES), BF16),
                jax.ShapeDtypeStruct((token_rows, half_width), BF16),
                jax.ShapeDtypeStruct((token_rows, model_width), BF16),
            ],
            (parts, residual[0], norm_gain.reshape(1, model_width), meta),
            vmem=6,
            moved=2 << 20,
        )
        firsts = [first] + [lax.ppermute(first, "zhi", ring(ZHI, step)) for step in range(1, ZHI)]
        firsts, second = lax.optimization_barrier((firsts, second))
        seconds = [second] + [lax.ppermute(second, "zhi", ring(ZHI, step)) for step in range(1, ZHI)]

    with jax.named_scope("dispatch"):
        dests = ctx_count * ZLO
        gathered_rows = ZHI * token_rows
        capacity = gathered_rows // SUB * CAP
        slots = dests * capacity
        over = ("cy", "cx", "zlo")
        rows, chosen = call(
            dispatch_kernel,
            [
                jax.ShapeDtypeStruct((slots, half_width + LANES), BF16),
                jax.ShapeDtypeStruct((gathered_rows, slots), BF16),
            ],
            firsts,
            vmem=12,
            scalars=(scalar(zhi),),
            flops=2 * slots * gathered_rows * half_width,
            moved=2 << 20,
        )
        got_first = exchange(rows.reshape(dests, capacity, half_width + LANES), over)
        got_first = got_first.reshape(slots, half_width + LANES)
        rows = call(
            pick_kernel,
            jax.ShapeDtypeStruct((slots, half_width), BF16),
            (chosen, *seconds),
            vmem=12,
            flops=2 * slots * gathered_rows * half_width,
            moved=2 << 20,
        )
        rows, got_first = lax.optimization_barrier((rows, got_first))
        got_second = exchange(rows.reshape(dests, capacity, half_width), over)
        got_second = got_second.reshape(slots, half_width)
        slot_weight = call(
            weight_kernel,
            jax.ShapeDtypeStruct((gathered_rows, slots), F32),
            (router_weight, *firsts, *seconds),
            vmem=8,
            scalars=(scalar(zhi),),
            flops=2 * gathered_rows * EXPERTS * model_width,
            moved=2 << 20,
        )

    with jax.named_scope("experts"):
        gates = own_experts[:2] + other_experts[:2]
        downs = [own_experts[2], other_experts[2]]
        units = gates[0].shape[1]
        half_held = [pltpu.VMEM((half_width, units), BF16) for _ in gates]
        begun = call(
            hidden_kernel,
            jax.ShapeDtypeStruct((slots, 4 * units), F32),
            (got_first,),
            vmem=20,
            any_args=gates,
            scratch=half_held + [pltpu.SemaphoreType.DMA((4,))],
            flops=2 * slots * model_width * 768,
            moved=9 << 20,
        )
        expert_out = call(
            expert_kernel,
            jax.ShapeDtypeStruct((slots, model_width), BF16),
            (got_first[:, half_width:], got_second, begun),
            vmem=32,
            scalars=(scalar(dp),),
            any_args=gates + downs,
            scratch=half_held
            + [pltpu.VMEM(a.shape, a.dtype) for a in downs]
            + [pltpu.SemaphoreType.DMA((6,))],
            flops=4 * slots * model_width * 768,
            moved=16 << 20,
        )
        back = exchange(expert_out.reshape(dests, capacity, model_width), over)

    with jax.named_scope("combine"):
        mixed = call(
            combine_kernel,
            jax.ShapeDtypeStruct((ZHI, token_rows, model_width), BF16),
            (slot_weight, back.reshape(slots, model_width)),
            vmem=14,
            scalars=(scalar(zhi),),
            flops=6 * gathered_rows * slots * model_width,
            moved=3 << 20,
        )
        mixture = jnp.sum(exchange(mixed, "zhi").astype(F32), axis=0)
        layer_out = (hidden_state.astype(F32) + mixture).astype(BF16)
    return layer_out[None]


def solution(mesh):
    fine = Mesh(
        mesh.devices.reshape(2, CY, CX, ZHI, ZLO), ("dp", "cy", "cx", "zhi", "zlo")
    )
    tp = ("zhi", "zlo")
    all_ctx = CTX + tp
    in_specs = (
        P("dp", CTX, tp),
        P("dp", CTX, None),
        P("dp", CTX, None),
        P("dp", CTX),
        P(tp, CTX),
        P("dp", all_ctx, None),
        P(),
        P(),
        P("dp", all_ctx, None),
        P("dp", all_ctx, None),
        P(all_ctx, None, "dp"),
        P(all_ctx, None, "dp"),
        P(all_ctx, "dp", None),
    )
    out_specs = P("dp", all_ctx, None)
    return jax.shard_map(local, mesh=fine, in_specs=in_specs, out_specs=out_specs, check_vma=False)
```

```python
import math

import jax
import jax.numpy as jnp
from jax import lax
from jax.experimental import pallas as pl
from jax.experimental.pallas import tpu as pltpu
from jax.sharding import Mesh
from jax.sharding import PartitionSpec as P

QUERY_HEADS = 64
KEY_VALUE_HEADS = 4
HEAD_SIZE = 128
MASK_BLOCKS = 6
TOP = 8
EXPERTS = 128
CAP = 2
SCORE_FLOOR = -1e30
LANES = 128
SUB = 16
MIB = 1024 * 1024

CY, CX, ZHI, ZLO = 4, 4, 4, 2
CTX = ("cy", "cx")
F32, BF16, I32 = jnp.float32, jnp.bfloat16, jnp.int32


def call(kernel, out_shape, args, vmem, scalars=(), any_args=(), scratch=(), flops=0, moved=0):
    specs = [pl.BlockSpec(memory_space=pltpu.SMEM) for _ in scalars]
    specs += [pl.BlockSpec(memory_space=pltpu.VMEM) for _ in args]
    specs += [pl.BlockSpec(memory_space=pl.ANY) for _ in any_args]
    many = isinstance(out_shape, (list, tuple))
    whole = pl.BlockSpec(memory_space=pltpu.VMEM)
    return pl.pallas_call(
        kernel,
        out_shape=out_shape,
        in_specs=specs,
        out_specs=[whole] * len(out_shape) if many else whole,
        scratch_shapes=list(scratch),
        cost_estimate=pl.CostEstimate(flops=flops, bytes_accessed=moved, transcendentals=0),
        compiler_params=pltpu.CompilerParams(vmem_limit_bytes=vmem * MIB),
    )(*scalars, *args, *any_args)


def head_kernel(head_ref, key_ref, value_ref, out_ref, pair_ref, sems):
    columns = pl.ds(pl.multiple_of(head_ref[0] * HEAD_SIZE, HEAD_SIZE), HEAD_SIZE)
    copies = [
        pltpu.make_async_copy(ref.at[:, columns], pair_ref.at[i], sems.at[i])
        for i, ref in enumerate((key_ref, value_ref))
    ]
    for copy in copies:
        copy.start()
    for copy in copies:
        copy.wait()
    pair = jnp.concatenate([pair_ref[0], pair_ref[1]], axis=1)
    for c in range(out_ref.shape[0]):
        out_ref[c] = pair


def attend_kernel(first_ref, kv_ref, start_ref, query_hbm, out_ref, bias_ref, query_ref, sem):
    copy = pltpu.make_async_copy(query_hbm, query_ref, sem.at[0])
    copy.start()
    tokens = query_ref.shape[0]
    heads = query_ref.shape[1] // HEAD_SIZE
    keys = kv_ref.shape[0] * kv_ref.shape[1]
    key_rows = kv_ref[:, :, :HEAD_SIZE].reshape(keys, HEAD_SIZE)
    value_rows = kv_ref[:, :, HEAD_SIZE:].reshape(keys, HEAD_SIZE)
    position = first_ref[0] + lax.broadcasted_iota(I32, (tokens, keys), 0)
    key_pos = lax.broadcasted_iota(I32, (tokens, keys), 1)
    visible = (key_pos >= start_ref[...]) & (key_pos <= position)
    bias_ref[...] = jnp.where(visible, 0.0, SCORE_FLOOR)
    copy.wait()
    scale = math.log2(math.e) / math.sqrt(HEAD_SIZE)
    for head in range(heads):
        columns = slice(head * HEAD_SIZE, (head + 1) * HEAD_SIZE)
        scores = lax.dot_general(
            query_ref[:, columns], key_rows, (((1,), (1,)), ((), ())), preferred_element_type=F32
        )
        scores = scores * scale + bias_ref[...]
        row_max = jnp.max(scores, axis=1, keepdims=True)
        weights = jnp.exp2(scores - row_max)
        row_sum = jnp.sum(weights, axis=1, keepdims=True)
        mixed = jnp.dot(weights.astype(BF16), value_rows, preferred_element_type=F32)
        attended = (mixed / row_sum).astype(BF16)
        for z in range(ZHI * ZLO):
            block = attended[z * SUB : (z + 1) * SUB]
            rows = slice((z // ZLO) * SUB, (z // ZLO + 1) * SUB)
            for y in range(CY):
                out_ref[y * ZLO + z % ZLO, rows, columns] = block


def project_kernel(dp_ref, zlo_ref, att_ref, *refs):
    count = 8
    sources, total_ref, held, sems = refs[:count], refs[count], refs[count + 1 : -1], refs[-1]
    copies = [pltpu.make_async_copy(a, b, sems.at[i]) for i, (a, b) in enumerate(zip(sources, held))]
    for copy in copies:
        copy.start()
    half = held[3].shape[0]
    rows = att_ref.shape[0] * att_ref.shape[2]

    def block(near, part):
        source = zlo_ref[0] if near == 0 else 1 - zlo_ref[0]
        columns = pl.ds(pl.multiple_of(part * half, half), half)
        return att_ref[:, source, :, columns].reshape(rows, half)

    def product(piece, near, part):
        copies[piece].wait() if near == 0 or piece in (4, 7) else None
        weight = held[piece][...] if len(held[piece].shape) == 2 else held[piece][near]
        return jnp.dot(block(near, part), weight, preferred_element_type=F32)

    mine, other = dp_ref[0], 1 - dp_ref[0]
    for step in range(3):
        total = product(step, 0, mine) + product(step, 1, mine)
        if step == 0:
            total += product(5, 0, other) + product(5, 1, other)
        total_ref[step] = total
    total_ref[3] = (
        product(3, 0, mine) + product(4, 1, mine) + product(6, 0, other) + product(7, 1, other)
    )


def finish_kernel(dp_ref, x_ref, zlo_ref, att_ref, total_ref, left_ref, right_ref, out_ref):
    half, width = left_ref.shape[1], left_ref.shape[2]
    rows = att_ref.shape[0] * att_ref.shape[2]
    columns = pl.ds(pl.multiple_of((1 - dp_ref[0]) * half, half), half)
    for step, away in enumerate((0, CX - 1, 1, 2)):
        total = total_ref[step]
        if step in (1, 2):
            piece_ref = left_ref if step == 1 else right_ref
            for near in range(ZLO):
                source = zlo_ref[0] if near == 0 else 1 - zlo_ref[0]
                total += jnp.dot(
                    att_ref[:, source, :, columns].reshape(rows, half),
                    piece_ref[near],
                    preferred_element_type=F32,
                )
        place = pl.multiple_of(((x_ref[0] + away) & (CX - 1)) * width, width)
        out_ref[:, :, pl.ds(place, width)] = total.astype(BF16).reshape(rows // SUB, SUB, width)


def norm_kernel(parts_ref, residual_ref, gain_ref, meta_ref, ext_ref, hidden_ref):
    model_width = residual_ref.shape[1]
    width = model_width // CY
    zs = ZHI
    pieces = []
    square_sum = jnp.zeros((SUB, 1), F32)
    for y in range(CY):
        columns = slice(y * width, (y + 1) * width)
        projected = sum(parts_ref[y * zs + z].astype(F32) for z in range(zs))
        hidden = (residual_ref[:, columns].astype(F32) + projected).astype(BF16)
        hidden_ref[:, columns] = hidden
        wide = hidden.astype(F32)
        square_sum += jnp.sum(wide * wide, axis=1, keepdims=True)
        pieces.append(wide)
    inverse = lax.rsqrt(square_sum / model_width + 1e-06)
    for y in range(CY):
        columns = slice(y * width, (y + 1) * width)
        normed = (pieces[y] * inverse * gain_ref[:, columns].astype(F32)).astype(BF16)
        ext_ref[:, columns] = normed
    ext_ref[:, model_width:] = meta_ref[...]


def slot_hits(meta, zhi, slots, slot_capacity):
    tokens = meta.shape[0]
    slot = lax.broadcasted_iota(I32, (tokens, slots), 1)
    dest = slot >> (slot_capacity.bit_length() - 1)
    expert = (dest >> 1) * (ZHI * ZLO) + zhi * ZLO + (dest & 1)
    hits = [meta[:, k : k + 1].astype(F32).astype(I32) == expert for k in range(TOP)]
    named = sum(h.astype(F32) for h in hits)
    later = lax.broadcasted_iota(I32, (tokens, tokens), 0) > lax.broadcasted_iota(
        I32, (tokens, tokens), 1
    )
    earlier = jnp.dot(later.astype(BF16), named.astype(BF16), preferred_element_type=F32)
    place = (slot & (slot_capacity - 1)).astype(F32)
    chosen = jnp.where((named > 0.5) & (earlier == place), 1.0, 0.0)
    return hits, chosen


def gathered_rows(refs):
    own, left, right, far_first, far_second = [ref[...] for ref in refs]
    far = jnp.concatenate([far_first, far_second], axis=1)
    return jnp.concatenate([own, left, right, far], axis=0)


def dispatch_kernel(zhi_ref, *refs):
    ext, rows_ref = gathered_rows(refs[:-1]), refs[-1]
    tokens = ext.shape[0]
    width = ext.shape[1] - LANES
    meta = ext[:, width:]
    hits, chosen = slot_hits(meta, zhi_ref[0], rows_ref.shape[0], tokens // SUB * CAP)
    masks = sum(
        jnp.where(hits[k], meta[:, TOP + k : TOP + k + 1].astype(F32), 0.0) for k in range(TOP)
    )
    along = (((0,), (0,)), ((), ()))
    rows_ref[:, :width] = lax.dot_general(
        chosen.astype(BF16), ext[:, :width], along, preferred_element_type=F32
    ).astype(BF16)
    ones = jnp.ones((tokens, LANES), BF16)
    rows_ref[:, width:] = lax.dot_general(
        (masks * chosen).astype(BF16), ones, along, preferred_element_type=F32
    ).astype(BF16)


def weight_kernel(zhi_ref, router_ref, *refs):
    ext, out_ref = gathered_rows(refs[:-1]), refs[-1]
    tokens = ext.shape[0]
    model_width = ext.shape[1] - LANES
    slots = out_ref.shape[1]
    meta, normed = ext[:, model_width:], ext[:, :model_width]
    logits = jnp.dot(normed, router_ref[...], preferred_element_type=F32)
    lanes = lax.broadcasted_iota(I32, (tokens, EXPERTS), 1)
    exps = []
    for k in range(TOP):
        route = meta[:, k : k + 1].astype(F32).astype(I32)
        picked = jnp.sum(jnp.where(lanes == route, logits, 0.0), axis=1, keepdims=True)
        exps.append(jnp.exp(picked))
    total = sum(exps)
    hits, chosen = slot_hits(meta, zhi_ref[0], slots, tokens // SUB * CAP)
    route_weight = sum(jnp.where(hits[k], exps[k] / total, 0.0) for k in range(TOP))
    out_ref[...] = route_weight * chosen


def expert_kernel(dp_ref, rows_ref, *refs):
    weights, out_ref, held, sems = refs[:6], refs[6], refs[7:13], refs[13]
    copies = [pltpu.make_async_copy(weights[i], held[i], sems.at[i]) for i in range(6)]
    for i in (0, 1, 3, 4, 2, 5):
        copies[i].start()
    model_width = out_ref.shape[1]
    masks = rows_ref[:, model_width:].astype(F32).astype(I32)
    blocks = MASK_BLOCKS // 2
    acts = []
    for part in range(2):
        gate_ref, up_ref = held[3 * part], held[3 * part + 1]
        first = (dp_ref[0] if part == 0 else 1 - dp_ref[0]) * blocks
        copies[3 * part].wait()
        copies[3 * part + 1].wait()
        both = jnp.dot(
            rows_ref[:, :model_width],
            jnp.concatenate([gate_ref[...], up_ref[...]], axis=1),
            preferred_element_type=F32,
        )
        units = gate_ref.shape[1]
        keep = jnp.concatenate(
            [(jnp.right_shift(masks, first + b) & 1).astype(F32) for b in range(blocks)], axis=1
        )
        acts.append((jax.nn.silu(both[:, :units]) * both[:, units:] * keep).astype(BF16))
    copies[2].wait()
    copies[5].wait()
    activated = jnp.concatenate(acts, axis=1)
    step = 512
    for j in range(model_width // step):
        columns = slice(j * step, (j + 1) * step)
        down = jnp.concatenate([held[2][:, columns], held[5][:, columns]], axis=0)
        out_ref[:, columns] = jnp.dot(activated, down, preferred_element_type=F32).astype(BF16)


def combine_kernel(zhi_ref, weight_ref, back_ref, out_ref):
    weight = weight_ref[...]
    high = weight.astype(BF16)
    rest = weight - high.astype(F32)
    middle = rest.astype(BF16)
    low = (rest - middle.astype(F32)).astype(BF16)
    stacked = jnp.concatenate([high, middle, low], axis=0)
    tokens = weight.shape[0]
    model_width = back_ref.shape[1]
    step = 1024
    for j in range(model_width // step):
        columns = slice(j * step, (j + 1) * step)
        parts = jnp.dot(stacked, back_ref[:, columns], preferred_element_type=F32)
        total = parts[:tokens] + parts[tokens : 2 * tokens] + parts[2 * tokens :]
        total = total.astype(BF16)
        for place, away in enumerate((0, ZHI - 1, 1, 2)):
            home = (zhi_ref[0] + away) & (ZHI - 1)
            out_ref[home, :, columns] = total[place * SUB : (place + 1) * SUB]


def stay(x):
    return pltpu.with_memory_space_constraint(x, pltpu.HBM)


def swap(n):
    return [(i, i ^ 1) for i in range(n)]


def ring(n, step):
    return [(i, (i + step) % n) for i in range(n)]


def exchange(x, axes):
    return lax.all_to_all(x, axes, split_axis=0, concat_axis=0, tiled=True)


def local(
    queries,
    keys,
    attention_values,
    key_start,
    out_weight,
    residual,
    norm_gain,
    router_weight,
    routes,
    block_masks,
    gate_weight,
    up_weight,
    down_weight,
):
    dp = lax.axis_index("dp").astype(I32)
    ctx = lax.axis_index(CTX).astype(I32)
    zhi, zlo = lax.axis_index("zhi").astype(I32), lax.axis_index("zlo").astype(I32)
    tokens = queries.shape[1]
    model_width = residual.shape[2]
    token_rows = residual.shape[1]
    ctx_count = CY * CX
    scalar = lambda v: v.reshape(1)

    with jax.named_scope("keys_values"):
        heads = queries.shape[2] // HEAD_SIZE
        kv_head = (zhi * ZLO + zlo) * heads // (QUERY_HEADS // KEY_VALUE_HEADS)
        copies = call(
            head_kernel,
            jax.ShapeDtypeStruct((ctx_count, tokens, 2 * HEAD_SIZE), BF16),
            (),
            vmem=8,
            scalars=(scalar(kv_head),),
            any_args=(stay(keys[0]), stay(attention_values[0])),
            scratch=[pltpu.VMEM((2, tokens, HEAD_SIZE), BF16), pltpu.SemaphoreType.DMA((2,))],
            moved=2 << 20,
        )
        all_kv = exchange(copies, CTX)

    with jax.named_scope("out_weight"):
        half = out_weight.shape[0] // 2
        own_half = lax.dynamic_slice_in_dim(out_weight, dp * half, half, 0)
        beside = lax.ppermute(own_half, "zlo", swap(ZLO))
        far = lax.ppermute(own_half, "cx", ring(CX, 2))
        all_kv, beside, far = lax.optimization_barrier((all_kv, beside, far))
        pair = jnp.stack([own_half, beside])
        from_left = lax.ppermute(pair, "cx", ring(CX, 1))
        from_right = lax.ppermute(pair, "cx", ring(CX, -1))
        far_beside = lax.ppermute(far, "zlo", swap(ZLO))
        early = [pair, far, far_beside]
        early_other = [lax.ppermute(w, "dp", swap(2)) for w in early]

    with jax.named_scope("attention"):
        attended = call(
            attend_kernel,
            jax.ShapeDtypeStruct((CY * ZLO, tokens // ZLO, queries.shape[2]), BF16),
            (all_kv, key_start.reshape(tokens, 1)),
            vmem=16,
            scalars=(scalar(ctx * tokens),),
            any_args=(stay(queries[0]),),
            scratch=[
                pltpu.VMEM((tokens, ctx_count * tokens), F32),
                pltpu.VMEM((tokens, queries.shape[2]), BF16),
                pltpu.SemaphoreType.DMA((1,)),
            ],
            flops=4 * tokens * heads * ctx_count * tokens * HEAD_SIZE,
            moved=4 << 20,
        )
        attended, early, early_other = lax.optimization_barrier((attended, early, early_other))
        gathered = exchange(attended, ("cy", "zlo"))
        gathered = gathered.reshape(CY, ZLO, tokens // ZLO, queries.shape[2])

    with jax.named_scope("out_weight"):
        gathered, from_left, from_right = lax.optimization_barrier((gathered, from_left, from_right))
        at_hand = [early[0], from_left, from_right, early[1], early[2], *early_other]
        late = [lax.ppermute(w, "dp", swap(2)) for w in (from_left, from_right)]

    with jax.named_scope("projection"):
        half, width = out_weight.shape[0] // 2, out_weight.shape[1]
        group_rows = CY * ZHI * token_rows
        mine, x = scalar(dp), scalar(lax.axis_index("cx").astype(I32))
        totals = call(
            project_kernel,
            jax.ShapeDtypeStruct((CX, group_rows, width), F32),
            (gathered,),
            vmem=14,
            scalars=(mine, scalar(zlo)),
            any_args=[w if i in (1, 2) else stay(w) for i, w in enumerate(at_hand)],
            scratch=[pltpu.VMEM(w.shape, BF16) for w in at_hand]
            + [pltpu.SemaphoreType.DMA((len(at_hand),))],
            flops=2 * group_rows * 12 * half * width,
            moved=5 << 20,
        )
        partial = call(
            finish_kernel,
            jax.ShapeDtypeStruct((CY * ZHI, SUB, model_width // CY), BF16),
            (gathered, totals, *late),
            vmem=10,
            scalars=(mine, x, scalar(zlo)),
            flops=2 * group_rows * 4 * half * width,
            moved=3 << 20,
        )
        own_experts = [a[0] for a in (gate_weight, up_weight, down_weight)]
        partial, *sent_experts = lax.optimization_barrier((partial, *own_experts))
        other_experts = [lax.ppermute(a, "dp", swap(2)) for a in sent_experts]
        parts = exchange(partial, ("cy", "zhi"))
        parts, other_experts = lax.optimization_barrier((parts, other_experts))

    with jax.named_scope("norm"):
        meta = jnp.concatenate([routes[0], block_masks[0]], axis=1).astype(BF16)
        meta = jnp.pad(meta, ((0, 0), (0, LANES - 2 * TOP)))
        ext, hidden_state = call(
            norm_kernel,
            [
                jax.ShapeDtypeStruct((token_rows, model_width + LANES), BF16),
                jax.ShapeDtypeStruct((token_rows, model_width), BF16),
            ],
            (parts, residual[0], norm_gain.reshape(1, model_width), meta),
            vmem=6,
            moved=2 << 20,
        )
        left = lax.ppermute(ext, "zhi", ring(ZHI, 1))
        right = lax.ppermute(ext, "zhi", ring(ZHI, -1))
        cut = model_width // 2
        far = [
            lax.ppermute(left[:, :cut], "zhi", ring(ZHI, 1)),
            lax.ppermute(right[:, cut:], "zhi", ring(ZHI, -1)),
        ]
        near_ext = (ext, left, right, *far)

    with jax.named_scope("dispatch"):
        dests = ctx_count * ZLO
        capacity = ZHI * token_rows // SUB * CAP
        slots = dests * capacity
        rows = call(
            dispatch_kernel,
            jax.ShapeDtypeStruct((slots, model_width + LANES), BF16),
            near_ext,
            vmem=16,
            scalars=(scalar(zhi),),
            flops=2 * slots * 64 * model_width,
            moved=3 << 20,
        )
        slot_weight = call(
            weight_kernel,
            jax.ShapeDtypeStruct((ZHI * token_rows, slots), F32),
            (router_weight, *near_ext),
            vmem=8,
            scalars=(scalar(zhi),),
            flops=2 * 64 * EXPERTS * model_width,
            moved=2 << 20,
        )
        over = ("cy", "cx", "zlo")
        got = exchange(rows.reshape(dests, capacity, model_width + LANES), over)

    with jax.named_scope("experts"):
        every = own_experts + other_experts
        expert_out = call(
            expert_kernel,
            jax.ShapeDtypeStruct((slots, model_width), BF16),
            (got.reshape(slots, model_width + LANES),),
            vmem=32,
            scalars=(scalar(dp),),
            any_args=every,
            scratch=[pltpu.VMEM(a.shape, a.dtype) for a in every] + [pltpu.SemaphoreType.DMA((6,))],
            flops=6 * slots * model_width * 768,
            moved=22 << 20,
        )
        back = exchange(expert_out.reshape(dests, capacity, model_width), over)

    with jax.named_scope("combine"):
        mixed = call(
            combine_kernel,
            jax.ShapeDtypeStruct((ZHI, token_rows, model_width), BF16),
            (slot_weight, back.reshape(slots, model_width)),
            vmem=14,
            scalars=(scalar(zhi),),
            flops=6 * 64 * slots * model_width,
            moved=3 << 20,
        )
        mixture = jnp.sum(exchange(mixed, "zhi").astype(F32), axis=0)
        layer_out = (hidden_state.astype(F32) + mixture).astype(BF16)
    return layer_out[None]


def solution(mesh):
    fine = Mesh(
        mesh.devices.reshape(2, CY, CX, ZHI, ZLO), ("dp", "cy", "cx", "zhi", "zlo")
    )
    tp = ("zhi", "zlo")
    all_ctx = CTX + tp
    in_specs = (
        P("dp", CTX, tp),
        P("dp", CTX, None),
        P("dp", CTX, None),
        P("dp", CTX),
        P(tp, CTX),
        P("dp", all_ctx, None),
        P(),
        P(),
        P("dp", all_ctx, None),
        P("dp", all_ctx, None),
        P(all_ctx, None, "dp"),
        P(all_ctx, None, "dp"),
        P(all_ctx, "dp", None),
    )
    out_specs = P("dp", all_ctx, None)
    return jax.shard_map(local, mesh=fine, in_specs=in_specs, out_specs=out_specs, check_vma=False)
```

```python
import math

import jax
import jax.numpy as jnp
from jax import lax
from jax.experimental import pallas as pl
from jax.experimental.pallas import tpu as pltpu
from jax.sharding import Mesh
from jax.sharding import PartitionSpec as P

QUERY_HEADS = 64
KEY_VALUE_HEADS = 4
HEAD_SIZE = 128
MASK_BLOCKS = 6
TOP = 8
EXPERTS = 128
CAP = 2
SCORE_FLOOR = -1e30
LANES = 128
SUB = 16
MIB = 1024 * 1024

CY, CX, ZHI, ZLO = 4, 4, 4, 2
CTX = ("cy", "cx")
F32, BF16, I32 = jnp.float32, jnp.bfloat16, jnp.int32


def call(kernel, out_shape, args, vmem, scalars=(), any_args=(), scratch=(), flops=0, moved=0):
    specs = [pl.BlockSpec(memory_space=pltpu.SMEM) for _ in scalars]
    specs += [pl.BlockSpec(memory_space=pltpu.VMEM) for _ in args]
    specs += [pl.BlockSpec(memory_space=pl.ANY) for _ in any_args]
    many = isinstance(out_shape, (list, tuple))
    whole = pl.BlockSpec(memory_space=pltpu.VMEM)
    return pl.pallas_call(
        kernel,
        out_shape=out_shape,
        in_specs=specs,
        out_specs=[whole] * len(out_shape) if many else whole,
        scratch_shapes=list(scratch),
        cost_estimate=pl.CostEstimate(flops=flops, bytes_accessed=moved, transcendentals=0),
        compiler_params=pltpu.CompilerParams(vmem_limit_bytes=vmem * MIB),
    )(*scalars, *args, *any_args)


def head_kernel(head_ref, key_ref, value_ref, out_ref, pair_ref, sems):
    columns = pl.ds(pl.multiple_of(head_ref[0] * HEAD_SIZE, HEAD_SIZE), HEAD_SIZE)
    copies = [
        pltpu.make_async_copy(ref.at[:, columns], pair_ref.at[i], sems.at[i])
        for i, ref in enumerate((key_ref, value_ref))
    ]
    for copy in copies:
        copy.start()
    for copy in copies:
        copy.wait()
    pair = jnp.concatenate([pair_ref[0], pair_ref[1]], axis=1)
    for c in range(out_ref.shape[0]):
        out_ref[c] = pair


def attend_kernel(first_ref, kv_ref, start_ref, query_hbm, out_ref, bias_ref, query_ref, sem):
    copy = pltpu.make_async_copy(query_hbm, query_ref, sem.at[0])
    copy.start()
    tokens = query_ref.shape[0]
    heads = query_ref.shape[1] // HEAD_SIZE
    keys = kv_ref.shape[0] * kv_ref.shape[1]
    key_rows = kv_ref[:, :, :HEAD_SIZE].reshape(keys, HEAD_SIZE)
    value_rows = kv_ref[:, :, HEAD_SIZE:].reshape(keys, HEAD_SIZE)
    position = first_ref[0] + lax.broadcasted_iota(I32, (tokens, keys), 0)
    key_pos = lax.broadcasted_iota(I32, (tokens, keys), 1)
    visible = (key_pos >= start_ref[...]) & (key_pos <= position)
    bias_ref[...] = jnp.where(visible, 0.0, SCORE_FLOOR)
    copy.wait()
    scale = math.log2(math.e) / math.sqrt(HEAD_SIZE)
    for head in range(heads):
        columns = slice(head * HEAD_SIZE, (head + 1) * HEAD_SIZE)
        scores = lax.dot_general(
            query_ref[:, columns], key_rows, (((1,), (1,)), ((), ())), preferred_element_type=F32
        )
        scores = scores * scale + bias_ref[...]
        row_max = jnp.max(scores, axis=1, keepdims=True)
        weights = jnp.exp2(scores - row_max)
        row_sum = jnp.sum(weights, axis=1, keepdims=True)
        mixed = jnp.dot(weights.astype(BF16), value_rows, preferred_element_type=F32)
        attended = (mixed / row_sum).astype(BF16)
        for z in range(ZHI * ZLO):
            block = attended[z * SUB : (z + 1) * SUB]
            rows = slice((z // ZLO) * SUB, (z // ZLO + 1) * SUB)
            for y in range(CY):
                out_ref[y * ZLO + z % ZLO, rows, columns] = block


def project_kernel(dp_ref, x_ref, zlo_ref, att_ref, *refs):
    count = 10
    sources, out_ref, held, sems = refs[:count], refs[count], refs[count + 1 : -1], refs[-1]
    copies = [pltpu.make_async_copy(a, b, sems.at[i]) for i, (a, b) in enumerate(zip(sources, held))]
    for copy in copies:
        copy.start()
    half, width = held[3].shape
    rows = att_ref.shape[0] * att_ref.shape[2]
    for step, away in enumerate((0, CX - 1, 1, 2)):
        total = jnp.zeros((rows, width), F32)
        for part in range(2):
            columns = pl.ds(
                pl.multiple_of((dp_ref[0] if part == 0 else 1 - dp_ref[0]) * half, half), half
            )
            for near in range(ZLO):
                source = zlo_ref[0] if near == 0 else 1 - zlo_ref[0]
                piece = 5 * part + step + (near if step == 3 else 0)
                if near == 0 or step == 3:
                    copies[piece].wait()
                weight = held[piece][...] if step == 3 else held[piece][near]
                total += jnp.dot(
                    att_ref[:, source, :, columns].reshape(rows, half),
                    weight,
                    preferred_element_type=F32,
                )
        place = pl.multiple_of(((x_ref[0] + away) & (CX - 1)) * width, width)
        out_ref[:, :, pl.ds(place, width)] = total.astype(BF16).reshape(rows // SUB, SUB, width)


def norm_kernel(parts_ref, residual_ref, gain_ref, meta_ref, ext_ref, hidden_ref):
    model_width = residual_ref.shape[1]
    width = model_width // CY
    zs = ZHI
    pieces = []
    square_sum = jnp.zeros((SUB, 1), F32)
    for y in range(CY):
        columns = slice(y * width, (y + 1) * width)
        projected = sum(parts_ref[y * zs + z].astype(F32) for z in range(zs))
        hidden = (residual_ref[:, columns].astype(F32) + projected).astype(BF16)
        hidden_ref[:, columns] = hidden
        wide = hidden.astype(F32)
        square_sum += jnp.sum(wide * wide, axis=1, keepdims=True)
        pieces.append(wide)
    inverse = lax.rsqrt(square_sum / model_width + 1e-06)
    for y in range(CY):
        columns = slice(y * width, (y + 1) * width)
        normed = (pieces[y] * inverse * gain_ref[:, columns].astype(F32)).astype(BF16)
        ext_ref[:, columns] = normed
    ext_ref[:, model_width:] = meta_ref[...]


def slot_hits(meta, zhi, slots, slot_capacity):
    tokens = meta.shape[0]
    slot = lax.broadcasted_iota(I32, (tokens, slots), 1)
    dest = slot >> (slot_capacity.bit_length() - 1)
    expert = (dest >> 1) * (ZHI * ZLO) + zhi * ZLO + (dest & 1)
    hits = [meta[:, k : k + 1].astype(F32).astype(I32) == expert for k in range(TOP)]
    named = sum(h.astype(F32) for h in hits)
    later = lax.broadcasted_iota(I32, (tokens, tokens), 0) > lax.broadcasted_iota(
        I32, (tokens, tokens), 1
    )
    earlier = jnp.dot(later.astype(BF16), named.astype(BF16), preferred_element_type=F32)
    place = (slot & (slot_capacity - 1)).astype(F32)
    chosen = jnp.where((named > 0.5) & (earlier == place), 1.0, 0.0)
    return hits, chosen


def gathered_rows(refs):
    own, left, right, far_first, far_second = [ref[...] for ref in refs]
    far = jnp.concatenate([far_first, far_second], axis=1)
    return jnp.concatenate([own, left, right, far], axis=0)


def dispatch_kernel(zhi_ref, *refs):
    ext, rows_ref = gathered_rows(refs[:-1]), refs[-1]
    tokens = ext.shape[0]
    width = ext.shape[1] - LANES
    meta = ext[:, width:]
    hits, chosen = slot_hits(meta, zhi_ref[0], rows_ref.shape[0], tokens // SUB * CAP)
    masks = sum(
        jnp.where(hits[k], meta[:, TOP + k : TOP + k + 1].astype(F32), 0.0) for k in range(TOP)
    )
    along = (((0,), (0,)), ((), ()))
    rows_ref[:, :width] = lax.dot_general(
        chosen.astype(BF16), ext[:, :width], along, preferred_element_type=F32
    ).astype(BF16)
    ones = jnp.ones((tokens, LANES), BF16)
    rows_ref[:, width:] = lax.dot_general(
        (masks * chosen).astype(BF16), ones, along, preferred_element_type=F32
    ).astype(BF16)


def weight_kernel(zhi_ref, router_ref, *refs):
    ext, out_ref = gathered_rows(refs[:-1]), refs[-1]
    tokens = ext.shape[0]
    model_width = ext.shape[1] - LANES
    slots = out_ref.shape[1]
    meta, normed = ext[:, model_width:], ext[:, :model_width]
    logits = jnp.dot(normed, router_ref[...], preferred_element_type=F32)
    lanes = lax.broadcasted_iota(I32, (tokens, EXPERTS), 1)
    exps = []
    for k in range(TOP):
        route = meta[:, k : k + 1].astype(F32).astype(I32)
        picked = jnp.sum(jnp.where(lanes == route, logits, 0.0), axis=1, keepdims=True)
        exps.append(jnp.exp(picked))
    total = sum(exps)
    hits, chosen = slot_hits(meta, zhi_ref[0], slots, tokens // SUB * CAP)
    route_weight = sum(jnp.where(hits[k], exps[k] / total, 0.0) for k in range(TOP))
    out_ref[...] = route_weight * chosen


def expert_kernel(dp_ref, rows_ref, *refs):
    weights, out_ref, held, sems = refs[:6], refs[6], refs[7:13], refs[13]
    copies = [pltpu.make_async_copy(weights[i], held[i], sems.at[i]) for i in range(6)]
    for i in (0, 1, 3, 4, 2, 5):
        copies[i].start()
    model_width = out_ref.shape[1]
    masks = rows_ref[:, model_width:].astype(F32).astype(I32)
    blocks = MASK_BLOCKS // 2
    acts = []
    for part in range(2):
        gate_ref, up_ref = held[3 * part], held[3 * part + 1]
        first = (dp_ref[0] if part == 0 else 1 - dp_ref[0]) * blocks
        copies[3 * part].wait()
        copies[3 * part + 1].wait()
        both = jnp.dot(
            rows_ref[:, :model_width],
            jnp.concatenate([gate_ref[...], up_ref[...]], axis=1),
            preferred_element_type=F32,
        )
        units = gate_ref.shape[1]
        keep = jnp.concatenate(
            [(jnp.right_shift(masks, first + b) & 1).astype(F32) for b in range(blocks)], axis=1
        )
        acts.append((jax.nn.silu(both[:, :units]) * both[:, units:] * keep).astype(BF16))
    copies[2].wait()
    copies[5].wait()
    activated = jnp.concatenate(acts, axis=1)
    step = 512
    for j in range(model_width // step):
        columns = slice(j * step, (j + 1) * step)
        down = jnp.concatenate([held[2][:, columns], held[5][:, columns]], axis=0)
        out_ref[:, columns] = jnp.dot(activated, down, preferred_element_type=F32).astype(BF16)


def combine_kernel(zhi_ref, weight_ref, back_ref, out_ref):
    weight = weight_ref[...]
    high = weight.astype(BF16)
    rest = weight - high.astype(F32)
    middle = rest.astype(BF16)
    low = (rest - middle.astype(F32)).astype(BF16)
    stacked = jnp.concatenate([high, middle, low], axis=0)
    tokens = weight.shape[0]
    model_width = back_ref.shape[1]
    step = 1024
    for j in range(model_width // step):
        columns = slice(j * step, (j + 1) * step)
        parts = jnp.dot(stacked, back_ref[:, columns], preferred_element_type=F32)
        total = parts[:tokens] + parts[tokens : 2 * tokens] + parts[2 * tokens :]
        total = total.astype(BF16)
        for place, away in enumerate((0, ZHI - 1, 1, 2)):
            home = (zhi_ref[0] + away) & (ZHI - 1)
            out_ref[home, :, columns] = total[place * SUB : (place + 1) * SUB]


def stay(x):
    return pltpu.with_memory_space_constraint(x, pltpu.HBM)


def swap(n):
    return [(i, i ^ 1) for i in range(n)]


def ring(n, step):
    return [(i, (i + step) % n) for i in range(n)]


def exchange(x, axes):
    return lax.all_to_all(x, axes, split_axis=0, concat_axis=0, tiled=True)


def local(
    queries,
    keys,
    attention_values,
    key_start,
    out_weight,
    residual,
    norm_gain,
    router_weight,
    routes,
    block_masks,
    gate_weight,
    up_weight,
    down_weight,
):
    dp = lax.axis_index("dp").astype(I32)
    ctx = lax.axis_index(CTX).astype(I32)
    zhi, zlo = lax.axis_index("zhi").astype(I32), lax.axis_index("zlo").astype(I32)
    tokens = queries.shape[1]
    model_width = residual.shape[2]
    token_rows = residual.shape[1]
    ctx_count = CY * CX
    scalar = lambda v: v.reshape(1)

    with jax.named_scope("keys_values"):
        heads = queries.shape[2] // HEAD_SIZE
        kv_head = (zhi * ZLO + zlo) * heads // (QUERY_HEADS // KEY_VALUE_HEADS)
        copies = call(
            head_kernel,
            jax.ShapeDtypeStruct((ctx_count, tokens, 2 * HEAD_SIZE), BF16),
            (),
            vmem=8,
            scalars=(scalar(kv_head),),
            any_args=(stay(keys[0]), stay(attention_values[0])),
            scratch=[pltpu.VMEM((2, tokens, HEAD_SIZE), BF16), pltpu.SemaphoreType.DMA((2,))],
            moved=2 << 20,
        )
        all_kv = exchange(copies, CTX)

    with jax.named_scope("expert_weights"):
        own_experts = [a[0] for a in (gate_weight, up_weight, down_weight)]
        other_experts = [lax.ppermute(a, "dp", swap(2)) for a in own_experts]

    with jax.named_scope("out_weight"):
        half = out_weight.shape[0] // 2
        own_half = lax.dynamic_slice_in_dim(out_weight, dp * half, half, 0)
        beside = lax.ppermute(own_half, "zlo", swap(ZLO))
        far = lax.ppermute(own_half, "cx", ring(CX, 2))
        all_kv, beside, far, other_experts = lax.optimization_barrier(
            (all_kv, beside, far, other_experts)
        )
        pair = jnp.stack([own_half, beside])
        from_left = lax.ppermute(pair, "cx", ring(CX, 1))
        from_right = lax.ppermute(pair, "cx", ring(CX, -1))
        far_beside = lax.ppermute(far, "zlo", swap(ZLO))
        early = [pair, from_left, from_right, far, far_beside]
        early_other = [lax.ppermute(w, "dp", swap(2)) for w in (pair, far)]

    with jax.named_scope("attention"):
        attended = call(
            attend_kernel,
            jax.ShapeDtypeStruct((CY * ZLO, tokens // ZLO, queries.shape[2]), BF16),
            (all_kv, key_start.reshape(tokens, 1)),
            vmem=16,
            scalars=(scalar(ctx * tokens),),
            any_args=(stay(queries[0]),),
            scratch=[
                pltpu.VMEM((tokens, ctx_count * tokens), F32),
                pltpu.VMEM((tokens, queries.shape[2]), BF16),
                pltpu.SemaphoreType.DMA((1,)),
            ],
            flops=4 * tokens * heads * ctx_count * tokens * HEAD_SIZE,
            moved=4 << 20,
        )
        attended, early, early_other = lax.optimization_barrier((attended, early, early_other))
        late = [lax.ppermute(w, "dp", swap(2)) for w in (early[1], early[2], early[4])]
        others = [early_other[0], late[0], late[1], early_other[1], late[2]]
        gathered = exchange(attended, ("cy", "zlo"))
        gathered = gathered.reshape(CY, ZLO, tokens // ZLO, queries.shape[2])

    with jax.named_scope("projection"):
        half, width = out_weight.shape[0] // 2, out_weight.shape[1]
        group_rows = CY * ZHI * token_rows
        mine, x = scalar(dp), scalar(lax.axis_index("cx").astype(I32))
        partial = call(
            project_kernel,
            jax.ShapeDtypeStruct((CY * ZHI, SUB, model_width // CY), BF16),
            (gathered,),
            vmem=14,
            scalars=(mine, x, scalar(zlo)),
            any_args=[stay(w) for w in early] + [stay(w) if i in (0, 3) else w for i, w in enumerate(others)],
            scratch=[pltpu.VMEM(w.shape, BF16) for w in early + others]
            + [pltpu.SemaphoreType.DMA((10,))],
            flops=2 * group_rows * 16 * half * width,
            moved=6 << 20,
        )
        parts = exchange(partial, ("cy", "zhi"))

    with jax.named_scope("norm"):
        meta = jnp.concatenate([routes[0], block_masks[0]], axis=1).astype(BF16)
        meta = jnp.pad(meta, ((0, 0), (0, LANES - 2 * TOP)))
        ext, hidden_state = call(
            norm_kernel,
            [
                jax.ShapeDtypeStruct((token_rows, model_width + LANES), BF16),
                jax.ShapeDtypeStruct((token_rows, model_width), BF16),
            ],
            (parts, residual[0], norm_gain.reshape(1, model_width), meta),
            vmem=6,
            moved=2 << 20,
        )
        left = lax.ppermute(ext, "zhi", ring(ZHI, 1))
        right = lax.ppermute(ext, "zhi", ring(ZHI, -1))
        cut = model_width // 2
        far = [
            lax.ppermute(left[:, :cut], "zhi", ring(ZHI, 1)),
            lax.ppermute(right[:, cut:], "zhi", ring(ZHI, -1)),
        ]
        near_ext = (ext, left, right, *far)

    with jax.named_scope("dispatch"):
        dests = ctx_count * ZLO
        capacity = ZHI * token_rows // SUB * CAP
        slots = dests * capacity
        rows = call(
            dispatch_kernel,
            jax.ShapeDtypeStruct((slots, model_width + LANES), BF16),
            near_ext,
            vmem=16,
            scalars=(scalar(zhi),),
            flops=2 * slots * 64 * model_width,
            moved=3 << 20,
        )
        slot_weight = call(
            weight_kernel,
            jax.ShapeDtypeStruct((ZHI * token_rows, slots), F32),
            (router_weight, *near_ext),
            vmem=8,
            scalars=(scalar(zhi),),
            flops=2 * 64 * EXPERTS * model_width,
            moved=2 << 20,
        )
        over = ("cy", "cx", "zlo")
        got = exchange(rows.reshape(dests, capacity, model_width + LANES), over)

    with jax.named_scope("experts"):
        every = own_experts + other_experts
        expert_out = call(
            expert_kernel,
            jax.ShapeDtypeStruct((slots, model_width), BF16),
            (got.reshape(slots, model_width + LANES),),
            vmem=32,
            scalars=(scalar(dp),),
            any_args=every,
            scratch=[pltpu.VMEM(a.shape, a.dtype) for a in every] + [pltpu.SemaphoreType.DMA((6,))],
            flops=6 * slots * model_width * 768,
            moved=22 << 20,
        )
        back = exchange(expert_out.reshape(dests, capacity, model_width), over)

    with jax.named_scope("combine"):
        mixed = call(
            combine_kernel,
            jax.ShapeDtypeStruct((ZHI, token_rows, model_width), BF16),
            (slot_weight, back.reshape(slots, model_width)),
            vmem=14,
            scalars=(scalar(zhi),),
            flops=6 * 64 * slots * model_width,
            moved=3 << 20,
        )
        mixture = jnp.sum(exchange(mixed, "zhi").astype(F32), axis=0)
        layer_out = (hidden_state.astype(F32) + mixture).astype(BF16)
    return layer_out[None]


def solution(mesh):
    fine = Mesh(
        mesh.devices.reshape(2, CY, CX, ZHI, ZLO), ("dp", "cy", "cx", "zhi", "zlo")
    )
    tp = ("zhi", "zlo")
    all_ctx = CTX + tp
    in_specs = (
        P("dp", CTX, tp),
        P("dp", CTX, None),
        P("dp", CTX, None),
        P("dp", CTX),
        P(tp, CTX),
        P("dp", all_ctx, None),
        P(),
        P(),
        P("dp", all_ctx, None),
        P("dp", all_ctx, None),
        P(all_ctx, None, "dp"),
        P(all_ctx, None, "dp"),
        P(all_ctx, "dp", None),
    )
    out_specs = P("dp", all_ctx, None)
    return jax.shard_map(local, mesh=fine, in_specs=in_specs, out_specs=out_specs, check_vma=False)
```

```python
import math

import jax
import jax.numpy as jnp
from jax import lax
from jax.experimental import pallas as pl
from jax.experimental.pallas import tpu as pltpu
from jax.sharding import Mesh
from jax.sharding import PartitionSpec as P

QUERY_HEADS = 64
KEY_VALUE_HEADS = 4
HEAD_SIZE = 128
MASK_BLOCKS = 6
TOP = 8
EXPERTS = 128
CAP = 2
SCORE_FLOOR = -1e30
LANES = 128
SUB = 16
MIB = 1024 * 1024

CY, CX, ZHI, ZLO = 4, 4, 4, 2
CTX = ("cy", "cx")
F32, BF16, I32 = jnp.float32, jnp.bfloat16, jnp.int32


def call(kernel, out_shape, args, vmem, scalars=(), any_args=(), scratch=(), flops=0, moved=0):
    specs = [pl.BlockSpec(memory_space=pltpu.SMEM) for _ in scalars]
    specs += [pl.BlockSpec(memory_space=pltpu.VMEM) for _ in args]
    specs += [pl.BlockSpec(memory_space=pl.ANY) for _ in any_args]
    many = isinstance(out_shape, (list, tuple))
    whole = pl.BlockSpec(memory_space=pltpu.VMEM)
    return pl.pallas_call(
        kernel,
        out_shape=out_shape,
        in_specs=specs,
        out_specs=[whole] * len(out_shape) if many else whole,
        scratch_shapes=list(scratch),
        cost_estimate=pl.CostEstimate(flops=flops, bytes_accessed=moved, transcendentals=0),
        compiler_params=pltpu.CompilerParams(vmem_limit_bytes=vmem * MIB),
    )(*scalars, *args, *any_args)


def head_kernel(head_ref, key_ref, value_ref, out_ref, pair_ref, sems):
    columns = pl.ds(pl.multiple_of(head_ref[0] * HEAD_SIZE, HEAD_SIZE), HEAD_SIZE)
    copies = [
        pltpu.make_async_copy(ref.at[:, columns], pair_ref.at[i], sems.at[i])
        for i, ref in enumerate((key_ref, value_ref))
    ]
    for copy in copies:
        copy.start()
    for copy in copies:
        copy.wait()
    pair = jnp.concatenate([pair_ref[0], pair_ref[1]], axis=1)
    for c in range(out_ref.shape[0]):
        out_ref[c] = pair


def attend_kernel(first_ref, kv_ref, start_ref, query_hbm, out_ref, bias_ref, query_ref, sem):
    copy = pltpu.make_async_copy(query_hbm, query_ref, sem.at[0])
    copy.start()
    tokens = query_ref.shape[0]
    heads = query_ref.shape[1] // HEAD_SIZE
    keys = kv_ref.shape[0] * kv_ref.shape[1]
    key_rows = kv_ref[:, :, :HEAD_SIZE].reshape(keys, HEAD_SIZE)
    value_rows = kv_ref[:, :, HEAD_SIZE:].reshape(keys, HEAD_SIZE)
    position = first_ref[0] + lax.broadcasted_iota(I32, (tokens, keys), 0)
    key_pos = lax.broadcasted_iota(I32, (tokens, keys), 1)
    visible = (key_pos >= start_ref[...]) & (key_pos <= position)
    bias_ref[...] = jnp.where(visible, 0.0, SCORE_FLOOR)
    copy.wait()
    scale = math.log2(math.e) / math.sqrt(HEAD_SIZE)
    bias = bias_ref[...]
    bias = jnp.concatenate([bias, bias], axis=0)
    for head in range(0, heads, 2):
        columns = [slice(h * HEAD_SIZE, (h + 1) * HEAD_SIZE) for h in (head, head + 1)]
        scores = lax.dot_general(
            jnp.concatenate([query_ref[:, c] for c in columns], axis=0),
            key_rows,
            (((1,), (1,)), ((), ())),
            preferred_element_type=F32,
        )
        scores = scores * scale + bias
        row_max = jnp.max(scores, axis=1, keepdims=True)
        weights = jnp.exp2(scores - row_max)
        row_sum = jnp.sum(weights, axis=1, keepdims=True)
        mixed = jnp.dot(weights.astype(BF16), value_rows, preferred_element_type=F32)
        attended = (mixed / row_sum).astype(BF16)
        for which in range(2):
            for z in range(ZHI * ZLO):
                block = attended[which * tokens + z * SUB : which * tokens + (z + 1) * SUB]
                rows = slice((z // ZLO) * SUB, (z // ZLO + 1) * SUB)
                for y in range(CY):
                    out_ref[y * ZLO + z % ZLO, rows, columns[which]] = block


def project_kernel(dp_ref, x_ref, zlo_ref, att_ref, *refs):
    count = 10
    sources, out_ref, held, sems = refs[:count], refs[count], refs[count + 1 : -1], refs[-1]
    copies = [pltpu.make_async_copy(a, b, sems.at[i]) for i, (a, b) in enumerate(zip(sources, held))]
    for copy in copies:
        copy.start()
    half, width = held[3].shape
    rows = att_ref.shape[0] * att_ref.shape[2]
    for step, away in enumerate((0, CX - 1, 1, 2)):
        total = jnp.zeros((rows, width), F32)
        for part in range(2):
            columns = pl.ds(
                pl.multiple_of((dp_ref[0] if part == 0 else 1 - dp_ref[0]) * half, half), half
            )
            for near in range(ZLO):
                source = zlo_ref[0] if near == 0 else 1 - zlo_ref[0]
                piece = 5 * part + step + (near if step == 3 else 0)
                if near == 0 or step == 3:
                    copies[piece].wait()
                weight = held[piece][...] if step == 3 else held[piece][near]
                total += jnp.dot(
                    att_ref[:, source, :, columns].reshape(rows, half),
                    weight,
                    preferred_element_type=F32,
                )
        place = pl.multiple_of(((x_ref[0] + away) & (CX - 1)) * width, width)
        out_ref[:, :, pl.ds(place, width)] = total.astype(BF16).reshape(rows // SUB, SUB, width)


def norm_kernel(parts_ref, residual_ref, gain_ref, meta_ref, ext_ref, hidden_ref):
    model_width = residual_ref.shape[1]
    width = model_width // CY
    zs = ZHI
    pieces = []
    square_sum = jnp.zeros((SUB, 1), F32)
    for y in range(CY):
        columns = slice(y * width, (y + 1) * width)
        projected = sum(parts_ref[y * zs + z].astype(F32) for z in range(zs))
        hidden = (residual_ref[:, columns].astype(F32) + projected).astype(BF16)
        hidden_ref[:, columns] = hidden
        wide = hidden.astype(F32)
        square_sum += jnp.sum(wide * wide, axis=1, keepdims=True)
        pieces.append(wide)
    inverse = lax.rsqrt(square_sum / model_width + 1e-06)
    for y in range(CY):
        columns = slice(y * width, (y + 1) * width)
        normed = (pieces[y] * inverse * gain_ref[:, columns].astype(F32)).astype(BF16)
        ext_ref[:, columns] = normed
    ext_ref[:, model_width:] = meta_ref[...]


def slot_hits(meta, zhi, slots, slot_capacity):
    tokens = meta.shape[0]
    slot = lax.broadcasted_iota(I32, (tokens, slots), 1)
    dest = slot >> (slot_capacity.bit_length() - 1)
    expert = (dest >> 1) * (ZHI * ZLO) + zhi * ZLO + (dest & 1)
    hits = [meta[:, k : k + 1].astype(F32).astype(I32) == expert for k in range(TOP)]
    named = sum(h.astype(F32) for h in hits)
    later = lax.broadcasted_iota(I32, (tokens, tokens), 0) > lax.broadcasted_iota(
        I32, (tokens, tokens), 1
    )
    earlier = jnp.dot(later.astype(BF16), named.astype(BF16), preferred_element_type=F32)
    place = (slot & (slot_capacity - 1)).astype(F32)
    chosen = jnp.where((named > 0.5) & (earlier == place), 1.0, 0.0)
    return hits, chosen


def gathered_rows(refs):
    own, left, right, far_first, far_second = [ref[...] for ref in refs]
    far = jnp.concatenate([far_first, far_second], axis=1)
    return jnp.concatenate([own, left, right, far], axis=0)


def dispatch_kernel(zhi_ref, *refs):
    ext, rows_ref = gathered_rows(refs[:-1]), refs[-1]
    tokens = ext.shape[0]
    width = ext.shape[1] - LANES
    meta = ext[:, width:]
    hits, chosen = slot_hits(meta, zhi_ref[0], rows_ref.shape[0], tokens // SUB * CAP)
    masks = sum(
        jnp.where(hits[k], meta[:, TOP + k : TOP + k + 1].astype(F32), 0.0) for k in range(TOP)
    )
    along = (((0,), (0,)), ((), ()))
    rows_ref[:, :width] = lax.dot_general(
        chosen.astype(BF16), ext[:, :width], along, preferred_element_type=F32
    ).astype(BF16)
    ones = jnp.ones((tokens, LANES), BF16)
    rows_ref[:, width:] = lax.dot_general(
        (masks * chosen).astype(BF16), ones, along, preferred_element_type=F32
    ).astype(BF16)


def weight_kernel(zhi_ref, router_ref, *refs):
    ext, out_ref = gathered_rows(refs[:-1]), refs[-1]
    tokens = ext.shape[0]
    model_width = ext.shape[1] - LANES
    slots = out_ref.shape[1]
    meta, normed = ext[:, model_width:], ext[:, :model_width]
    logits = jnp.dot(normed, router_ref[...], preferred_element_type=F32)
    lanes = lax.broadcasted_iota(I32, (tokens, EXPERTS), 1)
    exps = []
    for k in range(TOP):
        route = meta[:, k : k + 1].astype(F32).astype(I32)
        picked = jnp.sum(jnp.where(lanes == route, logits, 0.0), axis=1, keepdims=True)
        exps.append(jnp.exp(picked))
    total = sum(exps)
    hits, chosen = slot_hits(meta, zhi_ref[0], slots, tokens // SUB * CAP)
    route_weight = sum(jnp.where(hits[k], exps[k] / total, 0.0) for k in range(TOP))
    out_ref[...] = route_weight * chosen


def expert_kernel(dp_ref, rows_ref, *refs):
    weights, out_ref, held, sems = refs[:6], refs[6], refs[7:13], refs[13]
    copies = [pltpu.make_async_copy(weights[i], held[i], sems.at[i]) for i in range(6)]
    for i in (0, 1, 3, 4, 2, 5):
        copies[i].start()
    model_width = out_ref.shape[1]
    masks = rows_ref[:, model_width:].astype(F32).astype(I32)
    blocks = MASK_BLOCKS // 2
    acts = []
    for part in range(2):
        gate_ref, up_ref = held[3 * part], held[3 * part + 1]
        first = (dp_ref[0] if part == 0 else 1 - dp_ref[0]) * blocks
        copies[3 * part].wait()
        copies[3 * part + 1].wait()
        both = jnp.dot(
            rows_ref[:, :model_width],
            jnp.concatenate([gate_ref[...], up_ref[...]], axis=1),
            preferred_element_type=F32,
        )
        units = gate_ref.shape[1]
        keep = jnp.concatenate(
            [(jnp.right_shift(masks, first + b) & 1).astype(F32) for b in range(blocks)], axis=1
        )
        acts.append((jax.nn.silu(both[:, :units]) * both[:, units:] * keep).astype(BF16))
    copies[2].wait()
    copies[5].wait()
    activated = jnp.concatenate(acts, axis=1)
    step = 512
    for j in range(model_width // step):
        columns = slice(j * step, (j + 1) * step)
        down = jnp.concatenate([held[2][:, columns], held[5][:, columns]], axis=0)
        out_ref[:, columns] = jnp.dot(activated, down, preferred_element_type=F32).astype(BF16)


def combine_kernel(zhi_ref, weight_ref, back_ref, out_ref):
    weight = weight_ref[...]
    high = weight.astype(BF16)
    rest = weight - high.astype(F32)
    middle = rest.astype(BF16)
    low = (rest - middle.astype(F32)).astype(BF16)
    stacked = jnp.concatenate([high, middle, low], axis=0)
    tokens = weight.shape[0]
    model_width = back_ref.shape[1]
    step = 1024
    for j in range(model_width // step):
        columns = slice(j * step, (j + 1) * step)
        parts = jnp.dot(stacked, back_ref[:, columns], preferred_element_type=F32)
        total = parts[:tokens] + parts[tokens : 2 * tokens] + parts[2 * tokens :]
        total = total.astype(BF16)
        for place, away in enumerate((0, ZHI - 1, 1, 2)):
            home = (zhi_ref[0] + away) & (ZHI - 1)
            out_ref[home, :, columns] = total[place * SUB : (place + 1) * SUB]


def stay(x):
    return pltpu.with_memory_space_constraint(x, pltpu.HBM)


def swap(n):
    return [(i, i ^ 1) for i in range(n)]


def ring(n, step):
    return [(i, (i + step) % n) for i in range(n)]


def exchange(x, axes):
    return lax.all_to_all(x, axes, split_axis=0, concat_axis=0, tiled=True)


def local(
    queries,
    keys,
    attention_values,
    key_start,
    out_weight,
    residual,
    norm_gain,
    router_weight,
    routes,
    block_masks,
    gate_weight,
    up_weight,
    down_weight,
):
    dp = lax.axis_index("dp").astype(I32)
    ctx = lax.axis_index(CTX).astype(I32)
    zhi, zlo = lax.axis_index("zhi").astype(I32), lax.axis_index("zlo").astype(I32)
    tokens = queries.shape[1]
    model_width = residual.shape[2]
    token_rows = residual.shape[1]
    ctx_count = CY * CX
    scalar = lambda v: v.reshape(1)

    with jax.named_scope("keys_values"):
        heads = queries.shape[2] // HEAD_SIZE
        kv_head = (zhi * ZLO + zlo) * heads // (QUERY_HEADS // KEY_VALUE_HEADS)
        copies = call(
            head_kernel,
            jax.ShapeDtypeStruct((ctx_count, tokens, 2 * HEAD_SIZE), BF16),
            (),
            vmem=8,
            scalars=(scalar(kv_head),),
            any_args=(stay(keys[0]), stay(attention_values[0])),
            scratch=[pltpu.VMEM((2, tokens, HEAD_SIZE), BF16), pltpu.SemaphoreType.DMA((2,))],
            moved=2 << 20,
        )
        all_kv = exchange(copies, CTX)

    with jax.named_scope("expert_weights"):
        own_experts = [a[0] for a in (gate_weight, up_weight, down_weight)]
        other_experts = [lax.ppermute(a, "dp", swap(2)) for a in own_experts]

    with jax.named_scope("out_weight"):
        half = out_weight.shape[0] // 2
        own_half = lax.dynamic_slice_in_dim(out_weight, dp * half, half, 0)
        beside = lax.ppermute(own_half, "zlo", swap(ZLO))
        all_kv, beside, other_experts = lax.optimization_barrier((all_kv, beside, other_experts))
        pair = jnp.stack([own_half, beside])
        from_left = lax.ppermute(pair, "cx", ring(CX, 1))
        from_right = lax.ppermute(pair, "cx", ring(CX, -1))
        pair_other = lax.ppermute(pair, "dp", swap(2))

    with jax.named_scope("attention"):
        attended = call(
            attend_kernel,
            jax.ShapeDtypeStruct((CY * ZLO, tokens // ZLO, queries.shape[2]), BF16),
            (all_kv, key_start.reshape(tokens, 1)),
            vmem=28,
            scalars=(scalar(ctx * tokens),),
            any_args=(stay(queries[0]),),
            scratch=[
                pltpu.VMEM((tokens, ctx_count * tokens), F32),
                pltpu.VMEM((tokens, queries.shape[2]), BF16),
                pltpu.SemaphoreType.DMA((1,)),
            ],
            flops=4 * tokens * heads * ctx_count * tokens * HEAD_SIZE,
            moved=4 << 20,
        )
        attended, pair, from_left, from_right, pair_other = lax.optimization_barrier(
            (attended, pair, from_left, from_right, pair_other)
        )
        far = [
            lax.ppermute(from_left[0], "cx", ring(CX, 1)),
            lax.ppermute(from_right[1], "cx", ring(CX, -1)),
        ]
        early = [pair, from_left, from_right, *far]
        others = [pair_other] + [lax.ppermute(w, "dp", swap(2)) for w in early[1:]]
        gathered = exchange(attended, ("cy", "zlo"))
        gathered = gathered.reshape(CY, ZLO, tokens // ZLO, queries.shape[2])

    with jax.named_scope("projection"):
        half, width = out_weight.shape[0] // 2, out_weight.shape[1]
        group_rows = CY * ZHI * token_rows
        mine, x = scalar(dp), scalar(lax.axis_index("cx").astype(I32))
        partial = call(
            project_kernel,
            jax.ShapeDtypeStruct((CY * ZHI, SUB, model_width // CY), BF16),
            (gathered,),
            vmem=14,
            scalars=(mine, x, scalar(zlo)),
            any_args=[stay(w) for w in [*early, pair_other]] + others[1:],
            scratch=[pltpu.VMEM(w.shape, BF16) for w in early + others]
            + [pltpu.SemaphoreType.DMA((10,))],
            flops=2 * group_rows * 16 * half * width,
            moved=6 << 20,
        )
        parts = exchange(partial, ("cy", "zhi"))

    with jax.named_scope("norm"):
        meta = jnp.concatenate([routes[0], block_masks[0]], axis=1).astype(BF16)
        meta = jnp.pad(meta, ((0, 0), (0, LANES - 2 * TOP)))
        ext, hidden_state = call(
            norm_kernel,
            [
                jax.ShapeDtypeStruct((token_rows, model_width + LANES), BF16),
                jax.ShapeDtypeStruct((token_rows, model_width), BF16),
            ],
            (parts, residual[0], norm_gain.reshape(1, model_width), meta),
            vmem=6,
            moved=2 << 20,
        )
        left = lax.ppermute(ext, "zhi", ring(ZHI, 1))
        right = lax.ppermute(ext, "zhi", ring(ZHI, -1))
        cut = model_width // 2
        far = [
            lax.ppermute(left[:, :cut], "zhi", ring(ZHI, 1)),
            lax.ppermute(right[:, cut:], "zhi", ring(ZHI, -1)),
        ]
        near_ext = (ext, left, right, *far)

    with jax.named_scope("dispatch"):
        dests = ctx_count * ZLO
        capacity = ZHI * token_rows // SUB * CAP
        slots = dests * capacity
        rows = call(
            dispatch_kernel,
            jax.ShapeDtypeStruct((slots, model_width + LANES), BF16),
            near_ext,
            vmem=16,
            scalars=(scalar(zhi),),
            flops=2 * slots * 64 * model_width,
            moved=3 << 20,
        )
        slot_weight = call(
            weight_kernel,
            jax.ShapeDtypeStruct((ZHI * token_rows, slots), F32),
            (router_weight, *near_ext),
            vmem=8,
            scalars=(scalar(zhi),),
            flops=2 * 64 * EXPERTS * model_width,
            moved=2 << 20,
        )
        over = ("cy", "cx", "zlo")
        got = exchange(rows.reshape(dests, capacity, model_width + LANES), over)

    with jax.named_scope("experts"):
        every = own_experts + other_experts
        expert_out = call(
            expert_kernel,
            jax.ShapeDtypeStruct((slots, model_width), BF16),
            (got.reshape(slots, model_width + LANES),),
            vmem=32,
            scalars=(scalar(dp),),
            any_args=[stay(w) if i % 3 == 2 else w for i, w in enumerate(every)],
            scratch=[pltpu.VMEM(a.shape, a.dtype) for a in every] + [pltpu.SemaphoreType.DMA((6,))],
            flops=6 * slots * model_width * 768,
            moved=22 << 20,
        )
        back = exchange(expert_out.reshape(dests, capacity, model_width), over)

    with jax.named_scope("combine"):
        mixed = call(
            combine_kernel,
            jax.ShapeDtypeStruct((ZHI, token_rows, model_width), BF16),
            (slot_weight, back.reshape(slots, model_width)),
            vmem=14,
            scalars=(scalar(zhi),),
            flops=6 * 64 * slots * model_width,
            moved=3 << 20,
        )
        mixture = jnp.sum(exchange(mixed, "zhi").astype(F32), axis=0)
        layer_out = (hidden_state.astype(F32) + mixture).astype(BF16)
    return layer_out[None]


def solution(mesh):
    fine = Mesh(
        mesh.devices.reshape(2, CY, CX, ZHI, ZLO), ("dp", "cy", "cx", "zhi", "zlo")
    )
    tp = ("zhi", "zlo")
    all_ctx = CTX + tp
    in_specs = (
        P("dp", CTX, tp),
        P("dp", CTX, None),
        P("dp", CTX, None),
        P("dp", CTX),
        P(tp, CTX),
        P("dp", all_ctx, None),
        P(),
        P(),
        P("dp", all_ctx, None),
        P("dp", all_ctx, None),
        P(all_ctx, None, "dp"),
        P(all_ctx, None, "dp"),
        P(all_ctx, "dp", None),
    )
    out_specs = P("dp", all_ctx, None)
    return jax.shard_map(local, mesh=fine, in_specs=in_specs, out_specs=out_specs, check_vma=False)
```

```python
import math

import jax
import jax.numpy as jnp
from jax import lax
from jax.experimental import pallas as pl
from jax.experimental.pallas import tpu as pltpu
from jax.sharding import Mesh
from jax.sharding import PartitionSpec as P

QUERY_HEADS = 64
KEY_VALUE_HEADS = 4
HEAD_SIZE = 128
MASK_BLOCKS = 6
TOP = 8
EXPERTS = 128
CAP = 2
SCORE_FLOOR = -1e30
LANES = 128
SUB = 16
MIB = 1024 * 1024

CY, CX, ZHI, ZLO = 4, 4, 4, 2
CTX = ("cy", "cx")
F32, BF16, I32 = jnp.float32, jnp.bfloat16, jnp.int32


def call(kernel, out_shape, args, vmem, scalars=(), any_args=(), scratch=(), flops=0, moved=0):
    specs = [pl.BlockSpec(memory_space=pltpu.SMEM) for _ in scalars]
    specs += [pl.BlockSpec(memory_space=pltpu.VMEM) for _ in args]
    specs += [pl.BlockSpec(memory_space=pl.ANY) for _ in any_args]
    many = isinstance(out_shape, (list, tuple))
    whole = pl.BlockSpec(memory_space=pltpu.VMEM)
    return pl.pallas_call(
        kernel,
        out_shape=out_shape,
        in_specs=specs,
        out_specs=[whole] * len(out_shape) if many else whole,
        scratch_shapes=list(scratch),
        cost_estimate=pl.CostEstimate(flops=flops, bytes_accessed=moved, transcendentals=0),
        compiler_params=pltpu.CompilerParams(vmem_limit_bytes=vmem * MIB),
    )(*scalars, *args, *any_args)


def head_kernel(head_ref, key_ref, value_ref, out_ref, pair_ref, sems):
    columns = pl.ds(pl.multiple_of(head_ref[0] * HEAD_SIZE, HEAD_SIZE), HEAD_SIZE)
    copies = [
        pltpu.make_async_copy(ref.at[:, columns], pair_ref.at[i], sems.at[i])
        for i, ref in enumerate((key_ref, value_ref))
    ]
    for copy in copies:
        copy.start()
    for copy in copies:
        copy.wait()
    pair = jnp.concatenate([pair_ref[0], pair_ref[1]], axis=1)
    for c in range(out_ref.shape[0]):
        out_ref[c] = pair


def attend_kernel(first_ref, kv_ref, start_ref, query_hbm, out_ref, bias_ref, query_ref, sem):
    copy = pltpu.make_async_copy(query_hbm, query_ref, sem.at[0])
    copy.start()
    tokens = query_ref.shape[0]
    heads = query_ref.shape[1] // HEAD_SIZE
    keys = kv_ref.shape[0] * kv_ref.shape[1]
    key_rows = kv_ref[:, :, :HEAD_SIZE].reshape(keys, HEAD_SIZE)
    value_rows = kv_ref[:, :, HEAD_SIZE:].reshape(keys, HEAD_SIZE)
    position = first_ref[0] + lax.broadcasted_iota(I32, (tokens, keys), 0)
    key_pos = lax.broadcasted_iota(I32, (tokens, keys), 1)
    visible = (key_pos >= start_ref[...]) & (key_pos <= position)
    bias_ref[...] = jnp.where(visible, 0.0, SCORE_FLOOR)
    copy.wait()
    scale = math.log2(math.e) / math.sqrt(HEAD_SIZE)
    bias = bias_ref[...]
    bias = jnp.concatenate([bias, bias], axis=0)
    for head in range(0, heads, 2):
        columns = [slice(h * HEAD_SIZE, (h + 1) * HEAD_SIZE) for h in (head, head + 1)]
        scores = lax.dot_general(
            jnp.concatenate([query_ref[:, c] for c in columns], axis=0),
            key_rows,
            (((1,), (1,)), ((), ())),
            preferred_element_type=F32,
        )
        scores = scores * scale + bias
        row_max = jnp.max(scores, axis=1, keepdims=True)
        weights = jnp.exp2(scores - row_max)
        row_sum = jnp.sum(weights, axis=1, keepdims=True)
        mixed = jnp.dot(weights.astype(BF16), value_rows, preferred_element_type=F32)
        attended = (mixed / row_sum).astype(BF16)
        for which in range(2):
            for z in range(ZHI * ZLO):
                block = attended[which * tokens + z * SUB : which * tokens + (z + 1) * SUB]
                rows = slice((z // ZLO) * SUB, (z // ZLO + 1) * SUB)
                for y in range(CY):
                    out_ref[y * ZLO + z % ZLO, rows, columns[which]] = block


def project_kernel(dp_ref, x_ref, zlo_ref, att_ref, *refs):
    count = 2 * CX * ZLO
    sources, out_ref, held_ref, sems = refs[:count], refs[count], refs[count + 1], refs[count + 2]
    copies = [
        pltpu.make_async_copy(source, held_ref.at[i], sems.at[i]) for i, source in enumerate(sources)
    ]
    for copy in copies:
        copy.start()
    half, width = held_ref.shape[1:]
    rows = att_ref.shape[0] * att_ref.shape[2]
    for step, away in enumerate((0, CX - 1, 1, 2)):
        total = jnp.zeros((rows, width), F32)
        for part in range(2):
            columns = pl.ds(
                pl.multiple_of((dp_ref[0] if part == 0 else 1 - dp_ref[0]) * half, half), half
            )
            for near in range(ZLO):
                source = zlo_ref[0] if near == 0 else 1 - zlo_ref[0]
                piece = CX * ZLO * part + ZLO * step + near
                copies[piece].wait()
                total += jnp.dot(
                    att_ref[:, source, :, columns].reshape(rows, half),
                    held_ref[piece],
                    preferred_element_type=F32,
                )
        place = pl.multiple_of(((x_ref[0] + away) & (CX - 1)) * width, width)
        out_ref[:, :, pl.ds(place, width)] = total.astype(BF16).reshape(rows // SUB, SUB, width)


def norm_kernel(parts_ref, residual_ref, gain_ref, meta_ref, ext_ref, hidden_ref):
    model_width = residual_ref.shape[1]
    width = model_width // CY
    zs = ZHI
    pieces = []
    square_sum = jnp.zeros((SUB, 1), F32)
    for y in range(CY):
        columns = slice(y * width, (y + 1) * width)
        projected = sum(parts_ref[y * zs + z].astype(F32) for z in range(zs))
        hidden = (residual_ref[:, columns].astype(F32) + projected).astype(BF16)
        hidden_ref[:, columns] = hidden
        wide = hidden.astype(F32)
        square_sum += jnp.sum(wide * wide, axis=1, keepdims=True)
        pieces.append(wide)
    inverse = lax.rsqrt(square_sum / model_width + 1e-06)
    for y in range(CY):
        columns = slice(y * width, (y + 1) * width)
        normed = (pieces[y] * inverse * gain_ref[:, columns].astype(F32)).astype(BF16)
        ext_ref[:, columns] = normed
    ext_ref[:, model_width:] = meta_ref[...]


def slot_hits(meta, zhi, slots, slot_capacity):
    tokens = meta.shape[0]
    slot = lax.broadcasted_iota(I32, (tokens, slots), 1)
    dest = slot >> (slot_capacity.bit_length() - 1)
    expert = (dest >> 1) * (ZHI * ZLO) + zhi * ZLO + (dest & 1)
    hits = [meta[:, k : k + 1].astype(F32).astype(I32) == expert for k in range(TOP)]
    named = sum(h.astype(F32) for h in hits)
    later = lax.broadcasted_iota(I32, (tokens, tokens), 0) > lax.broadcasted_iota(
        I32, (tokens, tokens), 1
    )
    earlier = jnp.dot(later.astype(BF16), named.astype(BF16), preferred_element_type=F32)
    place = (slot & (slot_capacity - 1)).astype(F32)
    chosen = jnp.where((named > 0.5) & (earlier == place), 1.0, 0.0)
    return hits, chosen


def gathered_rows(refs):
    own, left, right, far_first, far_second = [ref[...] for ref in refs]
    far = jnp.concatenate([far_first, far_second], axis=1)
    return jnp.concatenate([own, left, right, far], axis=0)


def dispatch_kernel(zhi_ref, *refs):
    ext, rows_ref = gathered_rows(refs[:-1]), refs[-1]
    tokens = ext.shape[0]
    width = ext.shape[1] - LANES
    meta = ext[:, width:]
    hits, chosen = slot_hits(meta, zhi_ref[0], rows_ref.shape[0], tokens // SUB * CAP)
    masks = sum(
        jnp.where(hits[k], meta[:, TOP + k : TOP + k + 1].astype(F32), 0.0) for k in range(TOP)
    )
    along = (((0,), (0,)), ((), ()))
    rows_ref[:, :width] = lax.dot_general(
        chosen.astype(BF16), ext[:, :width], along, preferred_element_type=F32
    ).astype(BF16)
    ones = jnp.ones((tokens, LANES), BF16)
    rows_ref[:, width:] = lax.dot_general(
        (masks * chosen).astype(BF16), ones, along, preferred_element_type=F32
    ).astype(BF16)


def weight_kernel(zhi_ref, router_ref, *refs):
    ext, out_ref = gathered_rows(refs[:-1]), refs[-1]
    tokens = ext.shape[0]
    model_width = ext.shape[1] - LANES
    slots = out_ref.shape[1]
    meta, normed = ext[:, model_width:], ext[:, :model_width]
    logits = jnp.dot(normed, router_ref[...], preferred_element_type=F32)
    lanes = lax.broadcasted_iota(I32, (tokens, EXPERTS), 1)
    exps = []
    for k in range(TOP):
        route = meta[:, k : k + 1].astype(F32).astype(I32)
        picked = jnp.sum(jnp.where(lanes == route, logits, 0.0), axis=1, keepdims=True)
        exps.append(jnp.exp(picked))
    total = sum(exps)
    hits, chosen = slot_hits(meta, zhi_ref[0], slots, tokens // SUB * CAP)
    route_weight = sum(jnp.where(hits[k], exps[k] / total, 0.0) for k in range(TOP))
    out_ref[...] = route_weight * chosen


def expert_kernel(dp_ref, rows_ref, *refs):
    weights, out_ref, held, sems = refs[:6], refs[6], refs[7:13], refs[13]
    copies = [pltpu.make_async_copy(weights[i], held[i], sems.at[i]) for i in range(6)]
    for i in (0, 1, 3, 4, 2, 5):
        copies[i].start()
    model_width = out_ref.shape[1]
    masks = rows_ref[:, model_width:].astype(F32).astype(I32)
    blocks = MASK_BLOCKS // 2
    acts = []
    for part in range(2):
        gate_ref, up_ref = held[3 * part], held[3 * part + 1]
        first = (dp_ref[0] if part == 0 else 1 - dp_ref[0]) * blocks
        copies[3 * part].wait()
        copies[3 * part + 1].wait()
        both = jnp.dot(
            rows_ref[:, :model_width],
            jnp.concatenate([gate_ref[...], up_ref[...]], axis=1),
            preferred_element_type=F32,
        )
        units = gate_ref.shape[1]
        keep = jnp.concatenate(
            [(jnp.right_shift(masks, first + b) & 1).astype(F32) for b in range(blocks)], axis=1
        )
        acts.append((jax.nn.silu(both[:, :units]) * both[:, units:] * keep).astype(BF16))
    copies[2].wait()
    copies[5].wait()
    activated = jnp.concatenate(acts, axis=1)
    step = 512
    for j in range(model_width // step):
        columns = slice(j * step, (j + 1) * step)
        down = jnp.concatenate([held[2][:, columns], held[5][:, columns]], axis=0)
        out_ref[:, columns] = jnp.dot(activated, down, preferred_element_type=F32).astype(BF16)


def combine_kernel(zhi_ref, weight_ref, back_ref, out_ref):
    weight = weight_ref[...]
    high = weight.astype(BF16)
    rest = weight - high.astype(F32)
    middle = rest.astype(BF16)
    low = (rest - middle.astype(F32)).astype(BF16)
    stacked = jnp.concatenate([high, middle, low], axis=0)
    tokens = weight.shape[0]
    model_width = back_ref.shape[1]
    step = 1024
    for j in range(model_width // step):
        columns = slice(j * step, (j + 1) * step)
        parts = jnp.dot(stacked, back_ref[:, columns], preferred_element_type=F32)
        total = parts[:tokens] + parts[tokens : 2 * tokens] + parts[2 * tokens :]
        total = total.astype(BF16)
        for place, away in enumerate((0, ZHI - 1, 1, 2)):
            home = (zhi_ref[0] + away) & (ZHI - 1)
            out_ref[home, :, columns] = total[place * SUB : (place + 1) * SUB]


def stay(x):
    return pltpu.with_memory_space_constraint(x, pltpu.HBM)


def swap(n):
    return [(i, i ^ 1) for i in range(n)]


def ring(n, step):
    return [(i, (i + step) % n) for i in range(n)]


def exchange(x, axes):
    return lax.all_to_all(x, axes, split_axis=0, concat_axis=0, tiled=True)


def local(
    queries,
    keys,
    attention_values,
    key_start,
    out_weight,
    residual,
    norm_gain,
    router_weight,
    routes,
    block_masks,
    gate_weight,
    up_weight,
    down_weight,
):
    dp = lax.axis_index("dp").astype(I32)
    ctx = lax.axis_index(CTX).astype(I32)
    zhi, zlo = lax.axis_index("zhi").astype(I32), lax.axis_index("zlo").astype(I32)
    tokens = queries.shape[1]
    model_width = residual.shape[2]
    token_rows = residual.shape[1]
    ctx_count = CY * CX
    scalar = lambda v: v.reshape(1)

    with jax.named_scope("keys_values"):
        heads = queries.shape[2] // HEAD_SIZE
        kv_head = (zhi * ZLO + zlo) * heads // (QUERY_HEADS // KEY_VALUE_HEADS)
        copies = call(
            head_kernel,
            jax.ShapeDtypeStruct((ctx_count, tokens, 2 * HEAD_SIZE), BF16),
            (),
            vmem=8,
            scalars=(scalar(kv_head),),
            any_args=(stay(keys[0]), stay(attention_values[0])),
            scratch=[pltpu.VMEM((2, tokens, HEAD_SIZE), BF16), pltpu.SemaphoreType.DMA((2,))],
            moved=2 << 20,
        )
        all_kv = exchange(copies, CTX)

    with jax.named_scope("expert_weights"):
        own_experts = [a[0] for a in (gate_weight, up_weight, down_weight)]
        other_experts = [lax.ppermute(a, "dp", swap(2)) for a in own_experts]

    with jax.named_scope("out_weight"):
        half = out_weight.shape[0] // 2
        own_half = lax.dynamic_slice_in_dim(out_weight, dp * half, half, 0)
        beside = lax.ppermute(own_half, "zlo", swap(ZLO))
        own_other = lax.ppermute(own_half, "dp", swap(2))
        all_kv, beside, own_other, other_experts = lax.optimization_barrier(
            (all_kv, beside, own_other, other_experts)
        )
        left_own = lax.ppermute(own_half, "cx", ring(CX, 1))
        right_beside = lax.ppermute(beside, "cx", ring(CX, -1))
        left_beside = lax.ppermute(beside, "cx", ring(CX, 1))
        right_own = lax.ppermute(own_half, "cx", ring(CX, -1))
        beside_other = lax.ppermute(beside, "dp", swap(2))

    with jax.named_scope("attention"):
        attended = call(
            attend_kernel,
            jax.ShapeDtypeStruct((CY * ZLO, tokens // ZLO, queries.shape[2]), BF16),
            (all_kv, key_start.reshape(tokens, 1)),
            vmem=28,
            scalars=(scalar(ctx * tokens),),
            any_args=(stay(queries[0]),),
            scratch=[
                pltpu.VMEM((tokens, ctx_count * tokens), F32),
                pltpu.VMEM((tokens, queries.shape[2]), BF16),
                pltpu.SemaphoreType.DMA((1,)),
            ],
            flops=4 * tokens * heads * ctx_count * tokens * HEAD_SIZE,
            moved=4 << 20,
        )
        attended, left_own, left_beside, right_own, right_beside, beside_other = (
            lax.optimization_barrier(
                (attended, left_own, left_beside, right_own, right_beside, beside_other)
            )
        )
        far_own = lax.ppermute(left_own, "cx", ring(CX, 1))
        far_beside = lax.ppermute(right_beside, "cx", ring(CX, -1))
        near = [own_half, beside]
        later = [left_own, left_beside, right_own, right_beside, far_own, far_beside]
        others = [own_other, beside_other] + [lax.ppermute(w, "dp", swap(2)) for w in later]
        gathered = exchange(attended, ("cy", "zlo"))
        gathered = gathered.reshape(CY, ZLO, tokens // ZLO, queries.shape[2])

    with jax.named_scope("projection"):
        half, width = out_weight.shape[0] // 2, out_weight.shape[1]
        group_rows = CY * ZHI * token_rows
        mine, x = scalar(dp), scalar(lax.axis_index("cx").astype(I32))
        partial = call(
            project_kernel,
            jax.ShapeDtypeStruct((CY * ZHI, SUB, model_width // CY), BF16),
            (gathered,),
            vmem=14,
            scalars=(mine, x, scalar(zlo)),
            any_args=[stay(w) for w in near + later + others[:2]] + others[2:],
            scratch=[
                pltpu.VMEM((2 * CX * ZLO, half, width), BF16),
                pltpu.SemaphoreType.DMA((2 * CX * ZLO,)),
            ],
            flops=2 * group_rows * 16 * half * width,
            moved=6 << 20,
        )
        parts = exchange(partial, ("cy", "zhi"))

    with jax.named_scope("norm"):
        meta = jnp.concatenate([routes[0], block_masks[0]], axis=1).astype(BF16)
        meta = jnp.pad(meta, ((0, 0), (0, LANES - 2 * TOP)))
        ext, hidden_state = call(
            norm_kernel,
            [
                jax.ShapeDtypeStruct((token_rows, model_width + LANES), BF16),
                jax.ShapeDtypeStruct((token_rows, model_width), BF16),
            ],
            (parts, residual[0], norm_gain.reshape(1, model_width), meta),
            vmem=6,
            moved=2 << 20,
        )
        left = lax.ppermute(ext, "zhi", ring(ZHI, 1))
        right = lax.ppermute(ext, "zhi", ring(ZHI, -1))
        cut = model_width // 2
        far = [
            lax.ppermute(left[:, :cut], "zhi", ring(ZHI, 1)),
            lax.ppermute(right[:, cut:], "zhi", ring(ZHI, -1)),
        ]
        near_ext = (ext, left, right, *far)

    with jax.named_scope("dispatch"):
        dests = ctx_count * ZLO
        capacity = ZHI * token_rows // SUB * CAP
        slots = dests * capacity
        rows = call(
            dispatch_kernel,
            jax.ShapeDtypeStruct((slots, model_width + LANES), BF16),
            near_ext,
            vmem=16,
            scalars=(scalar(zhi),),
            flops=2 * slots * 64 * model_width,
            moved=3 << 20,
        )
        slot_weight = call(
            weight_kernel,
            jax.ShapeDtypeStruct((ZHI * token_rows, slots), F32),
            (router_weight, *near_ext),
            vmem=8,
            scalars=(scalar(zhi),),
            flops=2 * 64 * EXPERTS * model_width,
            moved=2 << 20,
        )
        over = ("cy", "cx", "zlo")
        got = exchange(rows.reshape(dests, capacity, model_width + LANES), over)

    with jax.named_scope("experts"):
        every = own_experts + other_experts
        expert_out = call(
            expert_kernel,
            jax.ShapeDtypeStruct((slots, model_width), BF16),
            (got.reshape(slots, model_width + LANES),),
            vmem=32,
            scalars=(scalar(dp),),
            any_args=[stay(w) if i % 3 == 2 else w for i, w in enumerate(every)],
            scratch=[pltpu.VMEM(a.shape, a.dtype) for a in every] + [pltpu.SemaphoreType.DMA((6,))],
            flops=6 * slots * model_width * 768,
            moved=22 << 20,
        )
        back = exchange(expert_out.reshape(dests, capacity, model_width), over)

    with jax.named_scope("combine"):
        mixed = call(
            combine_kernel,
            jax.ShapeDtypeStruct((ZHI, token_rows, model_width), BF16),
            (slot_weight, back.reshape(slots, model_width)),
            vmem=14,
            scalars=(scalar(zhi),),
            flops=6 * 64 * slots * model_width,
            moved=3 << 20,
        )
        mixture = jnp.sum(exchange(mixed, "zhi").astype(F32), axis=0)
        layer_out = (hidden_state.astype(F32) + mixture).astype(BF16)
    return layer_out[None]


def solution(mesh):
    fine = Mesh(
        mesh.devices.reshape(2, CY, CX, ZHI, ZLO), ("dp", "cy", "cx", "zhi", "zlo")
    )
    tp = ("zhi", "zlo")
    all_ctx = CTX + tp
    in_specs = (
        P("dp", CTX, tp),
        P("dp", CTX, None),
        P("dp", CTX, None),
        P("dp", CTX),
        P(tp, CTX),
        P("dp", all_ctx, None),
        P(),
        P(),
        P("dp", all_ctx, None),
        P("dp", all_ctx, None),
        P(all_ctx, None, "dp"),
        P(all_ctx, None, "dp"),
        P(all_ctx, "dp", None),
    )
    out_specs = P("dp", all_ctx, None)
    return jax.shard_map(local, mesh=fine, in_specs=in_specs, out_specs=out_specs, check_vma=False)
```

```python
import math

import jax
import jax.numpy as jnp
from jax import lax
from jax.experimental import pallas as pl
from jax.experimental.pallas import tpu as pltpu
from jax.sharding import Mesh
from jax.sharding import PartitionSpec as P

QUERY_HEADS = 64
KEY_VALUE_HEADS = 4
HEAD_SIZE = 128
MASK_BLOCKS = 6
TOP = 8
EXPERTS = 128
CAP = 2
SCORE_FLOOR = -1e30
LANES = 128
SUB = 16
DOWN_PARTS = 4
MIB = 1024 * 1024

CY, CX, ZHI, ZLO = 4, 4, 4, 2
CTX = ("cy", "cx")
F32, BF16, I32 = jnp.float32, jnp.bfloat16, jnp.int32


def call(kernel, out_shape, args, vmem, scalars=(), any_args=(), scratch=(), flops=0, moved=0):
    specs = [pl.BlockSpec(memory_space=pltpu.SMEM) for _ in scalars]
    specs += [pl.BlockSpec(memory_space=pltpu.VMEM) for _ in args]
    specs += [pl.BlockSpec(memory_space=pl.ANY) for _ in any_args]
    many = isinstance(out_shape, (list, tuple))
    whole = pl.BlockSpec(memory_space=pltpu.VMEM)
    return pl.pallas_call(
        kernel,
        out_shape=out_shape,
        in_specs=specs,
        out_specs=[whole] * len(out_shape) if many else whole,
        scratch_shapes=list(scratch),
        cost_estimate=pl.CostEstimate(flops=flops, bytes_accessed=moved, transcendentals=0),
        compiler_params=pltpu.CompilerParams(vmem_limit_bytes=vmem * MIB),
    )(*scalars, *args, *any_args)


def head_kernel(head_ref, key_ref, value_ref, out_ref, pair_ref, sems):
    columns = pl.ds(pl.multiple_of(head_ref[0] * HEAD_SIZE, HEAD_SIZE), HEAD_SIZE)
    copies = [
        pltpu.make_async_copy(ref.at[:, columns], pair_ref.at[i], sems.at[i])
        for i, ref in enumerate((key_ref, value_ref))
    ]
    for copy in copies:
        copy.start()
    for copy in copies:
        copy.wait()
    pair = jnp.concatenate([pair_ref[0], pair_ref[1]], axis=1)
    for c in range(out_ref.shape[0]):
        out_ref[c] = pair


def attend_kernel(first_ref, kv_ref, start_ref, query_hbm, out_ref, bias_ref, query_ref, sem):
    copy = pltpu.make_async_copy(query_hbm, query_ref, sem.at[0])
    copy.start()
    tokens = query_ref.shape[0]
    heads = query_ref.shape[1] // HEAD_SIZE
    keys = kv_ref.shape[0] * kv_ref.shape[1]
    key_rows = kv_ref[:, :, :HEAD_SIZE].reshape(keys, HEAD_SIZE)
    value_rows = kv_ref[:, :, HEAD_SIZE:].reshape(keys, HEAD_SIZE)
    position = first_ref[0] + lax.broadcasted_iota(I32, (tokens, keys), 0)
    key_pos = lax.broadcasted_iota(I32, (tokens, keys), 1)
    visible = (key_pos >= start_ref[...]) & (key_pos <= position)
    bias_ref[...] = jnp.where(visible, 0.0, SCORE_FLOOR)
    copy.wait()
    scale = math.log2(math.e) / math.sqrt(HEAD_SIZE)
    bias = bias_ref[...]
    bias = jnp.concatenate([bias, bias], axis=0)
    for head in range(0, heads, 2):
        columns = [slice(h * HEAD_SIZE, (h + 1) * HEAD_SIZE) for h in (head, head + 1)]
        scores = lax.dot_general(
            jnp.concatenate([query_ref[:, c] for c in columns], axis=0),
            key_rows,
            (((1,), (1,)), ((), ())),
            preferred_element_type=F32,
        )
        scores = scores * scale + bias
        row_max = jnp.max(scores, axis=1, keepdims=True)
        weights = jnp.exp2(scores - row_max)
        row_sum = jnp.sum(weights, axis=1, keepdims=True)
        mixed = jnp.dot(weights.astype(BF16), value_rows, preferred_element_type=F32)
        attended = (mixed / row_sum).astype(BF16)
        for which in range(2):
            for z in range(ZHI * ZLO):
                block = attended[which * tokens + z * SUB : which * tokens + (z + 1) * SUB]
                rows = slice((z // ZLO) * SUB, (z // ZLO + 1) * SUB)
                for y in range(CY):
                    out_ref[y * ZLO + z % ZLO, rows, columns[which]] = block


def project_kernel(dp_ref, x_ref, zlo_ref, att_ref, *refs):
    count = 2 * CX * ZLO
    sources, out_ref, held_ref, sems = refs[:count], refs[count], refs[count + 1], refs[count + 2]
    copies = [
        pltpu.make_async_copy(source, held_ref.at[i], sems.at[i]) for i, source in enumerate(sources)
    ]
    for step in range(CX):
        for part in range(2):
            for near in range(ZLO):
                copies[CX * ZLO * part + ZLO * step + near].start()
    half, width = held_ref.shape[1:]
    rows = att_ref.shape[0] * att_ref.shape[2]
    for step, away in enumerate((0, CX - 1, 1, 2)):
        total = jnp.zeros((rows, width), F32)
        for part in range(2):
            columns = pl.ds(
                pl.multiple_of((dp_ref[0] if part == 0 else 1 - dp_ref[0]) * half, half), half
            )
            for near in range(ZLO):
                source = zlo_ref[0] if near == 0 else 1 - zlo_ref[0]
                piece = CX * ZLO * part + ZLO * step + near
                copies[piece].wait()
                total += jnp.dot(
                    att_ref[:, source, :, columns].reshape(rows, half),
                    held_ref[piece],
                    preferred_element_type=F32,
                )
        place = pl.multiple_of(((x_ref[0] + away) & (CX - 1)) * width, width)
        out_ref[:, :, pl.ds(place, width)] = total.astype(BF16).reshape(rows // SUB, SUB, width)


def norm_kernel(parts_ref, residual_ref, gain_ref, meta_ref, ext_ref, hidden_ref):
    model_width = residual_ref.shape[1]
    width = model_width // CY
    zs = ZHI
    pieces = []
    square_sum = jnp.zeros((SUB, 1), F32)
    for y in range(CY):
        columns = slice(y * width, (y + 1) * width)
        projected = sum(parts_ref[y * zs + z].astype(F32) for z in range(zs))
        hidden = (residual_ref[:, columns].astype(F32) + projected).astype(BF16)
        hidden_ref[:, columns] = hidden
        wide = hidden.astype(F32)
        square_sum += jnp.sum(wide * wide, axis=1, keepdims=True)
        pieces.append(wide)
    inverse = lax.rsqrt(square_sum / model_width + 1e-06)
    for y in range(CY):
        columns = slice(y * width, (y + 1) * width)
        normed = (pieces[y] * inverse * gain_ref[:, columns].astype(F32)).astype(BF16)
        ext_ref[:, columns] = normed
    ext_ref[:, model_width:] = meta_ref[...]


def slot_hits(meta, zhi, slots, slot_capacity):
    tokens = meta.shape[0]
    slot = lax.broadcasted_iota(I32, (tokens, slots), 1)
    dest = slot >> (slot_capacity.bit_length() - 1)
    expert = (dest >> 1) * (ZHI * ZLO) + zhi * ZLO + (dest & 1)
    hits = [meta[:, k : k + 1].astype(F32).astype(I32) == expert for k in range(TOP)]
    named = sum(h.astype(F32) for h in hits)
    later = lax.broadcasted_iota(I32, (tokens, tokens), 0) > lax.broadcasted_iota(
        I32, (tokens, tokens), 1
    )
    earlier = jnp.dot(later.astype(BF16), named.astype(BF16), preferred_element_type=F32)
    place = (slot & (slot_capacity - 1)).astype(F32)
    chosen = jnp.where((named > 0.5) & (earlier == place), 1.0, 0.0)
    return hits, chosen


def gathered_rows(refs):
    own, left, right, far_first, far_second = [ref[...] for ref in refs]
    far = jnp.concatenate([far_first, far_second], axis=1)
    return jnp.concatenate([own, left, right, far], axis=0)


def dispatch_kernel(zhi_ref, *refs):
    ext, rows_ref = gathered_rows(refs[:-1]), refs[-1]
    tokens = ext.shape[0]
    width = ext.shape[1] - LANES
    meta = ext[:, width:]
    hits, chosen = slot_hits(meta, zhi_ref[0], rows_ref.shape[0], tokens // SUB * CAP)
    masks = sum(
        jnp.where(hits[k], meta[:, TOP + k : TOP + k + 1].astype(F32), 0.0) for k in range(TOP)
    )
    along = (((0,), (0,)), ((), ()))
    rows_ref[:, :width] = lax.dot_general(
        chosen.astype(BF16), ext[:, :width], along, preferred_element_type=F32
    ).astype(BF16)
    ones = jnp.ones((tokens, LANES), BF16)
    rows_ref[:, width:] = lax.dot_general(
        (masks * chosen).astype(BF16), ones, along, preferred_element_type=F32
    ).astype(BF16)


def weight_kernel(zhi_ref, router_ref, *refs):
    ext, out_ref = gathered_rows(refs[:-1]), refs[-1]
    tokens = ext.shape[0]
    model_width = ext.shape[1] - LANES
    slots = out_ref.shape[1]
    meta, normed = ext[:, model_width:], ext[:, :model_width]
    logits = jnp.dot(normed, router_ref[...], preferred_element_type=F32)
    lanes = lax.broadcasted_iota(I32, (tokens, EXPERTS), 1)
    exps = []
    for k in range(TOP):
        route = meta[:, k : k + 1].astype(F32).astype(I32)
        picked = jnp.sum(jnp.where(lanes == route, logits, 0.0), axis=1, keepdims=True)
        exps.append(jnp.exp(picked))
    total = sum(exps)
    hits, chosen = slot_hits(meta, zhi_ref[0], slots, tokens // SUB * CAP)
    route_weight = sum(jnp.where(hits[k], exps[k] / total, 0.0) for k in range(TOP))
    out_ref[...] = route_weight * chosen


def expert_kernel(dp_ref, rows_ref, *refs):
    weights, out_ref, held, sems = refs[:6], refs[6], refs[7:13], refs[13]
    model_width = out_ref.shape[1]
    step = model_width // DOWN_PARTS
    copies = {i: pltpu.make_async_copy(weights[i], held[i], sems.at[i]) for i in (0, 1, 3, 4)}
    downs = []
    for j in range(DOWN_PARTS):
        columns = pl.ds(j * step, step)
        downs.append(
            [
                pltpu.make_async_copy(
                    weights[i].at[:, columns], held[i].at[:, columns], sems.at[6 + 2 * j + i // 3]
                )
                for i in (2, 5)
            ]
        )
    for copy in copies.values():
        copy.start()
    for pair in downs:
        for copy in pair:
            copy.start()
    masks = rows_ref[:, model_width:].astype(F32).astype(I32)
    blocks = MASK_BLOCKS // 2
    acts = []
    for part in range(2):
        gate_ref, up_ref = held[3 * part], held[3 * part + 1]
        first = (dp_ref[0] if part == 0 else 1 - dp_ref[0]) * blocks
        copies[3 * part].wait()
        copies[3 * part + 1].wait()
        both = jnp.dot(
            rows_ref[:, :model_width],
            jnp.concatenate([gate_ref[...], up_ref[...]], axis=1),
            preferred_element_type=F32,
        )
        units = gate_ref.shape[1]
        keep = jnp.concatenate(
            [(jnp.right_shift(masks, first + b) & 1).astype(F32) for b in range(blocks)], axis=1
        )
        acts.append((jax.nn.silu(both[:, :units]) * both[:, units:] * keep).astype(BF16))
    activated = jnp.concatenate(acts, axis=1)
    for j in range(DOWN_PARTS):
        for copy in downs[j]:
            copy.wait()
        columns = slice(j * step, (j + 1) * step)
        down = jnp.concatenate([held[2][:, columns], held[5][:, columns]], axis=0)
        out_ref[:, columns] = jnp.dot(activated, down, preferred_element_type=F32).astype(BF16)


def combine_kernel(zhi_ref, weight_ref, back_ref, out_ref):
    weight = weight_ref[...]
    high = weight.astype(BF16)
    rest = weight - high.astype(F32)
    middle = rest.astype(BF16)
    low = (rest - middle.astype(F32)).astype(BF16)
    stacked = jnp.concatenate([high, middle, low], axis=0)
    tokens = weight.shape[0]
    model_width = back_ref.shape[1]
    step = 1024
    for j in range(model_width // step):
        columns = slice(j * step, (j + 1) * step)
        parts = jnp.dot(stacked, back_ref[:, columns], preferred_element_type=F32)
        total = parts[:tokens] + parts[tokens : 2 * tokens] + parts[2 * tokens :]
        total = total.astype(BF16)
        for place, away in enumerate((0, ZHI - 1, 1, 2)):
            home = (zhi_ref[0] + away) & (ZHI - 1)
            out_ref[home, :, columns] = total[place * SUB : (place + 1) * SUB]


def stay(x):
    return pltpu.with_memory_space_constraint(x, pltpu.HBM)


def swap(n):
    return [(i, i ^ 1) for i in range(n)]


def ring(n, step):
    return [(i, (i + step) % n) for i in range(n)]


def exchange(x, axes):
    return lax.all_to_all(x, axes, split_axis=0, concat_axis=0, tiled=True)


def local(
    queries,
    keys,
    attention_values,
    key_start,
    out_weight,
    residual,
    norm_gain,
    router_weight,
    routes,
    block_masks,
    gate_weight,
    up_weight,
    down_weight,
):
    dp = lax.axis_index("dp").astype(I32)
    ctx = lax.axis_index(CTX).astype(I32)
    zhi, zlo = lax.axis_index("zhi").astype(I32), lax.axis_index("zlo").astype(I32)
    tokens = queries.shape[1]
    model_width = residual.shape[2]
    token_rows = residual.shape[1]
    ctx_count = CY * CX
    scalar = lambda v: v.reshape(1)

    with jax.named_scope("keys_values"):
        heads = queries.shape[2] // HEAD_SIZE
        kv_head = (zhi * ZLO + zlo) * heads // (QUERY_HEADS // KEY_VALUE_HEADS)
        copies = call(
            head_kernel,
            jax.ShapeDtypeStruct((ctx_count, tokens, 2 * HEAD_SIZE), BF16),
            (),
            vmem=8,
            scalars=(scalar(kv_head),),
            any_args=(stay(keys[0]), stay(attention_values[0])),
            scratch=[pltpu.VMEM((2, tokens, HEAD_SIZE), BF16), pltpu.SemaphoreType.DMA((2,))],
            moved=2 << 20,
        )
        all_kv = exchange(copies, CTX)

    with jax.named_scope("expert_weights"):
        own_experts = [a[0] for a in (gate_weight, up_weight, down_weight)]
        other_experts = [lax.ppermute(a, "dp", swap(2)) for a in own_experts]

    with jax.named_scope("out_weight"):
        half = out_weight.shape[0] // 2
        own_half = lax.dynamic_slice_in_dim(out_weight, dp * half, half, 0)
        beside = lax.ppermute(own_half, "zlo", swap(ZLO))
        own_other = lax.ppermute(own_half, "dp", swap(2))
        all_kv, beside, own_other, other_experts = lax.optimization_barrier(
            (all_kv, beside, own_other, other_experts)
        )
        left_own = lax.ppermute(own_half, "cx", ring(CX, 1))
        right_beside = lax.ppermute(beside, "cx", ring(CX, -1))
        left_beside = lax.ppermute(beside, "cx", ring(CX, 1))
        right_own = lax.ppermute(own_half, "cx", ring(CX, -1))
        beside_other = lax.ppermute(beside, "dp", swap(2))

    with jax.named_scope("attention"):
        attended = call(
            attend_kernel,
            jax.ShapeDtypeStruct((CY * ZLO, tokens // ZLO, queries.shape[2]), BF16),
            (all_kv, key_start.reshape(tokens, 1)),
            vmem=28,
            scalars=(scalar(ctx * tokens),),
            any_args=(stay(queries[0]),),
            scratch=[
                pltpu.VMEM((tokens, ctx_count * tokens), F32),
                pltpu.VMEM((tokens, queries.shape[2]), BF16),
                pltpu.SemaphoreType.DMA((1,)),
            ],
            flops=4 * tokens * heads * ctx_count * tokens * HEAD_SIZE,
            moved=4 << 20,
        )
        attended, left_own, left_beside, right_own, right_beside, beside_other = (
            lax.optimization_barrier(
                (attended, left_own, left_beside, right_own, right_beside, beside_other)
            )
        )
        far_own = lax.ppermute(left_own, "cx", ring(CX, 1))
        far_beside = lax.ppermute(right_beside, "cx", ring(CX, -1))
        near = [own_half, beside]
        later = [left_own, left_beside, right_own, right_beside, far_own, far_beside]
        others = [own_other, beside_other] + [lax.ppermute(w, "dp", swap(2)) for w in later]
        gathered = exchange(attended, ("cy", "zlo"))
        gathered = gathered.reshape(CY, ZLO, tokens // ZLO, queries.shape[2])

    with jax.named_scope("projection"):
        half, width = out_weight.shape[0] // 2, out_weight.shape[1]
        group_rows = CY * ZHI * token_rows
        mine, x = scalar(dp), scalar(lax.axis_index("cx").astype(I32))
        partial = call(
            project_kernel,
            jax.ShapeDtypeStruct((CY * ZHI, SUB, model_width // CY), BF16),
            (gathered,),
            vmem=14,
            scalars=(mine, x, scalar(zlo)),
            any_args=[stay(w) for w in near + later + others[:2]] + others[2:],
            scratch=[
                pltpu.VMEM((2 * CX * ZLO, half, width), BF16),
                pltpu.SemaphoreType.DMA((2 * CX * ZLO,)),
            ],
            flops=2 * group_rows * 16 * half * width,
            moved=6 << 20,
        )
        parts = exchange(partial, ("cy", "zhi"))

    with jax.named_scope("norm"):
        meta = jnp.concatenate([routes[0], block_masks[0]], axis=1).astype(BF16)
        meta = jnp.pad(meta, ((0, 0), (0, LANES - 2 * TOP)))
        ext, hidden_state = call(
            norm_kernel,
            [
                jax.ShapeDtypeStruct((token_rows, model_width + LANES), BF16),
                jax.ShapeDtypeStruct((token_rows, model_width), BF16),
            ],
            (parts, residual[0], norm_gain.reshape(1, model_width), meta),
            vmem=6,
            moved=2 << 20,
        )
        left = lax.ppermute(ext, "zhi", ring(ZHI, 1))
        right = lax.ppermute(ext, "zhi", ring(ZHI, -1))
        cut = model_width // 2
        far = [
            lax.ppermute(left[:, :cut], "zhi", ring(ZHI, 1)),
            lax.ppermute(right[:, cut:], "zhi", ring(ZHI, -1)),
        ]
        near_ext = (ext, left, right, *far)

    with jax.named_scope("dispatch"):
        dests = ctx_count * ZLO
        capacity = ZHI * token_rows // SUB * CAP
        slots = dests * capacity
        rows = call(
            dispatch_kernel,
            jax.ShapeDtypeStruct((slots, model_width + LANES), BF16),
            near_ext,
            vmem=16,
            scalars=(scalar(zhi),),
            flops=2 * slots * 64 * model_width,
            moved=3 << 20,
        )
        slot_weight = call(
            weight_kernel,
            jax.ShapeDtypeStruct((ZHI * token_rows, slots), F32),
            (router_weight, *near_ext),
            vmem=8,
            scalars=(scalar(zhi),),
            flops=2 * 64 * EXPERTS * model_width,
            moved=2 << 20,
        )
        over = ("cy", "cx", "zlo")
        got = exchange(rows.reshape(dests, capacity, model_width + LANES), over)

    with jax.named_scope("experts"):
        every = own_experts + other_experts
        expert_out = call(
            expert_kernel,
            jax.ShapeDtypeStruct((slots, model_width), BF16),
            (got.reshape(slots, model_width + LANES),),
            vmem=32,
            scalars=(scalar(dp),),
            any_args=[stay(w) if i % 3 == 2 else w for i, w in enumerate(every)],
            scratch=[pltpu.VMEM(a.shape, a.dtype) for a in every] + [pltpu.SemaphoreType.DMA((6 + 2 * DOWN_PARTS,))],
            flops=6 * slots * model_width * 768,
            moved=22 << 20,
        )
        back = exchange(expert_out.reshape(dests, capacity, model_width), over)

    with jax.named_scope("combine"):
        mixed = call(
            combine_kernel,
            jax.ShapeDtypeStruct((ZHI, token_rows, model_width), BF16),
            (slot_weight, back.reshape(slots, model_width)),
            vmem=14,
            scalars=(scalar(zhi),),
            flops=6 * 64 * slots * model_width,
            moved=3 << 20,
        )
        mixture = jnp.sum(exchange(mixed, "zhi").astype(F32), axis=0)
        layer_out = (hidden_state.astype(F32) + mixture).astype(BF16)
    return layer_out[None]


def solution(mesh):
    fine = Mesh(
        mesh.devices.reshape(2, CY, CX, ZHI, ZLO), ("dp", "cy", "cx", "zhi", "zlo")
    )
    tp = ("zhi", "zlo")
    all_ctx = CTX + tp
    in_specs = (
        P("dp", CTX, tp),
        P("dp", CTX, None),
        P("dp", CTX, None),
        P("dp", CTX),
        P(tp, CTX),
        P("dp", all_ctx, None),
        P(),
        P(),
        P("dp", all_ctx, None),
        P("dp", all_ctx, None),
        P(all_ctx, None, "dp"),
        P(all_ctx, None, "dp"),
        P(all_ctx, "dp", None),
    )
    out_specs = P("dp", all_ctx, None)
    return jax.shard_map(local, mesh=fine, in_specs=in_specs, out_specs=out_specs, check_vma=False)
```

```python
import math

import jax
import jax.numpy as jnp
from jax import lax
from jax.experimental import pallas as pl
from jax.experimental.pallas import tpu as pltpu
from jax.sharding import Mesh
from jax.sharding import PartitionSpec as P

QUERY_HEADS = 64
KEY_VALUE_HEADS = 4
HEAD_SIZE = 128
MASK_BLOCKS = 6
TOP = 8
EXPERTS = 128
CAP = 2
SCORE_FLOOR = -1e30
LANES = 128
SUB = 16
MIB = 1024 * 1024

CY, CX, ZHI, ZLO = 4, 4, 4, 2
CTX = ("cy", "cx")
F32, BF16, I32 = jnp.float32, jnp.bfloat16, jnp.int32


def call(kernel, out_shape, args, vmem, scalars=(), any_args=(), scratch=(), flops=0, moved=0):
    specs = [pl.BlockSpec(memory_space=pltpu.SMEM) for _ in scalars]
    specs += [pl.BlockSpec(memory_space=pltpu.VMEM) for _ in args]
    specs += [pl.BlockSpec(memory_space=pl.ANY) for _ in any_args]
    many = isinstance(out_shape, (list, tuple))
    whole = pl.BlockSpec(memory_space=pltpu.VMEM)
    return pl.pallas_call(
        kernel,
        out_shape=out_shape,
        in_specs=specs,
        out_specs=[whole] * len(out_shape) if many else whole,
        scratch_shapes=list(scratch),
        cost_estimate=pl.CostEstimate(flops=flops, bytes_accessed=moved, transcendentals=0),
        compiler_params=pltpu.CompilerParams(vmem_limit_bytes=vmem * MIB),
    )(*scalars, *args, *any_args)


def head_kernel(head_ref, key_ref, value_ref, out_ref, pair_ref, sems):
    columns = pl.ds(pl.multiple_of(head_ref[0] * HEAD_SIZE, HEAD_SIZE), HEAD_SIZE)
    copies = [
        pltpu.make_async_copy(ref.at[:, columns], pair_ref.at[i], sems.at[i])
        for i, ref in enumerate((key_ref, value_ref))
    ]
    for copy in copies:
        copy.start()
    for copy in copies:
        copy.wait()
    pair = jnp.concatenate([pair_ref[0], pair_ref[1]], axis=1)
    for c in range(out_ref.shape[0]):
        out_ref[c] = pair


def attend_kernel(first_ref, kv_ref, start_ref, query_hbm, out_ref, bias_ref, query_ref, sem):
    copy = pltpu.make_async_copy(query_hbm, query_ref, sem.at[0])
    copy.start()
    tokens = query_ref.shape[0]
    heads = query_ref.shape[1] // HEAD_SIZE
    keys = kv_ref.shape[0] * kv_ref.shape[1]
    key_rows = kv_ref[:, :, :HEAD_SIZE].reshape(keys, HEAD_SIZE)
    value_rows = kv_ref[:, :, HEAD_SIZE:].reshape(keys, HEAD_SIZE)
    position = first_ref[0] + lax.broadcasted_iota(I32, (tokens, keys), 0)
    key_pos = lax.broadcasted_iota(I32, (tokens, keys), 1)
    visible = (key_pos >= start_ref[...]) & (key_pos <= position)
    bias_ref[...] = jnp.where(visible, 0.0, SCORE_FLOOR)
    copy.wait()
    scale = math.log2(math.e) / math.sqrt(HEAD_SIZE)
    bias = bias_ref[...]
    bias = jnp.concatenate([bias, bias], axis=0)
    for head in range(0, heads, 2):
        columns = [slice(h * HEAD_SIZE, (h + 1) * HEAD_SIZE) for h in (head, head + 1)]
        scores = lax.dot_general(
            jnp.concatenate([query_ref[:, c] for c in columns], axis=0),
            key_rows,
            (((1,), (1,)), ((), ())),
            preferred_element_type=F32,
        )
        scores = scores * scale + bias
        row_max = jnp.max(scores, axis=1, keepdims=True)
        weights = jnp.exp2(scores - row_max)
        row_sum = jnp.sum(weights, axis=1, keepdims=True)
        mixed = jnp.dot(weights.astype(BF16), value_rows, preferred_element_type=F32)
        attended = (mixed / row_sum).astype(BF16)
        for which in range(2):
            for z in range(ZHI * ZLO):
                block = attended[which * tokens + z * SUB : which * tokens + (z + 1) * SUB]
                rows = slice((z // ZLO) * SUB, (z // ZLO + 1) * SUB)
                for y in range(CY):
                    out_ref[z % ZLO * CY + y, rows, columns[which]] = block


def project_kernel(dp_ref, x_ref, zlo_ref, att_ref, *refs):
    count = 2 * CX * ZLO
    sources, out_ref, held_ref, sems = refs[:count], refs[count], refs[count + 1], refs[count + 2]
    copies = [
        pltpu.make_async_copy(source, held_ref.at[i], sems.at[i]) for i, source in enumerate(sources)
    ]
    for copy in copies:
        copy.start()
    half, width = held_ref.shape[1:]
    rows = att_ref.shape[1] * att_ref.shape[2]
    for step, away in enumerate((0, CX - 1, 1, 2)):
        total = jnp.zeros((rows, width), F32)
        for part in range(2):
            columns = pl.ds(
                pl.multiple_of((dp_ref[0] if part == 0 else 1 - dp_ref[0]) * half, half), half
            )
            for near in range(ZLO):
                source = zlo_ref[0] if near == 0 else 1 - zlo_ref[0]
                piece = CX * ZLO * part + ZLO * step + near
                copies[piece].wait()
                total += jnp.dot(
                    att_ref[source, :, :, columns].reshape(rows, half),
                    held_ref[piece],
                    preferred_element_type=F32,
                )
        place = pl.multiple_of(((x_ref[0] + away) & (CX - 1)) * width, width)
        total = total.astype(BF16).reshape(rows // SUB, SUB, width)
        for y in range(CY):
            for z in range(ZHI):
                out_ref[z * CY + y, :, pl.ds(place, width)] = total[y * ZHI + z]


def norm_kernel(parts_ref, residual_ref, gain_ref, meta_ref, ext_ref, hidden_ref):
    model_width = residual_ref.shape[1]
    width = model_width // CY
    zs = ZHI
    pieces = []
    square_sum = jnp.zeros((SUB, 1), F32)
    for y in range(CY):
        columns = slice(y * width, (y + 1) * width)
        projected = sum(parts_ref[z * CY + y].astype(F32) for z in range(zs))
        hidden = (residual_ref[:, columns].astype(F32) + projected).astype(BF16)
        hidden_ref[:, columns] = hidden
        wide = hidden.astype(F32)
        square_sum += jnp.sum(wide * wide, axis=1, keepdims=True)
        pieces.append(wide)
    inverse = lax.rsqrt(square_sum / model_width + 1e-06)
    for y in range(CY):
        columns = slice(y * width, (y + 1) * width)
        normed = (pieces[y] * inverse * gain_ref[:, columns].astype(F32)).astype(BF16)
        ext_ref[:, columns] = normed
    ext_ref[:, model_width:] = meta_ref[...]


def slot_hits(meta, zhi, slots, slot_capacity):
    tokens = meta.shape[0]
    slot = lax.broadcasted_iota(I32, (tokens, slots), 1)
    dest = slot >> (slot_capacity.bit_length() - 1)
    ctx = (dest >> 3) * CX + (dest & (CX - 1))
    expert = ctx * (ZHI * ZLO) + zhi * ZLO + ((dest >> 2) & (ZLO - 1))
    hits = [meta[:, k : k + 1].astype(F32).astype(I32) == expert for k in range(TOP)]
    named = sum(h.astype(F32) for h in hits)
    later = lax.broadcasted_iota(I32, (tokens, tokens), 0) > lax.broadcasted_iota(
        I32, (tokens, tokens), 1
    )
    earlier = jnp.dot(later.astype(BF16), named.astype(BF16), preferred_element_type=F32)
    place = (slot & (slot_capacity - 1)).astype(F32)
    chosen = jnp.where((named > 0.5) & (earlier == place), 1.0, 0.0)
    return hits, chosen


def gathered_rows(refs):
    own, left, right, far_first, far_second = [ref[...] for ref in refs]
    far = jnp.concatenate([far_first, far_second], axis=1)
    return jnp.concatenate([own, left, right, far], axis=0)


def dispatch_kernel(zhi_ref, *refs):
    ext, rows_ref = gathered_rows(refs[:-1]), refs[-1]
    tokens = ext.shape[0]
    width = ext.shape[1] - LANES
    meta = ext[:, width:]
    hits, chosen = slot_hits(meta, zhi_ref[0], rows_ref.shape[0], tokens // SUB * CAP)
    masks = sum(
        jnp.where(hits[k], meta[:, TOP + k : TOP + k + 1].astype(F32), 0.0) for k in range(TOP)
    )
    along = (((0,), (0,)), ((), ()))
    rows_ref[:, :width] = lax.dot_general(
        chosen.astype(BF16), ext[:, :width], along, preferred_element_type=F32
    ).astype(BF16)
    ones = jnp.ones((tokens, LANES), BF16)
    rows_ref[:, width:] = lax.dot_general(
        (masks * chosen).astype(BF16), ones, along, preferred_element_type=F32
    ).astype(BF16)


def weight_kernel(zhi_ref, router_ref, *refs):
    ext, out_ref = gathered_rows(refs[:-1]), refs[-1]
    tokens = ext.shape[0]
    model_width = ext.shape[1] - LANES
    slots = out_ref.shape[1]
    meta, normed = ext[:, model_width:], ext[:, :model_width]
    logits = jnp.dot(normed, router_ref[...], preferred_element_type=F32)
    lanes = lax.broadcasted_iota(I32, (tokens, EXPERTS), 1)
    exps = []
    for k in range(TOP):
        route = meta[:, k : k + 1].astype(F32).astype(I32)
        picked = jnp.sum(jnp.where(lanes == route, logits, 0.0), axis=1, keepdims=True)
        exps.append(jnp.exp(picked))
    total = sum(exps)
    hits, chosen = slot_hits(meta, zhi_ref[0], slots, tokens // SUB * CAP)
    route_weight = sum(jnp.where(hits[k], exps[k] / total, 0.0) for k in range(TOP))
    out_ref[...] = route_weight * chosen


def expert_kernel(dp_ref, rows_ref, *refs):
    weights, out_ref, held, sems = refs[:6], refs[6], refs[7:13], refs[13]
    copies = [pltpu.make_async_copy(weights[i], held[i], sems.at[i]) for i in range(6)]
    for i in (0, 1, 3, 4, 2, 5):
        copies[i].start()
    model_width = out_ref.shape[1]
    masks = rows_ref[:, model_width:].astype(F32).astype(I32)
    blocks = MASK_BLOCKS // 2
    acts = []
    for part in range(2):
        gate_ref, up_ref = held[3 * part], held[3 * part + 1]
        first = (dp_ref[0] if part == 0 else 1 - dp_ref[0]) * blocks
        copies[3 * part].wait()
        copies[3 * part + 1].wait()
        both = jnp.dot(
            rows_ref[:, :model_width],
            jnp.concatenate([gate_ref[...], up_ref[...]], axis=1),
            preferred_element_type=F32,
        )
        units = gate_ref.shape[1]
        keep = jnp.concatenate(
            [(jnp.right_shift(masks, first + b) & 1).astype(F32) for b in range(blocks)], axis=1
        )
        acts.append((jax.nn.silu(both[:, :units]) * both[:, units:] * keep).astype(BF16))
    copies[2].wait()
    copies[5].wait()
    activated = jnp.concatenate(acts, axis=1)
    step = 512
    for j in range(model_width // step):
        columns = slice(j * step, (j + 1) * step)
        down = jnp.concatenate([held[2][:, columns], held[5][:, columns]], axis=0)
        out_ref[:, columns] = jnp.dot(activated, down, preferred_element_type=F32).astype(BF16)


def combine_kernel(zhi_ref, weight_ref, back_ref, out_ref):
    weight = weight_ref[...]
    high = weight.astype(BF16)
    rest = weight - high.astype(F32)
    middle = rest.astype(BF16)
    low = (rest - middle.astype(F32)).astype(BF16)
    stacked = jnp.concatenate([high, middle, low], axis=0)
    tokens = weight.shape[0]
    model_width = back_ref.shape[1]
    step = 1024
    for j in range(model_width // step):
        columns = slice(j * step, (j + 1) * step)
        parts = jnp.dot(stacked, back_ref[:, columns], preferred_element_type=F32)
        total = parts[:tokens] + parts[tokens : 2 * tokens] + parts[2 * tokens :]
        total = total.astype(BF16)
        for place, away in enumerate((0, ZHI - 1, 1, 2)):
            home = (zhi_ref[0] + away) & (ZHI - 1)
            out_ref[home, :, columns] = total[place * SUB : (place + 1) * SUB]


def stay(x):
    return pltpu.with_memory_space_constraint(x, pltpu.HBM)


def swap(n):
    return [(i, i ^ 1) for i in range(n)]


def ring(n, step):
    return [(i, (i + step) % n) for i in range(n)]


def exchange(x, axes):
    return lax.all_to_all(x, axes, split_axis=0, concat_axis=0, tiled=True)


def local(
    queries,
    keys,
    attention_values,
    key_start,
    out_weight,
    residual,
    norm_gain,
    router_weight,
    routes,
    block_masks,
    gate_weight,
    up_weight,
    down_weight,
):
    dp = lax.axis_index("dp").astype(I32)
    ctx = lax.axis_index(CTX).astype(I32)
    zhi, zlo = lax.axis_index("zhi").astype(I32), lax.axis_index("zlo").astype(I32)
    tokens = queries.shape[1]
    model_width = residual.shape[2]
    token_rows = residual.shape[1]
    ctx_count = CY * CX
    scalar = lambda v: v.reshape(1)

    with jax.named_scope("keys_values"):
        heads = queries.shape[2] // HEAD_SIZE
        kv_head = (zhi * ZLO + zlo) * heads // (QUERY_HEADS // KEY_VALUE_HEADS)
        copies = call(
            head_kernel,
            jax.ShapeDtypeStruct((ctx_count, tokens, 2 * HEAD_SIZE), BF16),
            (),
            vmem=8,
            scalars=(scalar(kv_head),),
            any_args=(stay(keys[0]), stay(attention_values[0])),
            scratch=[pltpu.VMEM((2, tokens, HEAD_SIZE), BF16), pltpu.SemaphoreType.DMA((2,))],
            moved=2 << 20,
        )
        all_kv = exchange(copies, CTX)

    with jax.named_scope("expert_weights"):
        own_experts = [a[0] for a in (gate_weight, up_weight, down_weight)]
        other_experts = [lax.ppermute(a, "dp", swap(2)) for a in own_experts]

    with jax.named_scope("out_weight"):
        half = out_weight.shape[0] // 2
        own_half = lax.dynamic_slice_in_dim(out_weight, dp * half, half, 0)
        beside = lax.ppermute(own_half, "zlo", swap(ZLO))
        own_other = lax.ppermute(own_half, "dp", swap(2))
        all_kv, beside, own_other, other_experts = lax.optimization_barrier(
            (all_kv, beside, own_other, other_experts)
        )
        left_own = lax.ppermute(own_half, "cx", ring(CX, 1))
        right_beside = lax.ppermute(beside, "cx", ring(CX, -1))
        left_beside = lax.ppermute(beside, "cx", ring(CX, 1))
        right_own = lax.ppermute(own_half, "cx", ring(CX, -1))
        beside_other = lax.ppermute(beside, "dp", swap(2))

    with jax.named_scope("attention"):
        attended = call(
            attend_kernel,
            jax.ShapeDtypeStruct((CY * ZLO, tokens // ZLO, queries.shape[2]), BF16),
            (all_kv, key_start.reshape(tokens, 1)),
            vmem=28,
            scalars=(scalar(ctx * tokens),),
            any_args=(stay(queries[0]),),
            scratch=[
                pltpu.VMEM((tokens, ctx_count * tokens), F32),
                pltpu.VMEM((tokens, queries.shape[2]), BF16),
                pltpu.SemaphoreType.DMA((1,)),
            ],
            flops=4 * tokens * heads * ctx_count * tokens * HEAD_SIZE,
            moved=4 << 20,
        )
        attended, left_own, left_beside, right_own, right_beside, beside_other = (
            lax.optimization_barrier(
                (attended, left_own, left_beside, right_own, right_beside, beside_other)
            )
        )
        far_own = lax.ppermute(left_own, "cx", ring(CX, 1))
        far_beside = lax.ppermute(right_beside, "cx", ring(CX, -1))
        near = [own_half, beside]
        later = [left_own, left_beside, right_own, right_beside, far_own, far_beside]
        others = [own_other, beside_other] + [lax.ppermute(w, "dp", swap(2)) for w in later]
        gathered = exchange(attended, ("zlo", "cy"))
        gathered = gathered.reshape(ZLO, CY, tokens // ZLO, queries.shape[2])

    with jax.named_scope("projection"):
        half, width = out_weight.shape[0] // 2, out_weight.shape[1]
        group_rows = CY * ZHI * token_rows
        mine, x = scalar(dp), scalar(lax.axis_index("cx").astype(I32))
        partial = call(
            project_kernel,
            jax.ShapeDtypeStruct((CY * ZHI, SUB, model_width // CY), BF16),
            (gathered,),
            vmem=14,
            scalars=(mine, x, scalar(zlo)),
            any_args=[stay(w) for w in near + later + others[:2]] + others[2:],
            scratch=[
                pltpu.VMEM((2 * CX * ZLO, half, width), BF16),
                pltpu.SemaphoreType.DMA((2 * CX * ZLO,)),
            ],
            flops=2 * group_rows * 16 * half * width,
            moved=6 << 20,
        )
        parts = exchange(partial, ("zhi", "cy"))

    with jax.named_scope("norm"):
        meta = jnp.concatenate([routes[0], block_masks[0]], axis=1).astype(BF16)
        meta = jnp.pad(meta, ((0, 0), (0, LANES - 2 * TOP)))
        ext, hidden_state = call(
            norm_kernel,
            [
                jax.ShapeDtypeStruct((token_rows, model_width + LANES), BF16),
                jax.ShapeDtypeStruct((token_rows, model_width), BF16),
            ],
            (parts, residual[0], norm_gain.reshape(1, model_width), meta),
            vmem=6,
            moved=2 << 20,
        )
        left = lax.ppermute(ext, "zhi", ring(ZHI, 1))
        right = lax.ppermute(ext, "zhi", ring(ZHI, -1))
        cut = model_width // 2
        far = [
            lax.ppermute(left[:, :cut], "zhi", ring(ZHI, 1)),
            lax.ppermute(right[:, cut:], "zhi", ring(ZHI, -1)),
        ]
        near_ext = (ext, left, right, *far)

    with jax.named_scope("dispatch"):
        dests = ctx_count * ZLO
        capacity = ZHI * token_rows // SUB * CAP
        slots = dests * capacity
        rows = call(
            dispatch_kernel,
            jax.ShapeDtypeStruct((slots, model_width + LANES), BF16),
            near_ext,
            vmem=16,
            scalars=(scalar(zhi),),
            flops=2 * slots * 64 * model_width,
            moved=3 << 20,
        )
        slot_weight = call(
            weight_kernel,
            jax.ShapeDtypeStruct((ZHI * token_rows, slots), F32),
            (router_weight, *near_ext),
            vmem=8,
            scalars=(scalar(zhi),),
            flops=2 * 64 * EXPERTS * model_width,
            moved=2 << 20,
        )
        over = ("cy", "zlo", "cx")
        got = exchange(rows.reshape(dests, capacity, model_width + LANES), over)

    with jax.named_scope("experts"):
        every = own_experts + other_experts
        expert_out = call(
            expert_kernel,
            jax.ShapeDtypeStruct((slots, model_width), BF16),
            (got.reshape(slots, model_width + LANES),),
            vmem=32,
            scalars=(scalar(dp),),
            any_args=[stay(w) if i % 3 == 2 else w for i, w in enumerate(every)],
            scratch=[pltpu.VMEM(a.shape, a.dtype) for a in every] + [pltpu.SemaphoreType.DMA((6,))],
            flops=6 * slots * model_width * 768,
            moved=22 << 20,
        )
        back = exchange(expert_out.reshape(dests, capacity, model_width), over)

    with jax.named_scope("combine"):
        mixed = call(
            combine_kernel,
            jax.ShapeDtypeStruct((ZHI, token_rows, model_width), BF16),
            (slot_weight, back.reshape(slots, model_width)),
            vmem=14,
            scalars=(scalar(zhi),),
            flops=6 * 64 * slots * model_width,
            moved=3 << 20,
        )
        mixture = jnp.sum(exchange(mixed, "zhi").astype(F32), axis=0)
        layer_out = (hidden_state.astype(F32) + mixture).astype(BF16)
    return layer_out[None]


def solution(mesh):
    fine = Mesh(
        mesh.devices.reshape(2, CY, CX, ZHI, ZLO), ("dp", "cy", "cx", "zhi", "zlo")
    )
    tp = ("zhi", "zlo")
    all_ctx = CTX + tp
    in_specs = (
        P("dp", CTX, tp),
        P("dp", CTX, None),
        P("dp", CTX, None),
        P("dp", CTX),
        P(tp, CTX),
        P("dp", all_ctx, None),
        P(),
        P(),
        P("dp", all_ctx, None),
        P("dp", all_ctx, None),
        P(all_ctx, None, "dp"),
        P(all_ctx, None, "dp"),
        P(all_ctx, "dp", None),
    )
    out_specs = P("dp", all_ctx, None)
    return jax.shard_map(local, mesh=fine, in_specs=in_specs, out_specs=out_specs, check_vma=False)
```

```python
import math

import jax
import jax.numpy as jnp
from jax import lax
from jax.experimental import pallas as pl
from jax.experimental.pallas import tpu as pltpu
from jax.sharding import Mesh
from jax.sharding import PartitionSpec as P

QUERY_HEADS = 64
KEY_VALUE_HEADS = 4
HEAD_SIZE = 128
MASK_BLOCKS = 6
TOP = 8
EXPERTS = 128
CAP = 2
SCORE_FLOOR = -1e30
LANES = 128
SUB = 16
MIB = 1024 * 1024

CY, CX, ZHI, ZLO = 4, 4, 4, 2
CTX = ("cy", "cx")
F32, BF16, I32 = jnp.float32, jnp.bfloat16, jnp.int32


def call(kernel, out_shape, args, vmem, scalars=(), any_args=(), scratch=(), flops=0, moved=0):
    specs = [pl.BlockSpec(memory_space=pltpu.SMEM) for _ in scalars]
    specs += [pl.BlockSpec(memory_space=pltpu.VMEM) for _ in args]
    specs += [pl.BlockSpec(memory_space=pl.ANY) for _ in any_args]
    many = isinstance(out_shape, (list, tuple))
    whole = pl.BlockSpec(memory_space=pltpu.VMEM)
    return pl.pallas_call(
        kernel,
        out_shape=out_shape,
        in_specs=specs,
        out_specs=[whole] * len(out_shape) if many else whole,
        scratch_shapes=list(scratch),
        cost_estimate=pl.CostEstimate(flops=flops, bytes_accessed=moved, transcendentals=0),
        compiler_params=pltpu.CompilerParams(vmem_limit_bytes=vmem * MIB),
    )(*scalars, *args, *any_args)


def head_kernel(head_ref, key_ref, value_ref, out_ref, pair_ref, sems):
    columns = pl.ds(pl.multiple_of(head_ref[0] * HEAD_SIZE, HEAD_SIZE), HEAD_SIZE)
    copies = [
        pltpu.make_async_copy(ref.at[:, columns], pair_ref.at[i], sems.at[i])
        for i, ref in enumerate((key_ref, value_ref))
    ]
    for copy in copies:
        copy.start()
    for copy in copies:
        copy.wait()
    pair = jnp.concatenate([pair_ref[0], pair_ref[1]], axis=1)
    for c in range(out_ref.shape[0]):
        out_ref[c] = pair


def attend_kernel(first_ref, kv_ref, start_ref, query_hbm, out_ref, bias_ref, query_ref, sem):
    copy = pltpu.make_async_copy(query_hbm, query_ref, sem.at[0])
    copy.start()
    tokens = query_ref.shape[0]
    heads = query_ref.shape[1] // HEAD_SIZE
    keys = kv_ref.shape[0] * kv_ref.shape[1]
    key_rows = kv_ref[:, :, :HEAD_SIZE].reshape(keys, HEAD_SIZE)
    value_rows = kv_ref[:, :, HEAD_SIZE:].reshape(keys, HEAD_SIZE)
    position = first_ref[0] + lax.broadcasted_iota(I32, (tokens, keys), 0)
    key_pos = lax.broadcasted_iota(I32, (tokens, keys), 1)
    visible = (key_pos >= start_ref[...]) & (key_pos <= position)
    bias_ref[...] = jnp.where(visible, 0.0, SCORE_FLOOR)
    copy.wait()
    scale = math.log2(math.e) / math.sqrt(HEAD_SIZE)
    bias = bias_ref[...]
    bias = jnp.concatenate([bias, bias], axis=0)
    for head in range(0, heads, 2):
        columns = [slice(h * HEAD_SIZE, (h + 1) * HEAD_SIZE) for h in (head, head + 1)]
        scores = lax.dot_general(
            jnp.concatenate([query_ref[:, c] for c in columns], axis=0),
            key_rows,
            (((1,), (1,)), ((), ())),
            preferred_element_type=F32,
        )
        scores = scores * scale + bias
        row_max = jnp.max(scores, axis=1, keepdims=True)
        weights = jnp.exp2(scores - row_max)
        row_sum = jnp.sum(weights, axis=1, keepdims=True)
        mixed = jnp.dot(weights.astype(BF16), value_rows, preferred_element_type=F32)
        attended = (mixed / row_sum).astype(BF16)
        for which in range(2):
            for z in range(ZHI * ZLO):
                block = attended[which * tokens + z * SUB : which * tokens + (z + 1) * SUB]
                rows = slice((z // ZLO) * SUB, (z // ZLO + 1) * SUB)
                for y in range(CY):
                    out_ref[y * ZLO + z % ZLO, rows, columns[which]] = block


def project_kernel(dp_ref, x_ref, zlo_ref, att_ref, *refs):
    count = 2 * CX * ZLO
    sources, out_ref, held_ref, sems = refs[:count], refs[count], refs[count + 1], refs[count + 2]
    copies = [
        pltpu.make_async_copy(source, held_ref.at[i], sems.at[i]) for i, source in enumerate(sources)
    ]
    for copy in copies:
        copy.start()
    half, width = held_ref.shape[1:]
    rows = att_ref.shape[0] * att_ref.shape[2]
    for step, away in enumerate((0, CX - 1, 1, 2)):
        total = jnp.zeros((rows, width), F32)
        for part in range(2):
            columns = pl.ds(
                pl.multiple_of((dp_ref[0] if part == 0 else 1 - dp_ref[0]) * half, half), half
            )
            for near in range(ZLO):
                source = zlo_ref[0] if near == 0 else 1 - zlo_ref[0]
                piece = CX * ZLO * part + ZLO * step + near
                copies[piece].wait()
                total += jnp.dot(
                    att_ref[:, source, :, columns].reshape(rows, half),
                    held_ref[piece],
                    preferred_element_type=F32,
                )
        place = pl.multiple_of(((x_ref[0] + away) & (CX - 1)) * width, width)
        out_ref[:, :, pl.ds(place, width)] = total.astype(BF16).reshape(rows // SUB, SUB, width)


def norm_kernel(parts_ref, residual_ref, gain_ref, meta_ref, first_ref, second_ref, hidden_ref):
    model_width = residual_ref.shape[1]
    width = model_width // CY
    zs = ZHI
    pieces = []
    square_sum = jnp.zeros((SUB, 1), F32)
    for y in range(CY):
        columns = slice(y * width, (y + 1) * width)
        projected = sum(parts_ref[y * zs + z].astype(F32) for z in range(zs))
        hidden = (residual_ref[:, columns].astype(F32) + projected).astype(BF16)
        hidden_ref[:, columns] = hidden
        wide = hidden.astype(F32)
        square_sum += jnp.sum(wide * wide, axis=1, keepdims=True)
        pieces.append(wide)
    inverse = lax.rsqrt(square_sum / model_width + 1e-06)
    for y in range(CY):
        columns = slice(y * width, (y + 1) * width)
        normed = (pieces[y] * inverse * gain_ref[:, columns].astype(F32)).astype(BF16)
        out_ref = first_ref if y < CY // 2 else second_ref
        place = y % (CY // 2) * width
        out_ref[:, place : place + width] = normed
    second_ref[:, model_width // 2 :] = meta_ref[...]


def slot_hits(meta, zhi, slots, slot_capacity):
    tokens = meta.shape[0]
    slot = lax.broadcasted_iota(I32, (tokens, slots), 1)
    dest = slot >> (slot_capacity.bit_length() - 1)
    expert = (dest >> 1) * (ZHI * ZLO) + zhi * ZLO + (dest & 1)
    hits = [meta[:, k : k + 1].astype(F32).astype(I32) == expert for k in range(TOP)]
    named = sum(h.astype(F32) for h in hits)
    later = lax.broadcasted_iota(I32, (tokens, tokens), 0) > lax.broadcasted_iota(
        I32, (tokens, tokens), 1
    )
    earlier = jnp.dot(later.astype(BF16), named.astype(BF16), preferred_element_type=F32)
    place = (slot & (slot_capacity - 1)).astype(F32)
    chosen = jnp.where((named > 0.5) & (earlier == place), 1.0, 0.0)
    return hits, chosen


def gathered_rows(refs):
    halves = [jnp.concatenate([r[...] for r in refs[start::2]], axis=0) for start in range(2)]
    return jnp.concatenate(halves, axis=1)


def dispatch_kernel(zhi_ref, *refs):
    ext, rows_ref = gathered_rows(refs[:-1]), refs[-1]
    tokens = ext.shape[0]
    width = ext.shape[1] - LANES
    meta = ext[:, width:]
    hits, chosen = slot_hits(meta, zhi_ref[0], rows_ref.shape[0], tokens // SUB * CAP)
    masks = sum(
        jnp.where(hits[k], meta[:, TOP + k : TOP + k + 1].astype(F32), 0.0) for k in range(TOP)
    )
    along = (((0,), (0,)), ((), ()))
    rows_ref[:, :width] = lax.dot_general(
        chosen.astype(BF16), ext[:, :width], along, preferred_element_type=F32
    ).astype(BF16)
    ones = jnp.ones((tokens, LANES), BF16)
    rows_ref[:, width:] = lax.dot_general(
        (masks * chosen).astype(BF16), ones, along, preferred_element_type=F32
    ).astype(BF16)


def weight_kernel(zhi_ref, router_ref, *refs):
    ext, out_ref = gathered_rows(refs[:-1]), refs[-1]
    tokens = ext.shape[0]
    model_width = ext.shape[1] - LANES
    slots = out_ref.shape[1]
    meta, normed = ext[:, model_width:], ext[:, :model_width]
    logits = jnp.dot(normed, router_ref[...], preferred_element_type=F32)
    lanes = lax.broadcasted_iota(I32, (tokens, EXPERTS), 1)
    exps = []
    for k in range(TOP):
        route = meta[:, k : k + 1].astype(F32).astype(I32)
        picked = jnp.sum(jnp.where(lanes == route, logits, 0.0), axis=1, keepdims=True)
        exps.append(jnp.exp(picked))
    total = sum(exps)
    hits, chosen = slot_hits(meta, zhi_ref[0], slots, tokens // SUB * CAP)
    route_weight = sum(jnp.where(hits[k], exps[k] / total, 0.0) for k in range(TOP))
    out_ref[...] = route_weight * chosen


def expert_kernel(dp_ref, rows_ref, *refs):
    weights, out_ref, held, sems = refs[:6], refs[6], refs[7:13], refs[13]
    copies = [pltpu.make_async_copy(weights[i], held[i], sems.at[i]) for i in range(6)]
    for i in (0, 1, 3, 4, 2, 5):
        copies[i].start()
    model_width = out_ref.shape[1]
    masks = rows_ref[:, model_width:].astype(F32).astype(I32)
    blocks = MASK_BLOCKS // 2
    acts = []
    for part in range(2):
        gate_ref, up_ref = held[3 * part], held[3 * part + 1]
        first = (dp_ref[0] if part == 0 else 1 - dp_ref[0]) * blocks
        copies[3 * part].wait()
        copies[3 * part + 1].wait()
        both = jnp.dot(
            rows_ref[:, :model_width],
            jnp.concatenate([gate_ref[...], up_ref[...]], axis=1),
            preferred_element_type=F32,
        )
        units = gate_ref.shape[1]
        keep = jnp.concatenate(
            [(jnp.right_shift(masks, first + b) & 1).astype(F32) for b in range(blocks)], axis=1
        )
        acts.append((jax.nn.silu(both[:, :units]) * both[:, units:] * keep).astype(BF16))
    copies[2].wait()
    copies[5].wait()
    activated = jnp.concatenate(acts, axis=1)
    step = 512
    for j in range(model_width // step):
        columns = slice(j * step, (j + 1) * step)
        down = jnp.concatenate([held[2][:, columns], held[5][:, columns]], axis=0)
        out_ref[:, columns] = jnp.dot(activated, down, preferred_element_type=F32).astype(BF16)


def combine_kernel(zhi_ref, weight_ref, back_ref, out_ref):
    weight = weight_ref[...]
    high = weight.astype(BF16)
    rest = weight - high.astype(F32)
    middle = rest.astype(BF16)
    low = (rest - middle.astype(F32)).astype(BF16)
    stacked = jnp.concatenate([high, middle, low], axis=0)
    tokens = weight.shape[0]
    model_width = back_ref.shape[1]
    step = 1024
    for j in range(model_width // step):
        columns = slice(j * step, (j + 1) * step)
        parts = jnp.dot(stacked, back_ref[:, columns], preferred_element_type=F32)
        total = parts[:tokens] + parts[tokens : 2 * tokens] + parts[2 * tokens :]
        total = total.astype(BF16)
        for place, away in enumerate((0, ZHI - 1, 1, 2)):
            home = (zhi_ref[0] + away) & (ZHI - 1)
            out_ref[home, :, columns] = total[place * SUB : (place + 1) * SUB]


def stay(x):
    return pltpu.with_memory_space_constraint(x, pltpu.HBM)


def swap(n):
    return [(i, i ^ 1) for i in range(n)]


def ring(n, step):
    return [(i, (i + step) % n) for i in range(n)]


def exchange(x, axes):
    return lax.all_to_all(x, axes, split_axis=0, concat_axis=0, tiled=True)


def local(
    queries,
    keys,
    attention_values,
    key_start,
    out_weight,
    residual,
    norm_gain,
    router_weight,
    routes,
    block_masks,
    gate_weight,
    up_weight,
    down_weight,
):
    dp = lax.axis_index("dp").astype(I32)
    ctx = lax.axis_index(CTX).astype(I32)
    zhi, zlo = lax.axis_index("zhi").astype(I32), lax.axis_index("zlo").astype(I32)
    tokens = queries.shape[1]
    model_width = residual.shape[2]
    token_rows = residual.shape[1]
    ctx_count = CY * CX
    scalar = lambda v: v.reshape(1)

    with jax.named_scope("keys_values"):
        heads = queries.shape[2] // HEAD_SIZE
        kv_head = (zhi * ZLO + zlo) * heads // (QUERY_HEADS // KEY_VALUE_HEADS)
        copies = call(
            head_kernel,
            jax.ShapeDtypeStruct((ctx_count, tokens, 2 * HEAD_SIZE), BF16),
            (),
            vmem=8,
            scalars=(scalar(kv_head),),
            any_args=(stay(keys[0]), stay(attention_values[0])),
            scratch=[pltpu.VMEM((2, tokens, HEAD_SIZE), BF16), pltpu.SemaphoreType.DMA((2,))],
            moved=2 << 20,
        )
        all_kv = exchange(copies, CTX)

    with jax.named_scope("expert_weights"):
        own_experts = [a[0] for a in (gate_weight, up_weight, down_weight)]
        other_experts = [lax.ppermute(a, "dp", swap(2)) for a in own_experts]

    with jax.named_scope("out_weight"):
        half = out_weight.shape[0] // 2
        own_half = lax.dynamic_slice_in_dim(out_weight, dp * half, half, 0)
        beside = lax.ppermute(own_half, "zlo", swap(ZLO))
        own_other = lax.ppermute(own_half, "dp", swap(2))
        all_kv, beside, own_other, other_experts = lax.optimization_barrier(
            (all_kv, beside, own_other, other_experts)
        )
        left_own = lax.ppermute(own_half, "cx", ring(CX, 1))
        right_beside = lax.ppermute(beside, "cx", ring(CX, -1))
        left_beside = lax.ppermute(beside, "cx", ring(CX, 1))
        right_own = lax.ppermute(own_half, "cx", ring(CX, -1))
        beside_other = lax.ppermute(beside, "dp", swap(2))

    with jax.named_scope("attention"):
        attended = call(
            attend_kernel,
            jax.ShapeDtypeStruct((CY * ZLO, tokens // ZLO, queries.shape[2]), BF16),
            (all_kv, key_start.reshape(tokens, 1)),
            vmem=28,
            scalars=(scalar(ctx * tokens),),
            any_args=(stay(queries[0]),),
            scratch=[
                pltpu.VMEM((tokens, ctx_count * tokens), F32),
                pltpu.VMEM((tokens, queries.shape[2]), BF16),
                pltpu.SemaphoreType.DMA((1,)),
            ],
            flops=4 * tokens * heads * ctx_count * tokens * HEAD_SIZE,
            moved=4 << 20,
        )
        attended, left_own, left_beside, right_own, right_beside, beside_other = (
            lax.optimization_barrier(
                (attended, left_own, left_beside, right_own, right_beside, beside_other)
            )
        )
        far_own = lax.ppermute(left_own, "cx", ring(CX, 1))
        far_beside = lax.ppermute(right_beside, "cx", ring(CX, -1))
        near = [own_half, beside]
        later = [left_own, left_beside, right_own, right_beside, far_own, far_beside]
        others = [own_other, beside_other] + [lax.ppermute(w, "dp", swap(2)) for w in later]
        gathered = exchange(attended, ("cy", "zlo"))
        gathered = gathered.reshape(CY, ZLO, tokens // ZLO, queries.shape[2])

    with jax.named_scope("projection"):
        half, width = out_weight.shape[0] // 2, out_weight.shape[1]
        group_rows = CY * ZHI * token_rows
        mine, x = scalar(dp), scalar(lax.axis_index("cx").astype(I32))
        partial = call(
            project_kernel,
            jax.ShapeDtypeStruct((CY * ZHI, SUB, model_width // CY), BF16),
            (gathered,),
            vmem=14,
            scalars=(mine, x, scalar(zlo)),
            any_args=[stay(w) for w in near + later + others[:2]] + others[2:],
            scratch=[
                pltpu.VMEM((2 * CX * ZLO, half, width), BF16),
                pltpu.SemaphoreType.DMA((2 * CX * ZLO,)),
            ],
            flops=2 * group_rows * 16 * half * width,
            moved=6 << 20,
        )
        parts = exchange(partial, ("cy", "zhi"))

    with jax.named_scope("norm"):
        meta = jnp.concatenate([routes[0], block_masks[0]], axis=1).astype(BF16)
        meta = jnp.pad(meta, ((0, 0), (0, LANES - 2 * TOP)))
        first, second, hidden_state = call(
            norm_kernel,
            [
                jax.ShapeDtypeStruct((token_rows, model_width // 2), BF16),
                jax.ShapeDtypeStruct((token_rows, model_width // 2 + LANES), BF16),
                jax.ShapeDtypeStruct((token_rows, model_width), BF16),
            ],
            (parts, residual[0], norm_gain.reshape(1, model_width), meta),
            vmem=6,
            moved=2 << 20,
        )
        left_first = lax.ppermute(first, "zhi", ring(ZHI, 1))
        right_second = lax.ppermute(second, "zhi", ring(ZHI, -1))
        left_second = lax.ppermute(second, "zhi", ring(ZHI, 1))
        right_first = lax.ppermute(first, "zhi", ring(ZHI, -1))
        far_first = lax.ppermute(left_first, "zhi", ring(ZHI, 1))
        far_second = lax.ppermute(right_second, "zhi", ring(ZHI, -1))
        near_ext = (
            *(first, second, left_first, left_second),
            *(right_first, right_second, far_first, far_second),
        )

    with jax.named_scope("dispatch"):
        dests = ctx_count * ZLO
        capacity = ZHI * token_rows // SUB * CAP
        slots = dests * capacity
        rows = call(
            dispatch_kernel,
            jax.ShapeDtypeStruct((slots, model_width + LANES), BF16),
            near_ext,
            vmem=16,
            scalars=(scalar(zhi),),
            flops=2 * slots * 64 * model_width,
            moved=3 << 20,
        )
        slot_weight = call(
            weight_kernel,
            jax.ShapeDtypeStruct((ZHI * token_rows, slots), F32),
            (router_weight, *near_ext),
            vmem=8,
            scalars=(scalar(zhi),),
            flops=2 * 64 * EXPERTS * model_width,
            moved=2 << 20,
        )
        over = ("cy", "cx", "zlo")
        got = exchange(rows.reshape(dests, capacity, model_width + LANES), over)

    with jax.named_scope("experts"):
        every = own_experts + other_experts
        expert_out = call(
            expert_kernel,
            jax.ShapeDtypeStruct((slots, model_width), BF16),
            (got.reshape(slots, model_width + LANES),),
            vmem=32,
            scalars=(scalar(dp),),
            any_args=[stay(w) if i % 3 == 2 else w for i, w in enumerate(every)],
            scratch=[pltpu.VMEM(a.shape, a.dtype) for a in every] + [pltpu.SemaphoreType.DMA((6,))],
            flops=6 * slots * model_width * 768,
            moved=22 << 20,
        )
        back = exchange(expert_out.reshape(dests, capacity, model_width), over)

    with jax.named_scope("combine"):
        mixed = call(
            combine_kernel,
            jax.ShapeDtypeStruct((ZHI, token_rows, model_width), BF16),
            (slot_weight, back.reshape(slots, model_width)),
            vmem=14,
            scalars=(scalar(zhi),),
            flops=6 * 64 * slots * model_width,
            moved=3 << 20,
        )
        mixture = jnp.sum(exchange(mixed, "zhi").astype(F32), axis=0)
        layer_out = (hidden_state.astype(F32) + mixture).astype(BF16)
    return layer_out[None]


def solution(mesh):
    fine = Mesh(
        mesh.devices.reshape(2, CY, CX, ZHI, ZLO), ("dp", "cy", "cx", "zhi", "zlo")
    )
    tp = ("zhi", "zlo")
    all_ctx = CTX + tp
    in_specs = (
        P("dp", CTX, tp),
        P("dp", CTX, None),
        P("dp", CTX, None),
        P("dp", CTX),
        P(tp, CTX),
        P("dp", all_ctx, None),
        P(),
        P(),
        P("dp", all_ctx, None),
        P("dp", all_ctx, None),
        P(all_ctx, None, "dp"),
        P(all_ctx, None, "dp"),
        P(all_ctx, "dp", None),
    )
    out_specs = P("dp", all_ctx, None)
    return jax.shard_map(local, mesh=fine, in_specs=in_specs, out_specs=out_specs, check_vma=False)
```
